256 devices in a mesh: slide: 4 (over x), seq: 2 (over core), fsdp: 32 (over z, y).
Axes of the slice: x: 4, y: 4, z: 8, core: 2. Of those that a mesh axis runs over, the one named last changes fastest.
Arguments:
- head_out: bfloat16 [4, 65536, 768], P('slide', ('seq', 'fsdp')), may hold values from -6 to 6
- proj_weight: bfloat16 [768, 1536], P('fsdp'), may hold values from -0.21875 to 0.21875
- norm_gain: float32 [1536], replicated, may hold values from 0.1 to 1.9
- embed_cot: bfloat16 [4, 1024, 1536], P('slide', ('seq', 'fsdp')), may hold values from -96 to 96
- tile_counts: int32 [4], P('slide'), may hold values from 256 to 1024, as said below
- seg_lengths: int32 [5], replicated, may hold values from 64 to 1024, as said below
- dilation: int32 [5], replicated, may hold values from 1 to 16, as said below
- embed_weight: bfloat16 [1536, 768], P('fsdp'), may hold values from -1.25 to 1.25
- qkv_weight: bfloat16 [768, 2304], P('fsdp'), as said below
- out_weight: bfloat16 [768, 768], P('fsdp'), may hold values from -0.4375 to 0.4375
Outputs:
- slide_out: bfloat16 [4, 1024, 768], P('slide', 'seq')
- head_out_grad: bfloat16 [4, 65536, 768], P('slide', ('seq', 'fsdp'))
- proj_grad: bfloat16 [768, 1536], P('fsdp')
The draws below stay inside these ranges and needn't reach their ends.
Inputs may be any that keep to these rules, and one draw needn't show every extreme that they name: `tile_counts`: one slide has all 1024 positions filled. `seg_lengths`: the values are 1024 // 16 times 1, 2, 4, 8 and 16, each once, in any order. `dilation`: the values are 1, 2, 4, 8 and 16, each once, in any order. `qkv_weight`: entries lie between -30 / sqrt(768) and 30 / sqrt(768).
All inputs are finite; a program needn't handle non-finite values.
Results may differ from the reference program's by a relative error of at most 0.025.
Values may be sent and summed in bfloat16 or wider, within the bound.
No kernel may reach another device: no remote copies, remote signals or barrier semaphores. Data moves between devices by JAX's collectives and lax.ppermute only.
A program may use at most 128 MiB of HBM per device.

```python
import jax
import jax.numpy as jnp
from jax import lax

DT = 1536
AW = 768
TOK_TILE = 64
TILES_DEV = 16
SH = 16
HS = 48
CONFIGS = 5
DS = 768
SLIDES = 4
SLIDE_LEN = 1024
N_SEQ = 2
N_FSDP = 32


def draw_tile_counts(key, part):
    key = jax.random.fold_in(key, 5)
    full_key = jax.random.fold_in(key, 1)
    rest_key = jax.random.fold_in(key, 2)
    full_slide = jax.random.randint(full_key, (), 0, SLIDES).astype(jnp.int32)
    others = jax.random.randint(rest_key, (SLIDES,), SLIDE_LEN // 4, SLIDE_LEN + 1).astype(jnp.int32)
    slots = jnp.arange(SLIDES, dtype=jnp.int32)
    return jnp.where(slots == full_slide, jnp.int32(SLIDE_LEN), others).astype(jnp.int32)


def draw_seg_lengths(key, part):
    key = jax.random.fold_in(key, 11)
    order = jax.random.permutation(key, CONFIGS).astype(jnp.int32)
    return jnp.left_shift(jnp.full((CONFIGS,), SLIDE_LEN // 16, jnp.int32), order)


def draw_dilation(key, part):
    key = jax.random.fold_in(key, 23)
    order = jax.random.permutation(key, CONFIGS).astype(jnp.int32)
    return jnp.left_shift(jnp.ones((CONFIGS,), jnp.int32), order)


def draw_qkv_weight(key, part):
    key = jax.random.fold_in(key, 37)
    base_key = jax.random.fold_in(key, 1)
    base = jax.random.truncated_normal(base_key, -4.0, 4.0, (DS, 3 * DS), jnp.float32) * DS ** (-0.5)
    return base.astype(jnp.bfloat16)


def levels(rng, dims, shards, least, high):
    factor_of, own = 1.0, jax.random.fold_in(rng, 6)
    for axis_at, parts in shards:
        steps = jnp.exp(jax.random.uniform(jax.random.fold_in(own, axis_at), (parts,), jnp.float32, least / len(shards), high / len(shards)))
        factor_of = factor_of * jnp.repeat(steps, dims[axis_at] // parts).reshape([-1 if axis == axis_at else 1 for axis in range(len(dims))])
    return factor_of


def gaussian(stream_key, dims, spread, bound, shards=(), held_as=jnp.bfloat16):
    values = jax.random.normal(stream_key, dims, jnp.float32) * spread
    if len(shards) > 0:
        values = levels(stream_key, dims, shards, -0.22, 0.18) * values
    return jnp.clip(values, min=-bound, max=bound).astype(held_as)


def setup_inputs(seed: int = 0) -> dict:
    streams_of = jax.random.split(jax.random.key(seed), 11)
    return {
        "head_out": gaussian(streams_of[0], (SLIDES, SLIDE_LEN * TOK_TILE, AW), 1.0, 6.0, ((0, 4), (1, 64))),
        "proj_weight": gaussian(streams_of[1], (AW, DT), AW ** -0.5, 0.21875, ((0, 32),)),
        "norm_gain": jnp.clip(1.0 + 0.18 * jax.random.normal(streams_of[2], (DT,), jnp.float32), 0.1, 1.9),
        "embed_cot": gaussian(streams_of[3], (SLIDES, SLIDE_LEN, DT), 16.0, 96.0, ((0, 4), (1, 64))),
        "tile_counts": draw_tile_counts(jax.random.fold_in(streams_of[10], 71), 0),
        "seg_lengths": draw_seg_lengths(jax.random.fold_in(streams_of[10], 71), 0),
        "dilation": draw_dilation(jax.random.fold_in(streams_of[10], 71), 0),
        "embed_weight": gaussian(streams_of[7], (DT, DS), (DT // TOK_TILE) ** -0.5, 1.25, ((0, 32),)),
        "qkv_weight": draw_qkv_weight(jax.random.fold_in(streams_of[10], 71), 0),
        "out_weight": gaussian(streams_of[9], (DS, DS), (DS // 4) ** -0.5, 0.4375, ((0, 32),)),
    }


def multiplicity(query_pos, key_pos, seg_lengths, dilation, heads):
    head_ids = jnp.arange(heads, dtype=jnp.int32)
    counted = jnp.zeros((heads, query_pos.shape[0], key_pos.shape[0]), jnp.float32)
    for config in range(seg_lengths.shape[0]):
        width = seg_lengths[config]
        stride = dilation[config]
        same_seg = query_pos[:, None] // width == key_pos[None, :] // width
        same_res = query_pos[:, None] % stride == key_pos[None, :] % stride
        on_head = query_pos[None, :] % stride == head_ids[:, None] % stride
        joined = on_head[:, :, None] & (same_seg & same_res)[None]
        counted = counted + jnp.where(joined, 1.0, 0.0).astype(jnp.float32)
    return counted

def reference(head_out, proj_weight, norm_gain, embed_cot, tile_counts, seg_lengths, dilation, embed_weight, qkv_weight, out_weight):
    blocks = SLIDES * N_SEQ * N_FSDP
    rows_blk = TILES_DEV * TOK_TILE
    tokens_all = head_out.reshape(blocks, rows_blk, AW)
    cot_all = embed_cot.reshape(blocks, TILES_DEV, DT)
    tile_pos = jnp.arange(SLIDE_LEN, dtype=jnp.int32)
    tile_ok = (tile_pos[None, :] < tile_counts[:, None]).astype(jnp.float32)
    ok_all = tile_ok.reshape(blocks, TILES_DEV)

    def one_block(grad_acc, items):
        tokens_in, cotan, okay = items
        mixed = jnp.dot(tokens_in, proj_weight, preferred_element_type=jnp.float32)
        centre = lax.optimization_barrier(jnp.mean(mixed, axis=-1, keepdims=True))
        shifted = mixed - centre
        inv_std = lax.rsqrt(lax.optimization_barrier(jnp.mean(shifted * shifted, axis=-1, keepdims=True)) + 1e-06)
        normed = shifted * inv_std
        scaled = normed * norm_gain
        embeds = lax.optimization_barrier(jnp.mean(scaled.reshape(TILES_DEV, TOK_TILE, DT), axis=1)).astype(jnp.bfloat16)
        coef = cotan.astype(jnp.float32) * okay[:, None] / TOK_TILE
        grad_scaled = jnp.broadcast_to(coef[:, None, :], (TILES_DEV, TOK_TILE, DT)).reshape(rows_blk, DT)
        grad_normed = grad_scaled * norm_gain
        grad_mixed = inv_std * (grad_normed - lax.optimization_barrier(jnp.mean(grad_normed, axis=-1, keepdims=True)) - normed * lax.optimization_barrier(jnp.mean(grad_normed * normed, axis=-1, keepdims=True)))
        grad_mixed = grad_mixed.astype(jnp.bfloat16)
        grad_in = lax.dot_general(grad_mixed, proj_weight, (((1,), (1,)), ((), ())), preferred_element_type=jnp.float32).astype(jnp.bfloat16)
        term = lax.dot_general(tokens_in, grad_mixed, (((0,), (0,)), ((), ())), preferred_element_type=jnp.float32)
        return (grad_acc + term.astype(jnp.bfloat16).astype(jnp.float32), (embeds, grad_in))
    grad_acc, (embeds, grads_in) = lax.scan(one_block, jnp.zeros((AW, DT), jnp.float32), (tokens_all, cot_all, ok_all))
    proj_grad = grad_acc.astype(jnp.bfloat16)
    head_out_grad = grads_in.reshape(SLIDES, SLIDE_LEN * TOK_TILE, AW)
    embeds = embeds.reshape(SLIDES * SLIDE_LEN, DT)
    hidden = jnp.dot(embeds, embed_weight, preferred_element_type=jnp.float32).astype(jnp.bfloat16)
    qkv = jnp.dot(hidden, qkv_weight, preferred_element_type=jnp.float32).astype(jnp.bfloat16)
    qkv = qkv.reshape(SLIDES, SLIDE_LEN, 3, SH, HS)
    queries = qkv[:, :, 0].astype(jnp.float32)
    keys = qkv[:, :, 1].astype(jnp.float32)
    values = qkv[:, :, 2].astype(jnp.float32)
    counted = multiplicity(tile_pos, tile_pos, seg_lengths, dilation, SH)
    scores = jnp.einsum('sihd,sjhd->shij', queries, keys) * HS ** (-0.5)
    allowed = (counted[None] > 0.0) & (tile_ok[:, None, None, :] > 0.0)
    masked = jnp.where(allowed, scores, -1e+30)
    top = lax.optimization_barrier(jnp.max(masked, axis=-1, keepdims=True))
    weights = counted[None] * jnp.exp(masked - top)
    probs = (weights / lax.optimization_barrier(jnp.sum(weights, axis=-1, keepdims=True))).astype(jnp.bfloat16)
    attended = jnp.einsum('shij,sjhd->sihd', probs.astype(jnp.float32), values).astype(jnp.bfloat16)
    attended = attended.reshape(SLIDES * SLIDE_LEN, DS)
    mixed_out = hidden.astype(jnp.float32) + jnp.dot(attended, out_weight, preferred_element_type=jnp.float32)
    slide_out = (mixed_out.reshape(SLIDES, SLIDE_LEN, DS) * tile_ok[:, :, None]).astype(jnp.bfloat16)
    return (slide_out, head_out_grad, proj_grad)
```

```python
import functools

import jax
import jax.numpy as jnp
from jax import lax
from jax.experimental import pallas as pl
from jax.experimental.pallas import tpu as pltpu
from jax.sharding import PartitionSpec as P

HS = 48
NZ, NY = 8, 4
Z_GROUPS = [[z * NY + y for z in range(NZ)] for y in range(NY)]
Y_GROUPS = [[z * NY + y for y in range(NY)] for z in range(NZ)]
SWAP = [(0, 1), (1, 0)]
F32, BF16 = jnp.float32, jnp.bfloat16


def a2a_z(v):
    return lax.all_to_all(v, "fsdp", 0, 0, axis_index_groups=Z_GROUPS)


def a2a_y(v):
    return lax.all_to_all(v, "fsdp", 0, 0, axis_index_groups=Y_GROUPS)


def copies(v, n):
    return jnp.broadcast_to(v[None], (n,) + v.shape)


def gather_zy(v):
    return a2a_y(copies(a2a_z(copies(v, NZ)), NY))


def swap(v):
    return lax.ppermute(v, "seq", SWAP)


def attend_kernel(heads, own_ref, other_ref, wq_ref, wk_ref, wv_ref, featq_ref, featk_ref, out_ref, k_ref, v_ref, q_ref):
    rows = own_ref.shape[0]
    width = heads * HS
    dot = functools.partial(jnp.dot, preferred_element_type=F32)
    q_ref[...] = dot(own_ref[...], wq_ref[...]).astype(BF16)
    for at, ref in enumerate((own_ref, other_ref)):
        span = pl.ds(at * rows, rows)
        k_ref[span, :] = dot(ref[...], wk_ref[...]).astype(BF16)
        v_ref[span, :] = dot(ref[...], wv_ref[...]).astype(BF16)
    lane_head = lax.broadcasted_iota(jnp.int32, (1, width), 1) // HS
    scale = HS ** (-0.5) * 1.4426950408889634
    block = 128
    for head in range(heads):
        mine = lane_head == head
        keys = k_ref[...]
        values = jnp.where(mine, v_ref[...], 0).astype(BF16)
        for start in range(0, rows, block):
            span = pl.ds(start, block)
            queries = jnp.where(mine, q_ref[span, :], 0).astype(BF16)
            scores = lax.dot_general(queries, keys, (((1,), (1,)), ((), ())), preferred_element_type=F32) * scale
            counted = lax.dot_general(
                featq_ref[head, span, :], featk_ref[head], (((1,), (1,)), ((), ())), preferred_element_type=F32
            )
            masked = jnp.where(counted > 0.0, scores, -1e30)
            top = jnp.max(masked, axis=-1, keepdims=True)
            weights = counted * jnp.exp2(masked - top)
            total = jnp.maximum(jnp.sum(weights, axis=-1, keepdims=True), 0.5)
            probs = (weights * (1.0 / total)).astype(BF16)
            part = dot(probs, values)
            if head == 0:
                out_ref[span, :] = part.astype(BF16)
            else:
                out_ref[span, :] = jnp.where(mine, part.astype(BF16), out_ref[span, :])


def attend(own, other, wq, wk, wv, featq, featk):
    rows, width = own.shape[0], wq.shape[1]
    heads = width // HS
    vmem = pl.BlockSpec(memory_space=pltpu.VMEM)
    return pl.pallas_call(
        functools.partial(attend_kernel, heads),
        out_shape=jax.ShapeDtypeStruct((rows, width), BF16),
        in_specs=[vmem] * 7,
        out_specs=vmem,
        scratch_shapes=[
            pltpu.VMEM((2 * rows, width), BF16),
            pltpu.VMEM((2 * rows, width), BF16),
            pltpu.VMEM((rows, width), BF16),
        ],
        compiler_params=pltpu.CompilerParams(vmem_limit_bytes=40 * 1024 * 1024),
        cost_estimate=pl.CostEstimate(flops=3_000_000_000, bytes_accessed=5_000_000, transcendentals=2_000_000),
        name="attend",
    )(own, other, wq, wk, wv, featq, featk)


def features(pos, seg_lengths, dilation, head_ids, span):
    ids = span // seg_lengths[None, :] + pos[:, None] // seg_lengths[None, :]
    on = pos[None, :, None] % dilation[None, None, :] == head_ids[:, None, None] % dilation[None, None, :]
    columns = jnp.arange(128, dtype=jnp.int32)
    feats = jnp.zeros((head_ids.shape[0], pos.shape[0], 128), jnp.bool_)
    for config in range(seg_lengths.shape[0]):
        feats = feats | ((ids[:, config][None, :, None] == columns[None, None, :]) & on[:, :, config][:, :, None])
    return feats


def body(
    head_out,
    proj_weight,
    norm_gain,
    embed_cot,
    tile_counts,
    seg_lengths,
    dilation,
    embed_weight,
    qkv_weight,
    out_weight,
):
    tokens = head_out[0]
    n_rows, aw = tokens.shape
    dt = proj_weight.shape[1]
    half = dt // 2
    tiles = embed_cot.shape[1]
    per_tile = n_rows // tiles
    fsdp = NZ * NY
    f = lax.axis_index("fsdp")
    s = lax.axis_index("seq")
    count = tile_counts[0]
    ds = out_weight.shape[1]
    shard_len = fsdp * tiles
    slide_len = 2 * shard_len

    proj_mine = (
        gather_zy(lax.dynamic_slice_in_dim(proj_weight, s * half, half, 1)).transpose(1, 0, 2, 3).reshape(aw, half)
    )
    proj_other = swap(proj_mine)

    def halves(v, axis):
        return (
            lax.dynamic_slice_in_dim(v, s * half, half, axis),
            lax.dynamic_slice_in_dim(v, (1 - s) * half, half, axis),
        )

    def half_rows(v):
        n = v.shape[0] // 2
        return lax.dynamic_slice_in_dim(v, s * n, n, 0)

    rows_e = embed_weight.shape[0] // 2
    packed = jnp.concatenate([half_rows(embed_weight), half_rows(out_weight)], axis=0)
    packed = gather_zy(packed)
    packed_other = swap(packed)
    both = jnp.stack([jnp.where(s == 0, packed, packed_other), jnp.where(s == 0, packed_other, packed)])
    both = both.transpose(2, 1, 0, 3, 4)
    w_embed = both[:, :, :, :rows_e].reshape(dt, ds)
    w_out = both[:, :, :, rows_e:].reshape(ds, ds)

    heads = ds // HS // NY
    width = heads * HS
    w_heads = half_rows(qkv_weight)
    n_half = w_heads.shape[0]
    w_heads = w_heads.reshape(n_half, 3, NY, width).transpose(2, 1, 0, 3)
    w_heads = a2a_z(copies(a2a_y(w_heads), NZ))
    w_other = swap(w_heads)
    w_heads = jnp.stack([jnp.where(s == 0, w_heads, w_other), jnp.where(s == 0, w_other, w_heads)])
    w_heads = w_heads.transpose(3, 1, 2, 0, 4, 5).reshape(3, ds, width)

    local = (
        (jnp.arange(NZ, dtype=jnp.int32)[None, :, None] * NY + jnp.arange(NY, dtype=jnp.int32)[:, None, None]) * tiles
        + jnp.arange(tiles, dtype=jnp.int32)
    ).reshape(shard_len)
    query_pos = s * shard_len + local
    key_pos = jnp.concatenate([query_pos, (1 - s) * shard_len + local])
    head_ids = (f % NY) * heads + jnp.arange(heads, dtype=jnp.int32)
    feats = features(key_pos, seg_lengths, dilation, head_ids, slide_len)
    featq = feats[:, :shard_len].astype(BF16)
    featk = (feats & (key_pos < count)[None, :, None]).astype(BF16)

    gain = halves(norm_gain, 0)
    cot = halves(embed_cot[0].astype(F32), 1)
    proj = (proj_mine, proj_other)
    mixed = [jnp.dot(tokens, w, preferred_element_type=F32) for w in proj]
    centre = sum(jnp.sum(m, axis=-1, keepdims=True) for m in mixed) / dt
    shifted = [m - centre for m in mixed]
    inv_std = lax.rsqrt(sum(jnp.sum(m * m, axis=-1, keepdims=True) for m in shifted) / dt + 1e-06)
    normed = [m * inv_std for m in shifted]
    embed = [
        (jnp.mean(n.reshape(tiles, per_tile, half), axis=1) * g).astype(BF16) for n, g in zip(normed, gain)
    ]
    embed = jnp.concatenate(
        [jnp.where(s == 0, embed[0], embed[1]), jnp.where(s == 0, embed[1], embed[0])], axis=1
    )
    hidden = jnp.dot(embed, w_embed, preferred_element_type=F32).astype(BF16)
    hidden = gather_zy(hidden).reshape(shard_len, ds)
    hidden_other = swap(hidden)

    base = (s * fsdp + f) * tiles
    valid = (base + jnp.arange(tiles, dtype=jnp.int32) < count).astype(F32)
    grad_normed = [c * valid[:, None] / per_tile * g for c, g in zip(cot, gain)]
    grad_mean = sum(jnp.sum(g, axis=-1, keepdims=True) for g in grad_normed) / dt

    def per_token(v):
        return jnp.broadcast_to(v[:, None, :], (tiles, per_tile, v.shape[1])).reshape(n_rows, v.shape[1])

    along = sum(jnp.sum(per_token(g) * n, axis=-1, keepdims=True) for g, n in zip(grad_normed, normed)) / dt
    grad_mixed = [
        (inv_std * (per_token(g - grad_mean) - n * along)).astype(BF16) for g, n in zip(grad_normed, normed)
    ]
    grad_in = sum(
        lax.dot_general(g, w, (((1,), (1,)), ((), ())), preferred_element_type=F32) for g, w in zip(grad_mixed, proj)
    )
    head_out_grad = grad_in.astype(BF16)[None]
    term_mine, term_other = [
        lax.dot_general(tokens, g, (((0,), (0,)), ((), ())), preferred_element_type=F32).astype(BF16)
        for g in grad_mixed
    ]
    pair = (term_mine.astype(F32) + swap(term_other).astype(F32)).astype(BF16)
    nx = lax.axis_size("slide")
    quarter = half // nx
    share = lax.all_to_all(pair.reshape(aw, nx, quarter).transpose(1, 0, 2), "slide", 0, 0)
    share = jnp.sum(share.astype(F32), axis=0).astype(BF16)
    share = a2a_y(share.reshape(NZ, NY, aw // fsdp, quarter).transpose(1, 0, 2, 3))
    share = jnp.sum(share.astype(F32), axis=0).astype(BF16)
    share = jnp.sum(a2a_z(share).astype(F32), axis=0).astype(BF16)
    share = lax.all_to_all(copies(share, 2 * nx), ("slide", "seq"), 0, 0)
    proj_grad = share.reshape(nx, 2, aw // fsdp, quarter).transpose(2, 1, 0, 3).reshape(aw // fsdp, dt)

    attended = attend(hidden, hidden_other, w_heads[0], w_heads[1], w_heads[2], featq, featk)
    attended = a2a_y(copies(attended, NY)).transpose(1, 0, 2).reshape(shard_len, ds)
    mixed_out = hidden.astype(F32) + jnp.dot(attended, w_out, preferred_element_type=F32)
    slide_out = jnp.where((query_pos < count)[:, None], mixed_out, 0.0).astype(BF16)
    slide_out = slide_out.reshape(NY, NZ, tiles, ds).transpose(1, 0, 2, 3).reshape(1, shard_len, ds)
    return (slide_out, head_out_grad, proj_grad)


def solution(mesh):
    return jax.shard_map(
        body,
        mesh=mesh,
        in_specs=(
            P("slide", ("seq", "fsdp"), None),
            P("fsdp", None),
            P(),
            P("slide", ("seq", "fsdp"), None),
            P("slide"),
            P(),
            P(),
            P("fsdp", None),
            P("fsdp", None),
            P("fsdp", None),
        ),
        out_specs=(P("slide", "seq", None), P("slide", ("seq", "fsdp"), None), P("fsdp", None)),
        check_vma=False,
    )
```

```python
import functools

import jax
import jax.numpy as jnp
from jax import lax
from jax.experimental import pallas as pl
from jax.experimental.pallas import tpu as pltpu
from jax.sharding import PartitionSpec as P

HS = 48
NX, NZ, NY = 4, 8, 4
Z_GROUPS = [[z * NY + y for z in range(NZ)] for y in range(NY)]
Y_GROUPS = [[z * NY + y for y in range(NY)] for z in range(NZ)]
SWAP = [(0, 1), (1, 0)]
F32, BF16 = jnp.float32, jnp.bfloat16
VMEM = pl.BlockSpec(memory_space=pltpu.VMEM)
SMEM = pl.BlockSpec(memory_space=pltpu.SMEM)
CONTRACT_LAST = (((1,), (1,)), ((), ()))
CONTRACT_FIRST = (((0,), (0,)), ((), ()))
dot = functools.partial(jnp.dot, preferred_element_type=F32)
dot_general = functools.partial(lax.dot_general, preferred_element_type=F32)


def a2a_z(v):
    return lax.all_to_all(v, "fsdp", 0, 0, axis_index_groups=Z_GROUPS)


def a2a_y(v):
    return lax.all_to_all(v, "fsdp", 0, 0, axis_index_groups=Y_GROUPS)


def copies(v, n):
    return jnp.broadcast_to(v[None], (n,) + v.shape)


def swap(v):
    return lax.ppermute(v, "seq", SWAP)


def shift_y(v, k):
    return lax.ppermute(
        v, "fsdp", [(z * NY + y, z * NY + (y + k) % NY) for z in range(NZ) for y in range(NY)]
    )


def shift_x(v, k):
    return lax.ppermute(v, "slide", [(x, (x + k) % NX) for x in range(NX)])


def after(v, other):
    return v + (other[(0,) * other.ndim] * 0).astype(v.dtype)


def params(mib):
    return pltpu.CompilerParams(vmem_limit_bytes=mib * 1024 * 1024)


def cost(gflop, mb, mexp=0):
    return pl.CostEstimate(
        flops=int(gflop * 1e9), bytes_accessed=int(mb * 1e6), transcendentals=int(mexp * 1e6)
    )


def normalise(tok, pm_ref, po_ref):
    mixed = [dot(tok, pm_ref[...]), dot(tok, po_ref[...])]
    width = 2 * mixed[0].shape[1]
    centre = sum(jnp.sum(m, axis=-1, keepdims=True) for m in mixed) * (1.0 / width)
    shifted = [m - centre for m in mixed]
    var = sum(jnp.sum(m * m, axis=-1, keepdims=True) for m in shifted) * (1.0 / width)
    inv_std = lax.rsqrt(var + 1e-06)
    return [m * inv_std for m in shifted], inv_std


def forward_kernel(tiles, at_ref, tok_ref, pm_ref, po_ref, gain_ref, out_ref):
    normed, _ = normalise(tok_ref[...], pm_ref, po_ref)
    rows, half = normed[0].shape
    pooled = []
    for i, n in enumerate(normed):
        mean = jnp.sum(n.reshape(tiles, rows // tiles, half), axis=1) * (tiles / rows)
        pooled.append(mean * gain_ref[i : i + 1, :])
    span = pl.ds(pl.multiple_of(pl.program_id(0) * tiles, tiles), tiles)
    for s in range(2):

        @pl.when(at_ref[0] == s)
        def _():
            out_ref[span, :half] = pooled[s]
            out_ref[span, half:] = pooled[1 - s]


def forward(at, tokens, pm, po, gain, tiles):
    rows, aw = tokens.shape
    half = pm.shape[1]
    steps = 2
    return pl.pallas_call(
        functools.partial(forward_kernel, tiles // steps),
        out_shape=jax.ShapeDtypeStruct((tiles, 2 * half), F32),
        grid=(steps,),
        in_specs=[SMEM, pl.BlockSpec((rows // steps, aw), lambda i: (i, 0)), VMEM, VMEM, VMEM],
        out_specs=pl.BlockSpec((tiles, 2 * half), lambda i: (0, 0)),
        compiler_params=params(48),
        cost_estimate=cost(2.4, 4),
        name="forward",
    )(at, tokens, pm, po, gain)


def backward_kernel(tok_ref, pm_ref, po_ref, gm_ref, go_ref, grad_ref, tm_ref, to_ref, am_ref, ao_ref):
    step, steps = pl.program_id(0), pl.num_programs(0)
    tok = tok_ref[...]
    normed, inv_std = normalise(tok, pm_ref, po_ref)
    rows, half = normed[0].shape
    tiles = gm_ref.shape[1]
    grads = [gm_ref[0], go_ref[0]]
    mean = sum(jnp.sum(g, axis=-1, keepdims=True) for g in grads) * (0.5 / half)

    def per_token(v):
        return jnp.broadcast_to(v[:, None, :], (tiles, rows // tiles, v.shape[1])).reshape(rows, v.shape[1])

    along = sum(jnp.sum(per_token(g) * n, axis=-1, keepdims=True) for g, n in zip(grads, normed)) * (0.5 / half)
    mixed = [(inv_std * (per_token(g - mean) - n * along)).astype(BF16) for g, n in zip(grads, normed)]
    grad_in = dot_general(mixed[0], pm_ref[...], CONTRACT_LAST) + dot_general(mixed[1], po_ref[...], CONTRACT_LAST)
    grad_ref[...] = grad_in.astype(BF16)
    for acc_ref, term_ref, m in ((am_ref, tm_ref, mixed[0]), (ao_ref, to_ref, mixed[1])):
        term = dot_general(tok, m, CONTRACT_FIRST)

        @pl.when(step == 0)
        def _():
            acc_ref[...] = term

        @pl.when(step > 0)
        def _():
            acc_ref[...] += term

        @pl.when(step == steps - 1)
        def _():
            block = term_ref.shape[2]
            for z in range(NZ):
                for y in range(NY):
                    term_ref[y, z] = acc_ref[pl.ds((z * NY + y) * block, block), :].astype(BF16)


def backward(tokens, pm, po, grads):
    rows, aw = tokens.shape
    half = pm.shape[1]
    tiles = grads[0].shape[0]
    steps = 4
    grads = [g.reshape(steps, tiles // steps, half) for g in grads]
    gspec = pl.BlockSpec((1, tiles // steps, half), lambda i: (i, 0, 0))
    tspec = pl.BlockSpec((NY, NZ, aw // (NY * NZ), half), lambda i: (0, 0, 0, 0))
    term = jax.ShapeDtypeStruct((NY, NZ, aw // (NY * NZ), half), BF16)
    tok_spec = pl.BlockSpec((rows // steps, aw), lambda i: (i, 0))
    return pl.pallas_call(
        backward_kernel,
        out_shape=(jax.ShapeDtypeStruct((rows, aw), BF16), term, term),
        grid=(steps,),
        in_specs=[tok_spec, VMEM, VMEM, gspec, gspec],
        out_specs=(tok_spec, tspec, tspec),
        scratch_shapes=[pltpu.VMEM((aw, half), F32), pltpu.VMEM((aw, half), F32)],
        compiler_params=params(48),
        cost_estimate=cost(7.2, 8),
        name="backward",
    )(tokens, pm, po, *grads)


def place(row, s):
    return s * 512 + ((row // 16) % NZ * NY + row // (16 * NZ)) * 16 + row % 16


def features_kernel(heads, at_ref, seg_ref, dil_ref, q_ref, k_ref):
    s, y, count = at_ref[0], at_ref[1], at_ref[2]
    rows = q_ref.shape[1]

    def fill(ref, pos, valid):
        lane = lax.broadcasted_iota(jnp.int32, pos.shape, 1)
        hits, residues = [], []
        for c in range(seg_ref.shape[0]):
            width = seg_ref[c]
            bits = 6 + sum((width > 64 << b).astype(jnp.int32) for b in range(4))
            ids = lax.shift_right_logical(jnp.full_like(pos, 2 * rows), jnp.full_like(pos, bits))
            ids = ids + lax.shift_right_logical(pos, jnp.full_like(pos, bits))
            hits.append((ids == lane) & valid)
            residues.append(pos & (dil_ref[c] - 1))
        for h in range(heads):
            head = y * heads + h
            any_hit = None
            for c, (hit, residue) in enumerate(zip(hits, residues)):
                hit = hit & (residue == (head & (dil_ref[c] - 1)))
                any_hit = hit if any_hit is None else any_hit | hit
            ref[h] = jnp.where(any_hit, 1.0, 0.0).astype(BF16)

    row = lax.broadcasted_iota(jnp.int32, (rows, 128), 0)
    pos = place(row, s)
    fill(q_ref, pos, pos >= 0)
    row = lax.broadcasted_iota(jnp.int32, (2 * rows, 128), 0)
    pos = place(row // 32 * 16 + row % 16, row // 16 % 2)
    fill(k_ref, pos, pos < count)


def features(at, seg_lengths, dilation, heads, rows):
    return pl.pallas_call(
        functools.partial(features_kernel, heads),
        out_shape=(
            jax.ShapeDtypeStruct((heads, rows, 128), BF16),
            jax.ShapeDtypeStruct((heads, 2 * rows, 128), BF16),
        ),
        in_specs=[SMEM] * 3,
        out_specs=(VMEM, VMEM),
        compiler_params=params(32),
        cost_estimate=cost(0.01, 2),
        name="features",
    )(at, seg_lengths, dilation)


def attend_kernel(heads, at_ref, hm_ref, ho_ref, wm_ref, wo_ref, fq_ref, fk_ref, out_ref, w_ref, q_ref, k_ref, v_ref):
    s = at_ref[0]
    groups, _, tiles, half = hm_ref.shape
    rows = groups * tiles
    seg = w_ref.shape[-1] // 3
    for z in range(NZ):
        w_ref[z, s] = wm_ref[z]
        w_ref[z, 1 - s] = wo_ref[z]
    w_mine = w_ref[pl.ds(s * (NZ // 2), NZ // 2)].reshape(half, 3 * seg)
    w_other = w_ref[pl.ds((1 - s) * (NZ // 2), NZ // 2)].reshape(half, 3 * seg)
    hm = hm_ref[...].reshape(2 * rows, half)
    ho = ho_ref[...].reshape(2 * rows, half)

    def project(at):
        lanes = slice(at * seg, (at + 1) * seg)
        return (dot(hm, w_mine[:, lanes]) + dot(ho, w_other[:, lanes])).astype(BF16)

    q_ref[...] = project(0).reshape(groups, 2, tiles, seg)
    k_ref[...] = project(1)
    v_ref[...] = project(2)
    queries_all = q_ref[:, s].reshape(rows, seg)
    lane_head = lax.broadcasted_iota(jnp.int32, (1, seg), 1) // HS
    scale = HS ** (-0.5) * 1.4426950408889634
    block = 128
    for head in range(heads):
        for start in range(0, rows, block):
            span = pl.ds(start, block)
            queries = jnp.where(lane_head == head, queries_all[start : start + block], 0).astype(BF16)
            scores = dot_general(queries, k_ref[...], CONTRACT_LAST) * scale
            counted = dot_general(fq_ref[head, span, :], fk_ref[head], CONTRACT_LAST)
            masked = jnp.where(counted > 0.0, scores, -1e30)
            top = jnp.max(masked, axis=-1, keepdims=True)
            weights = counted * jnp.exp2(masked - top)
            total = jnp.maximum(jnp.sum(weights, axis=-1, keepdims=True), 0.5)
            probs = (weights * (1.0 / total)).astype(BF16)
            part = dot(probs, v_ref[...]).T
            out_ref[head * HS : (head + 1) * HS, span] = part[head * HS : (head + 1) * HS].astype(BF16)


def attend(at, hm, ho, wm, wo, fq, fk, heads):
    groups, _, tiles, half = hm.shape
    rows = groups * tiles
    seg = wm.shape[-1] // 3
    return pl.pallas_call(
        functools.partial(attend_kernel, heads),
        out_shape=jax.ShapeDtypeStruct((heads * HS, rows), BF16),
        in_specs=[SMEM] + [VMEM] * 6,
        out_specs=VMEM,
        scratch_shapes=[
            pltpu.VMEM((NZ, 2, wm.shape[1], 3 * seg), BF16),
            pltpu.VMEM((groups, 2, tiles, seg), BF16),
            pltpu.VMEM((2 * rows, seg), BF16),
            pltpu.VMEM((2 * rows, seg), BF16),
        ],
        compiler_params=params(48),
        cost_estimate=cost(6, 6, 2),
        name="attend",
    )(at, hm, ho, wm, wo, fq, fk)


def finish_kernel(at_ref, att_ref, w_ref, hm_ref, ho_ref, out_ref):
    s, count = at_ref[0], at_ref[2]
    groups, _, tiles, half = hm_ref.shape
    rows = groups * tiles
    mixed = dot_general(att_ref[...], w_ref[...], CONTRACT_FIRST)
    hm = hm_ref[:, s].reshape(rows, half).astype(F32)
    ho = ho_ref[:, s].reshape(rows, half).astype(F32)
    row = lax.broadcasted_iota(jnp.int32, (rows, half), 0)
    valid = place(row, s) < count
    left = jnp.where(valid, mixed[:, :half] + jnp.where(s == 0, hm, ho), 0.0).astype(BF16)
    right = jnp.where(valid, mixed[:, half:] + jnp.where(s == 0, ho, hm), 0.0).astype(BF16)
    span = NZ * tiles
    for y in range(NY):
        for part, lanes in ((left, slice(0, half)), (right, slice(half, 2 * half))):
            out_ref[:, y, :, lanes] = part[y * span : (y + 1) * span].reshape(NZ, tiles, half)


def finish(at, att, w_out, hm, ho):
    groups, _, tiles, half = hm.shape
    return pl.pallas_call(
        finish_kernel,
        out_shape=jax.ShapeDtypeStruct((NZ, NY, tiles, 2 * half), BF16),
        in_specs=[SMEM] + [VMEM] * 4,
        out_specs=VMEM,
        compiler_params=params(32),
        cost_estimate=cost(0.6, 4),
        name="finish",
    )(at, att, w_out, hm, ho)


def body(
    head_out,
    proj_weight,
    norm_gain,
    embed_cot,
    tile_counts,
    seg_lengths,
    dilation,
    embed_weight,
    qkv_weight,
    out_weight,
):
    tokens = head_out[0]
    n_rows, aw = tokens.shape
    dt = proj_weight.shape[1]
    half = dt // 2
    tiles = embed_cot.shape[1]
    per_tile = n_rows // tiles
    fsdp = NZ * NY
    f = lax.axis_index("fsdp")
    s = lax.axis_index("seq")
    y = f % NY
    count = tile_counts[0]
    ds = out_weight.shape[1]
    shard_len = fsdp * tiles
    at = jnp.stack([s, y, count]).astype(jnp.int32)
    dslice = lax.dynamic_slice_in_dim

    def of_y(v, k):
        return lax.dynamic_index_in_dim(v, (y + k) % NY, 0, keepdims=False)

    embed_half = dslice(embed_weight, s * (ds // 2), ds // 2, 1)
    rows = proj_weight.shape[0]
    first = jnp.concatenate(
        [dslice(proj_weight, s * half, half, 1), jnp.concatenate([embed_half[:rows], embed_half[rows:]], axis=1)],
        axis=0,
    )
    first = a2a_y(copies(a2a_z(copies(first, NZ)), NY))
    proj_mine = first[:, :, :rows].transpose(1, 0, 2, 3).reshape(aw, half)
    proj_other = swap(proj_mine)
    w_embed = first[:, :, rows:].reshape(NY, NZ, rows, 2, ds // 2).transpose(1, 0, 3, 2, 4).reshape(dt, ds // 2)

    heads = ds // HS // NY
    width = heads * HS
    w_heads = qkv_weight.reshape(rows, 3, NY, width).transpose(2, 0, 1, 3)
    w_heads = jnp.pad(w_heads, ((0, 0), (0, 0), (0, 0), (0, 256 - width))).reshape(NY, rows, 3 * 256)
    w_heads = [of_y(w_heads, 0)] + [shift_y(of_y(w_heads, k), k) for k in range(1, NY)]
    w_heads = jnp.stack([w_heads[-j % NY] for j in range(NY)])
    w_heads = dslice(jnp.concatenate([w_heads, w_heads]), (NY - y + 2 * s) % NY, 2, 0).reshape(2 * rows, 3 * 256)
    w_heads = a2a_z(copies(after(w_heads, first), NZ))
    w_heads_other = swap(w_heads)
    w_out = lax.all_gather(out_weight, "fsdp", axis=0, tiled=True)
    feat_q, feat_k = features(at, seg_lengths, dilation, heads, shard_len)

    def halves(v):
        return dslice(v, s * half, half, v.ndim - 1), dslice(v, (1 - s) * half, half, v.ndim - 1)

    gain = halves(norm_gain)
    embed = forward(at, tokens, proj_mine, proj_other, jnp.stack(gain), tiles).astype(BF16)
    embed_other = swap(embed)
    embed = jnp.concatenate([jnp.where(s == 0, embed, embed_other), jnp.where(s == 0, embed_other, embed)])
    hidden = dot(embed, w_embed).astype(BF16)
    hidden = a2a_y(copies(a2a_z(copies(hidden, NZ)), NY)).reshape(fsdp, 2, tiles, ds // 2)
    hidden_other = swap(hidden)

    base = (s * fsdp + f) * tiles
    valid = (base + jnp.arange(tiles, dtype=jnp.int32) < count).astype(F32)
    grads = [c * valid[:, None] / per_tile * g for c, g in zip(halves(embed_cot[0].astype(F32)), gain)]
    head_out_grad, term_mine, term_other = backward(tokens, proj_mine, proj_other, grads)

    pair = (term_mine.astype(F32) + swap(term_other).astype(F32)).astype(BF16)
    parts = [of_y(pair, 0)] + [shift_y(of_y(pair, k), k) for k in range(1, NY)]
    share = sum(p.astype(F32) for p in parts).astype(BF16)
    share = jnp.sum(a2a_z(share).astype(F32), axis=0).astype(BF16)
    share = sum(p.astype(F32) for p in [share] + [shift_x(share, k) for k in range(1, NX)]).astype(BF16)
    other = swap(share)
    proj_grad = jnp.concatenate([jnp.where(s == 0, share, other), jnp.where(s == 0, other, share)], axis=1)

    attended = attend(at, hidden, hidden_other, w_heads, w_heads_other, feat_q, feat_k, heads)
    attended = a2a_y(copies(attended, NY)).reshape(ds, shard_len)
    slide_out = finish(at, attended, w_out, hidden, hidden_other).reshape(1, shard_len, ds)
    return (slide_out, head_out_grad[None], proj_grad)


def solution(mesh):
    return jax.shard_map(
        body,
        mesh=mesh,
        in_specs=(
            P("slide", ("seq", "fsdp"), None),
            P("fsdp", None),
            P(),
            P("slide", ("seq", "fsdp"), None),
            P("slide"),
            P(),
            P(),
            P("fsdp", None),
            P("fsdp", None),
            P("fsdp", None),
        ),
        out_specs=(P("slide", "seq", None), P("slide", ("seq", "fsdp"), None), P("fsdp", None)),
        check_vma=False,
    )
```

```python
import functools

import jax
import jax.numpy as jnp
from jax import lax
from jax.experimental import pallas as pl
from jax.experimental.pallas import tpu as pltpu
from jax.sharding import PartitionSpec as P

HS = 48
NX, NZ, NY = 4, 8, 4
Z_GROUPS = [[z * NY + y for z in range(NZ)] for y in range(NY)]
Y_GROUPS = [[z * NY + y for y in range(NY)] for z in range(NZ)]
SWAP = [(0, 1), (1, 0)]
F32, BF16 = jnp.float32, jnp.bfloat16
VMEM = pl.BlockSpec(memory_space=pltpu.VMEM)
SMEM = pl.BlockSpec(memory_space=pltpu.SMEM)
CONTRACT_LAST = (((1,), (1,)), ((), ()))
CONTRACT_FIRST = (((0,), (0,)), ((), ()))
dot = functools.partial(jnp.dot, preferred_element_type=F32)
dot_general = functools.partial(lax.dot_general, preferred_element_type=F32)


def a2a_z(v):
    return lax.all_to_all(v, "fsdp", 0, 0, axis_index_groups=Z_GROUPS)


def a2a_y(v):
    return lax.all_to_all(v, "fsdp", 0, 0, axis_index_groups=Y_GROUPS)


def copies(v, n):
    return jnp.broadcast_to(v[None], (n,) + v.shape)


def swap(v):
    return lax.ppermute(v, "seq", SWAP)


def shift_y(v, k):
    return lax.ppermute(
        v, "fsdp", [(z * NY + y, z * NY + (y + k) % NY) for z in range(NZ) for y in range(NY)]
    )


def shift_x(v, k):
    return lax.ppermute(v, "slide", [(x, (x + k) % NX) for x in range(NX)])


def after(v, other):
    return v + (other[(0,) * other.ndim] * 0).astype(v.dtype)


def params(mib):
    return pltpu.CompilerParams(vmem_limit_bytes=mib * 1024 * 1024)


def cost(gflop, mb, mexp=0):
    return pl.CostEstimate(
        flops=int(gflop * 1e9), bytes_accessed=int(mb * 1e6), transcendentals=int(mexp * 1e6)
    )


def forward_kernel(tiles, at_ref, tok_ref, pm_ref, po_ref, gain_ref, out_ref, nm_ref, no_ref, inv_ref):
    tok = tok_ref[...]
    mixed = [dot(tok, pm_ref[...]), dot(tok, po_ref[...])]
    rows, half = mixed[0].shape
    centre = sum(jnp.sum(m, axis=-1, keepdims=True) for m in mixed) * (0.5 / half)
    shifted = [m - centre for m in mixed]
    var = sum(jnp.sum(m * m, axis=-1, keepdims=True) for m in shifted) * (0.5 / half)
    inv_std = lax.rsqrt(var + 1e-06)
    inv_ref[...] = jnp.broadcast_to(inv_std, inv_ref.shape)
    pooled = []
    for i, (m, n_ref) in enumerate(zip(shifted, (nm_ref, no_ref))):
        n = m * inv_std
        n_ref[...] = n
        mean = jnp.sum(n.reshape(tiles, rows // tiles, half), axis=1) * (tiles / rows)
        pooled.append(mean * gain_ref[i : i + 1, :])
    span = pl.ds(pl.multiple_of(pl.program_id(0) * tiles, tiles), tiles)
    for s in range(2):

        @pl.when(at_ref[0] == s)
        def _():
            out_ref[span, :half] = pooled[s]
            out_ref[span, half:] = pooled[1 - s]


def forward(at, tokens, pm, po, gain, tiles):
    rows, aw = tokens.shape
    half = pm.shape[1]
    steps = 2
    spec = pl.BlockSpec((rows // steps, half), lambda i: (i, 0))
    return pl.pallas_call(
        functools.partial(forward_kernel, tiles // steps),
        out_shape=(
            jax.ShapeDtypeStruct((tiles, 2 * half), F32),
            jax.ShapeDtypeStruct((rows, half), F32),
            jax.ShapeDtypeStruct((rows, half), F32),
            jax.ShapeDtypeStruct((rows, 128), F32),
        ),
        grid=(steps,),
        in_specs=[SMEM, pl.BlockSpec((rows // steps, aw), lambda i: (i, 0)), VMEM, VMEM, VMEM],
        out_specs=(
            pl.BlockSpec((tiles, 2 * half), lambda i: (0, 0)),
            spec,
            spec,
            pl.BlockSpec((rows // steps, 128), lambda i: (i, 0)),
        ),
        compiler_params=params(48),
        cost_estimate=cost(2.4, 10),
        name="forward",
    )(at, tokens, pm, po, gain)


def backward_kernel(tok_ref, nm_ref, no_ref, inv_ref, gm_ref, go_ref, xm_ref, xo_ref, tm_ref, to_ref, am_ref, ao_ref):
    step, steps = pl.program_id(0), pl.num_programs(0)
    tok = tok_ref[...]
    normed = [nm_ref[...], no_ref[...]]
    inv_std = inv_ref[:, :1]
    rows, half = normed[0].shape
    tiles = gm_ref.shape[1]
    grads = [gm_ref[0], go_ref[0]]
    mean = sum(jnp.sum(g, axis=-1, keepdims=True) for g in grads) * (0.5 / half)

    def per_token(v):
        return jnp.broadcast_to(v[:, None, :], (tiles, rows // tiles, v.shape[1])).reshape(rows, v.shape[1])

    along = sum(jnp.sum(per_token(g) * n, axis=-1, keepdims=True) for g, n in zip(grads, normed)) * (0.5 / half)
    mixed = [(inv_std * (per_token(g - mean) - n * along)).astype(BF16) for g, n in zip(grads, normed)]
    xm_ref[...] = mixed[0]
    xo_ref[...] = mixed[1]
    for acc_ref, term_ref, m in ((am_ref, tm_ref, mixed[0]), (ao_ref, to_ref, mixed[1])):
        term = dot_general(tok, m, CONTRACT_FIRST)

        @pl.when(step == 0)
        def _():
            acc_ref[...] = term

        @pl.when(step > 0)
        def _():
            acc_ref[...] += term

        @pl.when(step == steps - 1)
        def _():
            block = term_ref.shape[2]
            for z in range(NZ):
                for y in range(NY):
                    term_ref[y, z] = acc_ref[pl.ds((z * NY + y) * block, block), :].astype(BF16)


def backward(tokens, nm, no, inv_std, grads):
    rows, aw = tokens.shape
    half = nm.shape[1]
    tiles = grads[0].shape[0]
    steps = 2
    grads = [g.reshape(steps, tiles // steps, half) for g in grads]
    gspec = pl.BlockSpec((1, tiles // steps, half), lambda i: (i, 0, 0))
    tspec = pl.BlockSpec((NY, NZ, aw // (NY * NZ), half), lambda i: (0, 0, 0, 0))
    term = jax.ShapeDtypeStruct((NY, NZ, aw // (NY * NZ), half), BF16)
    wide = pl.BlockSpec((rows // steps, half), lambda i: (i, 0))
    mixed = jax.ShapeDtypeStruct((rows, half), BF16)
    return pl.pallas_call(
        backward_kernel,
        out_shape=(mixed, mixed, term, term),
        grid=(steps,),
        in_specs=[
            pl.BlockSpec((rows // steps, aw), lambda i: (i, 0)),
            wide,
            wide,
            pl.BlockSpec((rows // steps, 128), lambda i: (i, 0)),
            gspec,
            gspec,
        ],
        out_specs=(wide, wide, tspec, tspec),
        scratch_shapes=[pltpu.VMEM((aw, half), F32), pltpu.VMEM((aw, half), F32)],
        compiler_params=params(56),
        cost_estimate=cost(2.4, 16),
        name="backward",
    )(tokens, nm, no, inv_std, *grads)


def gather_embed_kernel(at_ref, *refs):
    out_ref = refs[-1]
    cols = out_ref.shape[-1]
    per = NZ // NX
    for k, ref in enumerate(refs[:-1]):
        x = lax.rem(at_ref[3] + NX - k, NX)
        for zz in range(per):
            for y in range(NY):
                for h in range(2):
                    out_ref[x * per + zz, y, h] = ref[y, zz, :, h * cols : (h + 1) * cols]


def gather_embed(at, pieces):
    _, _, rows, cols = pieces[0].shape
    return pl.pallas_call(
        gather_embed_kernel,
        out_shape=jax.ShapeDtypeStruct((NZ, NY, 2, rows, cols // 2), BF16),
        in_specs=[SMEM] + [VMEM] * NX,
        out_specs=VMEM,
        compiler_params=params(32),
        cost_estimate=cost(0.01, 3),
        name="gather_embed",
    )(at, *pieces)


def gather_out_kernel(at_ref, *refs):
    out_ref = refs[-1]
    for k, ref in enumerate(refs[:-1]):
        y = lax.rem(at_ref[1] + NY - k, NY)
        for z in range(ref.shape[0]):
            out_ref[z, y] = ref[z]


def gather_out(at, pieces):
    zs, rows, cols = pieces[0].shape
    return pl.pallas_call(
        gather_out_kernel,
        out_shape=jax.ShapeDtypeStruct((zs, NY, rows, cols), BF16),
        in_specs=[SMEM] + [VMEM] * NY,
        out_specs=VMEM,
        compiler_params=params(32),
        cost_estimate=cost(0.01, 1.2),
        name="gather_out",
    )(at, *pieces)


def place(row, s):
    return s * 512 + ((row // 16) % NZ * NY + row // (16 * NZ)) * 16 + row % 16


def features_kernel(heads, at_ref, seg_ref, dil_ref, q_ref, k_ref):
    s, y, count = at_ref[0], at_ref[1], at_ref[2]
    rows = q_ref.shape[1]

    def fill(ref, pos, valid):
        lane = lax.broadcasted_iota(jnp.int32, pos.shape, 1)
        hits, residues = [], []
        for c in range(seg_ref.shape[0]):
            width = seg_ref[c]
            bits = 6 + sum((width > 64 << b).astype(jnp.int32) for b in range(4))
            ids = lax.shift_right_logical(jnp.full_like(pos, 2 * rows), jnp.full_like(pos, bits))
            ids = ids + lax.shift_right_logical(pos, jnp.full_like(pos, bits))
            hits.append((ids == lane) & valid)
            residues.append(pos & (dil_ref[c] - 1))
        for h in range(heads):
            head = y * heads + h
            any_hit = None
            for c, (hit, residue) in enumerate(zip(hits, residues)):
                hit = hit & (residue == (head & (dil_ref[c] - 1)))
                any_hit = hit if any_hit is None else any_hit | hit
            ref[h] = jnp.where(any_hit, 1.0, 0.0).astype(BF16)

    row = lax.broadcasted_iota(jnp.int32, (rows, 128), 0)
    pos = place(row, s)
    fill(q_ref, pos, pos >= 0)
    row = lax.broadcasted_iota(jnp.int32, (2 * rows, 128), 0)
    pos = place(row // 32 * 16 + row % 16, row // 16 % 2)
    fill(k_ref, pos, pos < count)


def features(at, seg_lengths, dilation, heads, rows):
    return pl.pallas_call(
        functools.partial(features_kernel, heads),
        out_shape=(
            jax.ShapeDtypeStruct((heads, rows, 128), BF16),
            jax.ShapeDtypeStruct((heads, 2 * rows, 128), BF16),
        ),
        in_specs=[SMEM] * 3,
        out_specs=(VMEM, VMEM),
        compiler_params=params(32),
        cost_estimate=cost(0.01, 2),
        name="features",
    )(at, seg_lengths, dilation)


def attend_kernel(heads, at_ref, hm_ref, ho_ref, wm_ref, wo_ref, fq_ref, fk_ref, out_ref, w_ref, q_ref, k_ref, v_ref):
    s = at_ref[0]
    groups, _, tiles, half = hm_ref.shape
    rows = groups * tiles
    seg = w_ref.shape[-1] // 3
    for z in range(NZ):
        w_ref[z, s] = wm_ref[z]
        w_ref[z, 1 - s] = wo_ref[z]
    w_mine = w_ref[pl.ds(s * (NZ // 2), NZ // 2)].reshape(half, 3 * seg)
    w_other = w_ref[pl.ds((1 - s) * (NZ // 2), NZ // 2)].reshape(half, 3 * seg)
    hm = hm_ref[...].reshape(2 * rows, half)
    ho = ho_ref[...].reshape(2 * rows, half)

    def project(at):
        lanes = slice(at * seg, (at + 1) * seg)
        return (dot(hm, w_mine[:, lanes]) + dot(ho, w_other[:, lanes])).astype(BF16)

    q_ref[...] = project(0).reshape(groups, 2, tiles, seg)
    k_ref[...] = project(1)
    v_ref[...] = project(2)
    queries_all = q_ref[:, s].reshape(rows, seg)
    lane_head = lax.broadcasted_iota(jnp.int32, (1, seg), 1) // HS
    scale = HS ** (-0.5) * 1.4426950408889634
    block = 128
    for head in range(heads):
        for start in range(0, rows, block):
            span = pl.ds(start, block)
            queries = jnp.where(lane_head == head, queries_all[start : start + block], 0).astype(BF16)
            scores = dot_general(queries, k_ref[...], CONTRACT_LAST) * scale
            counted = dot_general(fq_ref[head, span, :], fk_ref[head], CONTRACT_LAST)
            masked = jnp.where(counted > 0.0, scores, -1e30)
            top = jnp.max(masked, axis=-1, keepdims=True)
            weights = counted * jnp.exp2(masked - top)
            total = jnp.maximum(jnp.sum(weights, axis=-1, keepdims=True), 0.5)
            probs = (weights * (1.0 / total)).astype(BF16)
            part = dot(probs, v_ref[...]).T
            out_ref[head * HS : (head + 1) * HS, span] = part[head * HS : (head + 1) * HS].astype(BF16)


def attend(at, hm, ho, wm, wo, fq, fk, heads):
    groups, _, tiles, half = hm.shape
    rows = groups * tiles
    seg = wm.shape[-1] // 3
    return pl.pallas_call(
        functools.partial(attend_kernel, heads),
        out_shape=jax.ShapeDtypeStruct((heads * HS, rows), BF16),
        in_specs=[SMEM] + [VMEM] * 6,
        out_specs=VMEM,
        scratch_shapes=[
            pltpu.VMEM((NZ, 2, wm.shape[1], 3 * seg), BF16),
            pltpu.VMEM((groups, 2, tiles, seg), BF16),
            pltpu.VMEM((2 * rows, seg), BF16),
            pltpu.VMEM((2 * rows, seg), BF16),
        ],
        compiler_params=params(48),
        cost_estimate=cost(6, 6, 2),
        name="attend",
    )(at, hm, ho, wm, wo, fq, fk)


def finish_kernel(at_ref, att_ref, wm_ref, wo_ref, hm_ref, ho_ref, out_ref):
    s, count = at_ref[0], at_ref[2]
    groups, _, tiles, half = hm_ref.shape
    rows = groups * tiles
    depth = wm_ref.shape[0]
    mixed = dot_general(att_ref[pl.ds(s * depth, depth), :], wm_ref[...], CONTRACT_FIRST)
    mixed = mixed + dot_general(att_ref[pl.ds((1 - s) * depth, depth), :], wo_ref[...], CONTRACT_FIRST)
    hm = hm_ref[:, s].reshape(rows, half).astype(F32)
    ho = ho_ref[:, s].reshape(rows, half).astype(F32)
    row = lax.broadcasted_iota(jnp.int32, (rows, half), 0)
    valid = place(row, s) < count
    left = jnp.where(valid, mixed[:, :half] + jnp.where(s == 0, hm, ho), 0.0).astype(BF16)
    right = jnp.where(valid, mixed[:, half:] + jnp.where(s == 0, ho, hm), 0.0).astype(BF16)
    span = NZ * tiles
    for y in range(NY):
        for part, lanes in ((left, slice(0, half)), (right, slice(half, 2 * half))):
            out_ref[:, y, :, lanes] = part[y * span : (y + 1) * span].reshape(NZ, tiles, half)


def finish(at, att, wm, wo, hm, ho):
    groups, _, tiles, half = hm.shape
    return pl.pallas_call(
        finish_kernel,
        out_shape=jax.ShapeDtypeStruct((NZ, NY, tiles, 2 * half), BF16),
        in_specs=[SMEM] + [VMEM] * 5,
        out_specs=VMEM,
        compiler_params=params(32),
        cost_estimate=cost(0.6, 4),
        name="finish",
    )(at, att, wm, wo, hm, ho)


def body(
    head_out,
    proj_weight,
    norm_gain,
    embed_cot,
    tile_counts,
    seg_lengths,
    dilation,
    embed_weight,
    qkv_weight,
    out_weight,
):
    tokens = head_out[0]
    n_rows, aw = tokens.shape
    dt = proj_weight.shape[1]
    half = dt // 2
    tiles = embed_cot.shape[1]
    per_tile = n_rows // tiles
    fsdp = NZ * NY
    f = lax.axis_index("fsdp")
    s = lax.axis_index("seq")
    y = f % NY
    count = tile_counts[0]
    ds = out_weight.shape[1]
    shard_len = fsdp * tiles
    x = lax.axis_index("slide")
    at = jnp.stack([s, y, count, x]).astype(jnp.int32)
    dslice = lax.dynamic_slice_in_dim
    heads = ds // HS // NY
    width = heads * HS

    def of_y(v, k):
        return lax.dynamic_index_in_dim(v, (y + k) % NY, 0, keepdims=False)

    feat_q, feat_k = features(at, seg_lengths, dilation, heads, shard_len)

    embed_half = dslice(embed_weight, s * (ds // 2), ds // 2, 1)
    rows = proj_weight.shape[0]
    first = jnp.concatenate(
        [dslice(proj_weight, s * half, half, 1), jnp.concatenate([embed_half[:rows], embed_half[rows:]], axis=1)],
        axis=0,
    )
    first = a2a_z(copies(first, NZ))
    first = jnp.concatenate([first[:, :rows], dslice(first[:, rows:], x * (NZ // NX), NZ // NX, 0)])
    first = a2a_y(copies(after(first, feat_k), NY))
    proj_mine = first[:, :NZ].transpose(1, 0, 2, 3).reshape(aw, half)
    proj_other = swap(proj_mine)
    w_embed = first[:, NZ:]
    w_embed = gather_embed(at, [w_embed] + [shift_x(w_embed, k) for k in range(1, NX)]).reshape(dt, ds // 2)

    w_heads = qkv_weight.reshape(rows, 3, NY, width).transpose(2, 0, 1, 3)
    w_heads = jnp.pad(w_heads, ((0, 0), (0, 0), (0, 0), (0, 256 - width))).reshape(NY, rows, 3 * 256)
    w_heads = [of_y(w_heads, 0)] + [shift_y(of_y(w_heads, k), k) for k in range(1, NY)]
    w_heads = jnp.stack([w_heads[-j % NY] for j in range(NY)])
    w_heads = dslice(jnp.concatenate([w_heads, w_heads]), (NY - y + 2 * s) % NY, 2, 0).reshape(2 * rows, 3 * 256)
    second = jnp.concatenate([w_heads, out_weight])
    second = a2a_z(copies(after(second, first), NZ))
    w_heads = second[:, : 2 * rows]
    w_heads_other = swap(w_heads)
    w_out = dslice(second[:, 2 * rows :], s * (NZ // 2), NZ // 2, 0)
    w_out = gather_out(at, [w_out] + [shift_y(w_out, k) for k in range(1, NY)]).reshape(ds // 2, ds)
    w_out_other = swap(w_out)

    def halves(v):
        return dslice(v, s * half, half, v.ndim - 1), dslice(v, (1 - s) * half, half, v.ndim - 1)

    gain = halves(norm_gain)
    embed, normed_mine, normed_other, inv_std = forward(at, tokens, proj_mine, proj_other, jnp.stack(gain), tiles)
    embed = embed.astype(BF16)
    embed_other = swap(embed)
    embed = jnp.concatenate([jnp.where(s == 0, embed, embed_other), jnp.where(s == 0, embed_other, embed)])
    hidden = dot(embed, w_embed).astype(BF16)
    hidden = a2a_z(copies(after(hidden, second), NZ))
    hidden = a2a_y(copies(hidden, NY)).reshape(fsdp, 2, tiles, ds // 2)
    hidden_other = swap(hidden)

    base = (s * fsdp + f) * tiles
    valid = (base + jnp.arange(tiles, dtype=jnp.int32) < count).astype(F32)
    grads = [c * valid[:, None] / per_tile * g for c, g in zip(halves(embed_cot[0].astype(F32)), gain)]
    mixed_mine, mixed_other, term_mine, term_other = backward(tokens, normed_mine, normed_other, inv_std, grads)
    head_out_grad = dot_general(mixed_mine, proj_mine, CONTRACT_LAST) + dot_general(
        mixed_other, proj_other, CONTRACT_LAST
    )
    head_out_grad = head_out_grad.astype(BF16)

    pair = (term_mine.astype(F32) + swap(term_other).astype(F32)).astype(BF16)
    parts = [of_y(pair, 0)] + [shift_y(of_y(pair, k), k) for k in range(1, NY)]
    share = sum(p.astype(F32) for p in parts).astype(BF16)
    share = jnp.sum(a2a_z(after(share, hidden)).astype(F32), axis=0).astype(BF16)
    share = sum(p.astype(F32) for p in [share] + [shift_x(share, k) for k in range(1, NX)]).astype(BF16)
    other = swap(share)
    proj_grad = jnp.concatenate([jnp.where(s == 0, share, other), jnp.where(s == 0, other, share)], axis=1)

    attended = attend(at, hidden, hidden_other, w_heads, w_heads_other, feat_q, feat_k, heads)
    attended = a2a_y(copies(attended, NY)).reshape(ds, shard_len)
    slide_out = finish(at, attended, w_out, w_out_other, hidden, hidden_other).reshape(1, shard_len, ds)
    return (slide_out, head_out_grad[None], proj_grad)


def solution(mesh):
    return jax.shard_map(
        body,
        mesh=mesh,
        in_specs=(
            P("slide", ("seq", "fsdp"), None),
            P("fsdp", None),
            P(),
            P("slide", ("seq", "fsdp"), None),
            P("slide"),
            P(),
            P(),
            P("fsdp", None),
            P("fsdp", None),
            P("fsdp", None),
        ),
        out_specs=(P("slide", "seq", None), P("slide", ("seq", "fsdp"), None), P("fsdp", None)),
        check_vma=False,
    )
```

```python
import functools

import jax
import jax.numpy as jnp
from jax import lax
from jax.experimental import pallas as pl
from jax.experimental.pallas import tpu as pltpu
from jax.sharding import PartitionSpec as P

HS = 48
NX, NZ, NY = 4, 8, 4
Z_GROUPS = [[z * NY + y for z in range(NZ)] for y in range(NY)]
Y_GROUPS = [[z * NY + y for y in range(NY)] for z in range(NZ)]
SWAP = [(0, 1), (1, 0)]
F32, BF16 = jnp.float32, jnp.bfloat16
VMEM = pl.BlockSpec(memory_space=pltpu.VMEM)
SMEM = pl.BlockSpec(memory_space=pltpu.SMEM)
CONTRACT_LAST = (((1,), (1,)), ((), ()))
CONTRACT_FIRST = (((0,), (0,)), ((), ()))
dot = functools.partial(jnp.dot, preferred_element_type=F32)
dot_general = functools.partial(lax.dot_general, preferred_element_type=F32)


def a2a_z(v):
    return lax.all_to_all(v, "fsdp", 0, 0, axis_index_groups=Z_GROUPS)


def a2a_y(v):
    return lax.all_to_all(v, "fsdp", 0, 0, axis_index_groups=Y_GROUPS)


def copies(v, n):
    return jnp.broadcast_to(v[None], (n,) + v.shape)


def swap(v):
    return lax.ppermute(v, "seq", SWAP)


def shift_y(v, k):
    return lax.ppermute(
        v, "fsdp", [(z * NY + y, z * NY + (y + k) % NY) for z in range(NZ) for y in range(NY)]
    )


def shift_z(v, k):
    return lax.ppermute(
        v, "fsdp", [(z * NY + y, (z + k) % NZ * NY + y) for z in range(NZ) for y in range(NY)]
    )


def shift_x(v, k):
    return lax.ppermute(v, "slide", [(x, (x + k) % NX) for x in range(NX)])


def after(v, other):
    return v + (other[(0,) * other.ndim].astype(F32) * 0).astype(v.dtype)


def params(mib):
    return pltpu.CompilerParams(vmem_limit_bytes=mib * 1024 * 1024)


def cost(gflop, mb, mexp=0):
    return pl.CostEstimate(
        flops=int(gflop * 1e9), bytes_accessed=int(mb * 1e6), transcendentals=int(mexp * 1e6)
    )


def forward_kernel(tiles, at_ref, tok_ref, pm_ref, po_ref, gain_ref, out_ref, nm_ref, no_ref, inv_ref):
    tok = tok_ref[...]
    mixed = [dot(tok, pm_ref[...]), dot(tok, po_ref[...])]
    rows, half = mixed[0].shape
    centre = sum(jnp.sum(m, axis=-1, keepdims=True) for m in mixed) * (0.5 / half)
    shifted = [m - centre for m in mixed]
    var = sum(jnp.sum(m * m, axis=-1, keepdims=True) for m in shifted) * (0.5 / half)
    inv_std = lax.rsqrt(var + 1e-06)
    inv_ref[...] = jnp.broadcast_to(inv_std, inv_ref.shape)
    pooled = []
    for i, (m, n_ref) in enumerate(zip(shifted, (nm_ref, no_ref))):
        n = m * inv_std
        n_ref[...] = n
        mean = jnp.sum(n.reshape(tiles, rows // tiles, half), axis=1) * (tiles / rows)
        pooled.append(mean * gain_ref[i : i + 1, :])
    span = pl.ds(pl.multiple_of(pl.program_id(0) * tiles, tiles), tiles)
    for s in range(2):

        @pl.when(at_ref[0] == s)
        def _():
            out_ref[span, :half] = pooled[s]
            out_ref[span, half:] = pooled[1 - s]


def forward(at, tokens, pm, po, gain, tiles):
    rows, aw = tokens.shape
    half = pm.shape[1]
    steps = 2
    spec = pl.BlockSpec((rows // steps, half), lambda i: (i, 0))
    return pl.pallas_call(
        functools.partial(forward_kernel, tiles // steps),
        out_shape=(
            jax.ShapeDtypeStruct((tiles, 2 * half), F32),
            jax.ShapeDtypeStruct((rows, half), F32),
            jax.ShapeDtypeStruct((rows, half), F32),
            jax.ShapeDtypeStruct((rows, 128), F32),
        ),
        grid=(steps,),
        in_specs=[SMEM, pl.BlockSpec((rows // steps, aw), lambda i: (i, 0)), VMEM, VMEM, VMEM],
        out_specs=(
            pl.BlockSpec((tiles, 2 * half), lambda i: (0, 0)),
            spec,
            spec,
            pl.BlockSpec((rows // steps, 128), lambda i: (i, 0)),
        ),
        compiler_params=params(48),
        cost_estimate=cost(2.4, 10),
        name="forward",
    )(at, tokens, pm, po, gain)


def backward_kernel(tok_ref, nm_ref, no_ref, inv_ref, gm_ref, go_ref, xm_ref, xo_ref, tm_ref, to_ref, am_ref, ao_ref):
    step, steps = pl.program_id(0), pl.num_programs(0)
    tok = tok_ref[...]
    normed = [nm_ref[...], no_ref[...]]
    inv_std = inv_ref[:, :1]
    rows, half = normed[0].shape
    tiles = gm_ref.shape[1]
    grads = [gm_ref[0], go_ref[0]]
    mean = sum(jnp.sum(g, axis=-1, keepdims=True) for g in grads) * (0.5 / half)

    def per_token(v):
        return jnp.broadcast_to(v[:, None, :], (tiles, rows // tiles, v.shape[1])).reshape(rows, v.shape[1])

    along = sum(jnp.sum(per_token(g) * n, axis=-1, keepdims=True) for g, n in zip(grads, normed)) * (0.5 / half)
    mixed = [(inv_std * (per_token(g - mean) - n * along)).astype(BF16) for g, n in zip(grads, normed)]
    xm_ref[...] = mixed[0]
    xo_ref[...] = mixed[1]
    for acc_ref, term_ref, m in ((am_ref, tm_ref, mixed[0]), (ao_ref, to_ref, mixed[1])):
        term = dot_general(tok, m, CONTRACT_FIRST)

        @pl.when(step == 0)
        def _():
            acc_ref[...] = term

        @pl.when(step > 0)
        def _():
            acc_ref[...] += term

        @pl.when(step == steps - 1)
        def _():
            block = term_ref.shape[2]
            for z in range(NZ):
                for y in range(NY):
                    term_ref[y, z] = acc_ref[pl.ds((z * NY + y) * block, block), :].astype(BF16)


def backward(tokens, nm, no, inv_std, grads):
    rows, aw = tokens.shape
    half = nm.shape[1]
    tiles = grads[0].shape[0]
    steps = 2
    grads = [g.reshape(steps, tiles // steps, half) for g in grads]
    gspec = pl.BlockSpec((1, tiles // steps, half), lambda i: (i, 0, 0))
    tspec = pl.BlockSpec((NY, NZ, aw // (NY * NZ), half), lambda i: (0, 0, 0, 0))
    term = jax.ShapeDtypeStruct((NY, NZ, aw // (NY * NZ), half), BF16)
    wide = pl.BlockSpec((rows // steps, half), lambda i: (i, 0))
    mixed = jax.ShapeDtypeStruct((rows, half), BF16)
    return pl.pallas_call(
        backward_kernel,
        out_shape=(mixed, mixed, term, term),
        grid=(steps,),
        in_specs=[
            pl.BlockSpec((rows // steps, aw), lambda i: (i, 0)),
            wide,
            wide,
            pl.BlockSpec((rows // steps, 128), lambda i: (i, 0)),
            gspec,
            gspec,
        ],
        out_specs=(wide, wide, tspec, tspec),
        scratch_shapes=[pltpu.VMEM((aw, half), F32), pltpu.VMEM((aw, half), F32)],
        compiler_params=params(56),
        cost_estimate=cost(2.4, 16),
        name="backward",
    )(tokens, nm, no, inv_std, *grads)


def head_out_grad_kernel(at_ref, xm_ref, xo_ref, pm_ref, po_ref, out_ref):
    grad = dot_general(xm_ref[...], pm_ref[...], CONTRACT_LAST) + dot_general(xo_ref[...], po_ref[...], CONTRACT_LAST)
    out_ref[...] = grad.astype(BF16)


def head_out_grad_of(at, xm, xo, pm, po):
    rows, half = xm.shape
    aw = pm.shape[0]
    steps = 2
    spec = pl.BlockSpec((rows // steps, half), lambda i: (i, 0))
    return pl.pallas_call(
        head_out_grad_kernel,
        out_shape=jax.ShapeDtypeStruct((rows, aw), BF16),
        grid=(steps,),
        in_specs=[SMEM, spec, spec, VMEM, VMEM],
        out_specs=pl.BlockSpec((rows // steps, aw), lambda i: (i, 0)),
        compiler_params=params(32),
        cost_estimate=cost(2.4, 7),
        name="head_out_grad",
    )(at, xm, xo, pm, po)


def by_z_kernel(cuts, at_ref, *refs):
    for k, ref in enumerate(refs[:NZ]):
        z = lax.rem(at_ref[4] + NZ - k, NZ)
        for (start, stop), out_ref in zip(cuts, refs[NZ:]):
            out_ref[z] = ref[start:stop, :]


def by_z(at, pieces, *sizes):
    cols = pieces[0].shape[1]
    stops = [sum(sizes[: i + 1]) for i in range(len(sizes))]
    cuts = [(stop - size, stop) for stop, size in zip(stops, sizes)]
    return pl.pallas_call(
        functools.partial(by_z_kernel, cuts),
        out_shape=[jax.ShapeDtypeStruct((NZ, size, cols), BF16) for size in sizes],
        in_specs=[SMEM] + [VMEM] * NZ,
        out_specs=[VMEM] * len(sizes),
        compiler_params=params(32),
        cost_estimate=cost(0.01, 1),
        name="by_z",
    )(at, *pieces)


def gather_embed_kernel(at_ref, *refs):
    out_ref = refs[-1]
    cols = out_ref.shape[-1]
    for k, ref in enumerate(refs[:-1]):
        y = lax.rem(at_ref[1] + NY - k, NY)
        for z in range(NZ):
            for h in range(2):
                out_ref[z, y, h] = ref[z, :, h * cols : (h + 1) * cols]


def gather_embed(at, pieces):
    _, rows, cols = pieces[0].shape
    return pl.pallas_call(
        gather_embed_kernel,
        out_shape=jax.ShapeDtypeStruct((NZ, NY, 2, rows, cols // 2), BF16),
        in_specs=[SMEM] + [VMEM] * NY,
        out_specs=VMEM,
        compiler_params=params(32),
        cost_estimate=cost(0.01, 3),
        name="gather_embed",
    )(at, *pieces)


def gather_out_kernel(at_ref, *refs):
    out_ref = refs[-1]
    for k, ref in enumerate(refs[:-1]):
        y = lax.rem(at_ref[1] + NY - k, NY)
        for z in range(ref.shape[0]):
            out_ref[z, y] = ref[z]


def gather_out(at, pieces):
    zs, rows, cols = pieces[0].shape
    return pl.pallas_call(
        gather_out_kernel,
        out_shape=jax.ShapeDtypeStruct((zs, NY, rows, cols), BF16),
        in_specs=[SMEM] + [VMEM] * NY,
        out_specs=VMEM,
        compiler_params=params(32),
        cost_estimate=cost(0.01, 1.2),
        name="gather_out",
    )(at, *pieces)


def place(row, s):
    return s * 512 + ((row // 16) % NZ * NY + row // (16 * NZ)) * 16 + row % 16


def bias_kernel(heads, at_ref, seg_ref, dil_ref, out_ref, q_ref, k_ref):
    s, y, count = at_ref[0], at_ref[1], at_ref[2]
    rows = q_ref.shape[1]

    def fill(ref, pos, valid):
        lane = lax.broadcasted_iota(jnp.int32, pos.shape, 1)
        hits, residues = [], []
        for c in range(seg_ref.shape[0]):
            width = seg_ref[c]
            bits = 6 + sum((width > 64 << b).astype(jnp.int32) for b in range(4))
            ids = lax.shift_right_logical(jnp.full_like(pos, 2 * rows), jnp.full_like(pos, bits))
            ids = ids + lax.shift_right_logical(pos, jnp.full_like(pos, bits))
            hits.append((ids == lane) & valid)
            residues.append(pos & (dil_ref[c] - 1))
        for h in range(heads):
            head = y * heads + h
            any_hit = None
            for c, (hit, residue) in enumerate(zip(hits, residues)):
                hit = hit & (residue == (head & (dil_ref[c] - 1)))
                any_hit = hit if any_hit is None else any_hit | hit
            ref[h] = jnp.where(any_hit, 1.0, 0.0).astype(BF16)

    row = lax.broadcasted_iota(jnp.int32, (rows, 128), 0)
    pos = place(row, s)
    fill(q_ref, pos, pos >= 0)
    row = lax.broadcasted_iota(jnp.int32, (2 * rows, 128), 0)
    pos = place(row // 32 * 16 + row % 16, row // 16 % 2)
    fill(k_ref, pos, pos < count)
    block = 128
    for h in range(heads):
        for start in range(0, rows, block):
            span = pl.ds(start, block)
            counted = dot_general(q_ref[h, span, :], k_ref[h], CONTRACT_LAST)
            bias = jnp.full(counted.shape, -1e30, F32)
            for n, log2 in enumerate((0.0, 1.0, 1.584962500721156, 2.0, 2.321928094887362)):
                bias = jnp.where(counted > n + 0.5, log2, bias)
            out_ref[h, span, :] = bias


def biases(at, seg_lengths, dilation, heads, rows):
    return pl.pallas_call(
        functools.partial(bias_kernel, heads),
        out_shape=jax.ShapeDtypeStruct((heads, rows, 2 * rows), F32),
        in_specs=[SMEM] * 3,
        out_specs=VMEM,
        scratch_shapes=[pltpu.VMEM((heads, rows, 128), BF16), pltpu.VMEM((heads, 2 * rows, 128), BF16)],
        compiler_params=params(40),
        cost_estimate=cost(4, 8),
        name="biases",
    )(at, seg_lengths, dilation)


def attend_kernel(heads, at_ref, hm_ref, ho_ref, wm_ref, wo_ref, bias_ref, out_ref, w_ref, q_ref, k_ref, v_ref):
    s = at_ref[0]
    groups, _, tiles, half = hm_ref.shape
    rows = groups * tiles
    seg = w_ref.shape[-1] // 3
    for z in range(NZ):
        w_ref[z, s] = wm_ref[z]
        w_ref[z, 1 - s] = wo_ref[z]
    w_mine = w_ref[pl.ds(s * (NZ // 2), NZ // 2)].reshape(half, 3 * seg)
    w_other = w_ref[pl.ds((1 - s) * (NZ // 2), NZ // 2)].reshape(half, 3 * seg)
    hm = hm_ref[...].reshape(2 * rows, half)
    ho = ho_ref[...].reshape(2 * rows, half)

    def project(at):
        lanes = slice(at * seg, (at + 1) * seg)
        return (dot(hm, w_mine[:, lanes]) + dot(ho, w_other[:, lanes])).astype(BF16)

    q_ref[...] = project(0).reshape(groups, 2, tiles, seg)
    k_ref[...] = project(1)
    v_ref[...] = project(2)
    queries_all = q_ref[:, s].reshape(rows, seg)
    lane_head = lax.broadcasted_iota(jnp.int32, (1, seg), 1) // HS
    scale = HS ** (-0.5) * 1.4426950408889634
    block = 128
    for start in range(0, rows, block):
        span = pl.ds(start, block)
        queries = queries_all[start : start + block]
        queries = jnp.concatenate([jnp.where(lane_head == h, queries, 0).astype(BF16) for h in range(heads)])
        scores = dot_general(queries, k_ref[...], CONTRACT_LAST)
        scores = scores * scale + bias_ref[:, span, :].reshape(heads * block, 2 * rows)
        weights = jnp.exp2(scores - jnp.max(scores, axis=-1, keepdims=True))
        total = jnp.sum(weights, axis=-1, keepdims=True)
        part = dot(weights.astype(BF16), v_ref[...]) * (1.0 / total)
        for h in range(heads):
            turned = part[h * block : (h + 1) * block].T
            out_ref[h * HS : (h + 1) * HS, span] = turned[h * HS : (h + 1) * HS].astype(BF16)


def attend(at, hm, ho, wm, wo, bias):
    heads = bias.shape[0]
    groups, _, tiles, half = hm.shape
    rows = groups * tiles
    seg = wm.shape[-1] // 3
    return pl.pallas_call(
        functools.partial(attend_kernel, heads),
        out_shape=jax.ShapeDtypeStruct((heads * HS, rows), BF16),
        in_specs=[SMEM] + [VMEM] * 5,
        out_specs=VMEM,
        scratch_shapes=[
            pltpu.VMEM((NZ, 2, wm.shape[1], 3 * seg), BF16),
            pltpu.VMEM((groups, 2, tiles, seg), BF16),
            pltpu.VMEM((2 * rows, seg), BF16),
            pltpu.VMEM((2 * rows, seg), BF16),
        ],
        compiler_params=params(48),
        cost_estimate=cost(6, 6, 2),
        name="attend",
    )(at, hm, ho, wm, wo, bias)


def finish_kernel(at_ref, a0_ref, a1_ref, a2_ref, a3_ref, wm_ref, wo_ref, hm_ref, ho_ref, out_ref, w_ref):
    s, y, count = at_ref[0], at_ref[1], at_ref[2]
    groups, _, tiles, half = hm_ref.shape
    rows = groups * tiles
    w_ref[s] = wm_ref[...]
    w_ref[1 - s] = wo_ref[...]
    mixed = 0.0
    for k, att_ref in enumerate((a0_ref, a1_ref, a2_ref, a3_ref)):
        depth = att_ref.shape[0]
        owner = lax.rem(y + NY - k, NY)
        w = w_ref[owner // 2, pl.ds(pl.multiple_of(owner % 2 * depth, depth), depth), :]
        mixed = mixed + dot_general(att_ref[...], w, CONTRACT_FIRST)
    hm = hm_ref[:, s].reshape(rows, half).astype(F32)
    ho = ho_ref[:, s].reshape(rows, half).astype(F32)
    row = lax.broadcasted_iota(jnp.int32, (rows, half), 0)
    valid = place(row, s) < count
    left = jnp.where(valid, mixed[:, :half] + jnp.where(s == 0, hm, ho), 0.0).astype(BF16)
    right = jnp.where(valid, mixed[:, half:] + jnp.where(s == 0, ho, hm), 0.0).astype(BF16)
    span = NZ * tiles
    for y in range(NY):
        for part, lanes in ((left, slice(0, half)), (right, slice(half, 2 * half))):
            out_ref[:, y, :, lanes] = part[y * span : (y + 1) * span].reshape(NZ, tiles, half)


def finish(at, att, wm, wo, hm, ho):
    groups, _, tiles, half = hm.shape
    return pl.pallas_call(
        finish_kernel,
        out_shape=jax.ShapeDtypeStruct((NZ, NY, tiles, 2 * half), BF16),
        in_specs=[SMEM] + [VMEM] * 8,
        out_specs=VMEM,
        scratch_shapes=[pltpu.VMEM((2,) + wm.shape, BF16)],
        compiler_params=params(32),
        cost_estimate=cost(0.6, 4),
        name="finish",
    )(at, *att, wm, wo, hm, ho)


def body(
    head_out,
    proj_weight,
    norm_gain,
    embed_cot,
    tile_counts,
    seg_lengths,
    dilation,
    embed_weight,
    qkv_weight,
    out_weight,
):
    tokens = head_out[0]
    n_rows, aw = tokens.shape
    dt = proj_weight.shape[1]
    half = dt // 2
    tiles = embed_cot.shape[1]
    per_tile = n_rows // tiles
    fsdp = NZ * NY
    f = lax.axis_index("fsdp")
    s = lax.axis_index("seq")
    y = f % NY
    count = tile_counts[0]
    ds = out_weight.shape[1]
    shard_len = fsdp * tiles
    x = lax.axis_index("slide")
    at = jnp.stack([s, y, count, x, f // NY]).astype(jnp.int32)
    dslice = lax.dynamic_slice_in_dim
    heads = ds // HS // NY
    width = heads * HS

    def of_y(v, k):
        return lax.dynamic_index_in_dim(v, (y + k) % NY, 0, keepdims=False)

    bias = biases(at, seg_lengths, dilation, heads, shard_len)

    rows = proj_weight.shape[0]
    first = a2a_z(copies(dslice(proj_weight, s * half, half, 1), NZ))
    proj_mine = a2a_y(copies(after(first, bias), NY))
    proj_mine = proj_mine.transpose(1, 0, 2, 3).reshape(aw, half)
    proj_other = swap(proj_mine)

    w_embed = dslice(embed_weight, s * (ds // 2), ds // 2, 1)
    w_embed = after(jnp.concatenate([w_embed[:rows], w_embed[rows:]], axis=1), first)
    (w_embed,) = by_z(at, [w_embed] + [shift_z(w_embed, k) for k in range(1, NZ)], rows)
    w_embed = [w_embed] + [shift_y(w_embed, k) for k in range(1, NY)]
    w_embed = gather_embed(at, w_embed).reshape(dt, ds // 2)

    w_heads = qkv_weight.reshape(rows, 3, NY, width).transpose(2, 0, 1, 3)
    w_heads = jnp.pad(w_heads, ((0, 0), (0, 0), (0, 0), (0, 256 - width))).reshape(NY, rows, 3 * 256)
    w_heads = [of_y(w_heads, 0)] + [shift_y(of_y(w_heads, k), k) for k in range(1, NY)]
    w_heads = jnp.stack([w_heads[-j % NY] for j in range(NY)])
    w_heads = dslice(jnp.concatenate([w_heads, w_heads]), (NY - y + 2 * s) % NY, 2, 0).reshape(2 * rows, 3 * 256)
    second = after(jnp.concatenate([w_heads, out_weight]), first)
    w_heads, w_out = by_z(at, [second] + [shift_z(second, k) for k in range(1, NZ)], 2 * rows, rows)
    w_heads_other = swap(w_heads)
    w_out = dslice(w_out, s * (NZ // 2), NZ // 2, 0)
    w_out = gather_out(at, [w_out] + [shift_y(w_out, k) for k in range(1, NY)]).reshape(ds // 2, ds)
    w_out_other = swap(w_out)

    def halves(v):
        return dslice(v, s * half, half, v.ndim - 1), dslice(v, (1 - s) * half, half, v.ndim - 1)

    gain = halves(norm_gain)
    embed, normed_mine, normed_other, inv_std = forward(at, tokens, proj_mine, proj_other, jnp.stack(gain), tiles)
    embed = embed.astype(BF16)
    embed_other = swap(embed)
    embed = jnp.concatenate([jnp.where(s == 0, embed, embed_other), jnp.where(s == 0, embed_other, embed)])
    hidden = dot(embed, w_embed).astype(BF16)
    local_hidden = hidden
    over_z = a2a_z(copies(hidden, NZ))
    hidden = a2a_y(copies(after(over_z, w_heads_other), NY)).reshape(fsdp, 2, tiles, ds // 2)
    hidden_other = swap(hidden)

    base = (s * fsdp + f) * tiles
    valid = (base + jnp.arange(tiles, dtype=jnp.int32) < count).astype(F32)
    valid = after(valid, local_hidden)
    grads = [c * valid[:, None] / per_tile * g for c, g in zip(halves(embed_cot[0].astype(F32)), gain)]
    mixed_mine, mixed_other, term_mine, term_other = backward(tokens, normed_mine, normed_other, inv_std, grads)
    head_out_grad = head_out_grad_of(after(at, over_z), mixed_mine, mixed_other, proj_mine, proj_other)

    pair = (term_mine.astype(F32) + swap(term_other).astype(F32)).astype(BF16)
    parts = [of_y(pair, 0)] + [shift_y(of_y(pair, k), k) for k in range(1, NY)]

    attended = attend(at, hidden, hidden_other, w_heads, w_heads_other, bias)
    received = [attended] + [shift_y(attended, k) for k in range(1, NY)]
    slide_out = finish(at, received, w_out, w_out_other, hidden, hidden_other).reshape(1, shard_len, ds)

    parts[0] = after(parts[0], attended)
    share = sum(p.astype(F32) for p in parts).astype(BF16)
    share = jnp.sum(a2a_z(share).astype(F32), axis=0).astype(BF16)
    share = sum(p.astype(F32) for p in [share] + [shift_x(share, k) for k in range(1, NX)]).astype(BF16)
    other = swap(share)
    proj_grad = jnp.concatenate([jnp.where(s == 0, share, other), jnp.where(s == 0, other, share)], axis=1)
    return (slide_out, head_out_grad[None], proj_grad)


def solution(mesh):
    return jax.shard_map(
        body,
        mesh=mesh,
        in_specs=(
            P("slide", ("seq", "fsdp"), None),
            P("fsdp", None),
            P(),
            P("slide", ("seq", "fsdp"), None),
            P("slide"),
            P(),
            P(),
            P("fsdp", None),
            P("fsdp", None),
            P("fsdp", None),
        ),
        out_specs=(P("slide", "seq", None), P("slide", ("seq", "fsdp"), None), P("fsdp", None)),
        check_vma=False,
    )
```

```python
import functools

import jax
import jax.numpy as jnp
from jax import lax
from jax.experimental import pallas as pl
from jax.experimental.pallas import tpu as pltpu
from jax.sharding import PartitionSpec as P

HS = 48
NX, NZ, NY = 4, 8, 4
Z_GROUPS = [[z * NY + y for z in range(NZ)] for y in range(NY)]
Y_GROUPS = [[z * NY + y for y in range(NY)] for z in range(NZ)]
SWAP = [(0, 1), (1, 0)]
F32, BF16 = jnp.float32, jnp.bfloat16
VMEM = pl.BlockSpec(memory_space=pltpu.VMEM)
SMEM = pl.BlockSpec(memory_space=pltpu.SMEM)
CONTRACT_LAST = (((1,), (1,)), ((), ()))
CONTRACT_FIRST = (((0,), (0,)), ((), ()))
dot = functools.partial(jnp.dot, preferred_element_type=F32)
dot_general = functools.partial(lax.dot_general, preferred_element_type=F32)


def a2a_z(v):
    return lax.all_to_all(v, "fsdp", 0, 0, axis_index_groups=Z_GROUPS)


def a2a_y(v):
    return lax.all_to_all(v, "fsdp", 0, 0, axis_index_groups=Y_GROUPS)


def copies(v, n):
    return jnp.broadcast_to(v[None], (n,) + v.shape)


def swap(v):
    return lax.ppermute(v, "seq", SWAP)


def shift_y(v, k):
    return lax.ppermute(
        v, "fsdp", [(z * NY + y, z * NY + (y + k) % NY) for z in range(NZ) for y in range(NY)]
    )


def shift_x(v, k):
    return lax.ppermute(v, "slide", [(x, (x + k) % NX) for x in range(NX)])


def after(v, other):
    return v + (other[(0,) * other.ndim].astype(F32) * 0).astype(v.dtype)


def params(mib):
    return pltpu.CompilerParams(vmem_limit_bytes=mib * 1024 * 1024)


def cost(gflop, mb, mexp=0):
    return pl.CostEstimate(
        flops=int(gflop * 1e9), bytes_accessed=int(mb * 1e6), transcendentals=int(mexp * 1e6)
    )


def forward_kernel(tiles, at_ref, tok_ref, pm_ref, po_ref, gain_ref, out_ref, nm_ref, no_ref, inv_ref):
    tok = tok_ref[...]
    mixed = [dot(tok, pm_ref[...]), dot(tok, po_ref[...])]
    rows, half = mixed[0].shape
    centre = sum(jnp.sum(m, axis=-1, keepdims=True) for m in mixed) * (0.5 / half)
    shifted = [m - centre for m in mixed]
    var = sum(jnp.sum(m * m, axis=-1, keepdims=True) for m in shifted) * (0.5 / half)
    inv_std = lax.rsqrt(var + 1e-06)
    inv_ref[...] = jnp.broadcast_to(inv_std, inv_ref.shape)
    pooled = []
    for i, (m, n_ref) in enumerate(zip(shifted, (nm_ref, no_ref))):
        n = m * inv_std
        n_ref[...] = n
        mean = jnp.sum(n.reshape(tiles, rows // tiles, half), axis=1) * (tiles / rows)
        pooled.append(mean * gain_ref[i : i + 1, :])
    span = pl.ds(pl.multiple_of(pl.program_id(0) * tiles, tiles), tiles)
    for s in range(2):

        @pl.when(at_ref[0] == s)
        def _():
            out_ref[span, :half] = pooled[s]
            out_ref[span, half:] = pooled[1 - s]


def forward(at, tokens, pm, po, gain, tiles):
    rows, aw = tokens.shape
    half = pm.shape[1]
    steps = 2
    spec = pl.BlockSpec((rows // steps, half), lambda i: (i, 0))
    return pl.pallas_call(
        functools.partial(forward_kernel, tiles // steps),
        out_shape=(
            jax.ShapeDtypeStruct((tiles, 2 * half), F32),
            jax.ShapeDtypeStruct((rows, half), F32),
            jax.ShapeDtypeStruct((rows, half), F32),
            jax.ShapeDtypeStruct((rows, 128), F32),
        ),
        grid=(steps,),
        in_specs=[SMEM, pl.BlockSpec((rows // steps, aw), lambda i: (i, 0)), VMEM, VMEM, VMEM],
        out_specs=(
            pl.BlockSpec((tiles, 2 * half), lambda i: (0, 0)),
            spec,
            spec,
            pl.BlockSpec((rows // steps, 128), lambda i: (i, 0)),
        ),
        compiler_params=params(48),
        cost_estimate=cost(2.4, 10),
        name="forward",
    )(at, tokens, pm, po, gain)


def backward_kernel(tok_ref, nm_ref, no_ref, inv_ref, gm_ref, go_ref, xm_ref, xo_ref, tm_ref, to_ref, am_ref, ao_ref):
    step, steps = pl.program_id(0), pl.num_programs(0)
    tok = tok_ref[...]
    normed = [nm_ref[...], no_ref[...]]
    inv_std = inv_ref[:, :1]
    rows, half = normed[0].shape
    tiles = gm_ref.shape[1]
    grads = [gm_ref[0], go_ref[0]]
    mean = sum(jnp.sum(g, axis=-1, keepdims=True) for g in grads) * (0.5 / half)

    def per_token(v):
        return jnp.broadcast_to(v[:, None, :], (tiles, rows // tiles, v.shape[1])).reshape(rows, v.shape[1])

    along = sum(jnp.sum(per_token(g) * n, axis=-1, keepdims=True) for g, n in zip(grads, normed)) * (0.5 / half)
    mixed = [(inv_std * (per_token(g - mean) - n * along)).astype(BF16) for g, n in zip(grads, normed)]
    xm_ref[...] = mixed[0]
    xo_ref[...] = mixed[1]
    for acc_ref, term_ref, m in ((am_ref, tm_ref, mixed[0]), (ao_ref, to_ref, mixed[1])):
        term = dot_general(tok, m, CONTRACT_FIRST)

        @pl.when(step == 0)
        def _():
            acc_ref[...] = term

        @pl.when(step > 0)
        def _():
            acc_ref[...] += term

        @pl.when(step == steps - 1)
        def _():
            block = term_ref.shape[2]
            for z in range(NZ):
                for y in range(NY):
                    term_ref[y, z] = acc_ref[pl.ds((z * NY + y) * block, block), :].astype(BF16)


def backward(tokens, nm, no, inv_std, grads):
    rows, aw = tokens.shape
    half = nm.shape[1]
    tiles = grads[0].shape[0]
    steps = 2
    grads = [g.reshape(steps, tiles // steps, half) for g in grads]
    gspec = pl.BlockSpec((1, tiles // steps, half), lambda i: (i, 0, 0))
    tspec = pl.BlockSpec((NY, NZ, aw // (NY * NZ), half), lambda i: (0, 0, 0, 0))
    term = jax.ShapeDtypeStruct((NY, NZ, aw // (NY * NZ), half), BF16)
    wide = pl.BlockSpec((rows // steps, half), lambda i: (i, 0))
    mixed = jax.ShapeDtypeStruct((rows, half), BF16)
    return pl.pallas_call(
        backward_kernel,
        out_shape=(mixed, mixed, term, term),
        grid=(steps,),
        in_specs=[
            pl.BlockSpec((rows // steps, aw), lambda i: (i, 0)),
            wide,
            wide,
            pl.BlockSpec((rows // steps, 128), lambda i: (i, 0)),
            gspec,
            gspec,
        ],
        out_specs=(wide, wide, tspec, tspec),
        scratch_shapes=[pltpu.VMEM((aw, half), F32), pltpu.VMEM((aw, half), F32)],
        compiler_params=params(56),
        cost_estimate=cost(2.4, 16),
        name="backward",
    )(tokens, nm, no, inv_std, *grads)


def head_out_grad_kernel(at_ref, xm_ref, xo_ref, pm_ref, po_ref, out_ref):
    grad = dot_general(xm_ref[...], pm_ref[...], CONTRACT_LAST) + dot_general(xo_ref[...], po_ref[...], CONTRACT_LAST)
    out_ref[...] = grad.astype(BF16)


def head_out_grad_of(at, xm, xo, pm, po):
    rows, half = xm.shape
    aw = pm.shape[0]
    steps = 2
    spec = pl.BlockSpec((rows // steps, half), lambda i: (i, 0))
    return pl.pallas_call(
        head_out_grad_kernel,
        out_shape=jax.ShapeDtypeStruct((rows, aw), BF16),
        grid=(steps,),
        in_specs=[SMEM, spec, spec, VMEM, VMEM],
        out_specs=pl.BlockSpec((rows // steps, aw), lambda i: (i, 0)),
        compiler_params=params(32),
        cost_estimate=cost(2.4, 7),
        name="head_out_grad",
    )(at, xm, xo, pm, po)


def by_y_kernel(at_ref, *refs):
    out_ref = refs[-1]
    for k, ref in enumerate(refs[:-1]):
        y = lax.rem(at_ref[1] + NY - k, NY)
        for z in range(NZ):
            out_ref[z, y] = ref[z]


def by_y(at, pieces):
    zs, rows, cols = pieces[0].shape
    return pl.pallas_call(
        by_y_kernel,
        out_shape=jax.ShapeDtypeStruct((zs, NY, rows, cols), BF16),
        in_specs=[SMEM] + [VMEM] * NY,
        out_specs=VMEM,
        compiler_params=params(32),
        cost_estimate=cost(0.01, 3),
        name="by_y",
    )(at, *pieces)


def place(row, s):
    return s * 512 + ((row // 16) % NZ * NY + row // (16 * NZ)) * 16 + row % 16


def bias_kernel(heads, at_ref, seg_ref, dil_ref, out_ref, q_ref, k_ref):
    s, y, count = at_ref[0], at_ref[1], at_ref[2]
    rows = q_ref.shape[1]

    def fill(ref, pos, valid):
        lane = lax.broadcasted_iota(jnp.int32, pos.shape, 1)
        hits, residues = [], []
        for c in range(seg_ref.shape[0]):
            width = seg_ref[c]
            bits = 6 + sum((width > 64 << b).astype(jnp.int32) for b in range(4))
            ids = lax.shift_right_logical(jnp.full_like(pos, 2 * rows), jnp.full_like(pos, bits))
            ids = ids + lax.shift_right_logical(pos, jnp.full_like(pos, bits))
            hits.append((ids == lane) & valid)
            residues.append(pos & (dil_ref[c] - 1))
        for h in range(heads):
            head = y * heads + h
            any_hit = None
            for c, (hit, residue) in enumerate(zip(hits, residues)):
                hit = hit & (residue == (head & (dil_ref[c] - 1)))
                any_hit = hit if any_hit is None else any_hit | hit
            ref[h] = jnp.where(any_hit, 1.0, 0.0).astype(BF16)

    row = lax.broadcasted_iota(jnp.int32, (rows, 128), 0)
    pos = place(row, s)
    fill(q_ref, pos, pos >= 0)
    row = lax.broadcasted_iota(jnp.int32, (2 * rows, 128), 0)
    pos = place(row // 32 * 16 + row % 16, row // 16 % 2)
    fill(k_ref, pos, pos < count)
    block = 128
    for h in range(heads):
        for start in range(0, rows, block):
            span = pl.ds(start, block)
            counted = dot_general(q_ref[h, span, :], k_ref[h], CONTRACT_LAST)
            bias = jnp.full(counted.shape, -1e30, F32)
            for n, log2 in enumerate((0.0, 1.0, 1.584962500721156, 2.0, 2.321928094887362)):
                bias = jnp.where(counted > n + 0.5, log2, bias)
            out_ref[h, span, :] = bias


def biases(at, seg_lengths, dilation, heads, rows):
    return pl.pallas_call(
        functools.partial(bias_kernel, heads),
        out_shape=jax.ShapeDtypeStruct((heads, rows, 2 * rows), F32),
        in_specs=[SMEM] * 3,
        out_specs=VMEM,
        scratch_shapes=[pltpu.VMEM((heads, rows, 128), BF16), pltpu.VMEM((heads, 2 * rows, 128), BF16)],
        compiler_params=params(40),
        cost_estimate=cost(4, 8),
        name="biases",
    )(at, seg_lengths, dilation)


def attend_kernel(pair, at_ref, hm_ref, ho_ref, w_ref, bias_ref, out_ref, q_ref, k_ref, v_ref):
    s = at_ref[0]
    groups, _, tiles, half = hm_ref.shape
    rows = groups * tiles
    heads = bias_ref.shape[0] // 2
    seg = w_ref.shape[1] // 6
    w_mine = pl.ds(pl.multiple_of(s * half, half), half)
    w_other = pl.ds(pl.multiple_of((1 - s) * half, half), half)
    hm = hm_ref[...].reshape(2 * rows, half)
    ho = ho_ref[...].reshape(2 * rows, half)

    def project(part):
        lanes = slice((3 * pair + part) * seg, (3 * pair + part + 1) * seg)
        return (dot(hm, w_ref[w_mine, lanes]) + dot(ho, w_ref[w_other, lanes])).astype(BF16)

    q_ref[...] = project(0).reshape(groups, 2, tiles, seg)
    k_ref[...] = project(1)
    v_ref[...] = project(2)
    queries_all = q_ref[:, s].reshape(rows, seg)
    lane_head = lax.broadcasted_iota(jnp.int32, (1, seg), 1) // HS
    scale = HS ** (-0.5) * 1.4426950408889634
    block = 256
    for start in range(0, rows, block):
        span = pl.ds(start, block)
        queries = queries_all[start : start + block]
        queries = jnp.concatenate([jnp.where(lane_head == h, queries, 0).astype(BF16) for h in range(heads)])
        scores = dot_general(queries, k_ref[...], CONTRACT_LAST)
        bias = bias_ref[pair * heads : (pair + 1) * heads, span, :]
        scores = scores * scale + bias.reshape(heads * block, 2 * rows)
        weights = jnp.exp2(scores - jnp.max(scores, axis=-1, keepdims=True))
        total = jnp.sum(weights, axis=-1, keepdims=True)
        part = dot(weights.astype(BF16), v_ref[...]) * (1.0 / total)
        for h in range(heads):
            turned = part[h * block : (h + 1) * block].T
            out_ref[h * HS : (h + 1) * HS, span] = turned[h * HS : (h + 1) * HS].astype(BF16)


def attend(pair, at, hm, ho, w, bias):
    heads = bias.shape[0] // 2
    groups, _, tiles, half = hm.shape
    rows = groups * tiles
    seg = w.shape[1] // 6
    return pl.pallas_call(
        functools.partial(attend_kernel, pair),
        out_shape=jax.ShapeDtypeStruct((heads * HS, rows), BF16),
        in_specs=[SMEM] + [VMEM] * 4,
        out_specs=VMEM,
        scratch_shapes=[
            pltpu.VMEM((groups, 2, tiles, seg), BF16),
            pltpu.VMEM((2 * rows, seg), BF16),
            pltpu.VMEM((2 * rows, seg), BF16),
        ],
        compiler_params=params(48),
        cost_estimate=cost(5, 6, 1),
        name="attend",
    )(at, hm, ho, w, bias)


def finish_kernel(at_ref, a0_ref, a1_ref, a2_ref, a3_ref, wm_ref, wo_ref, hm_ref, ho_ref, out_ref):
    s, y, count = at_ref[0], at_ref[1], at_ref[2]
    groups, _, tiles, half = hm_ref.shape
    rows = groups * tiles
    mine = other = 0.0
    for k, att_ref in enumerate((a0_ref, a1_ref, a2_ref, a3_ref)):
        depth = att_ref.shape[0]
        span = pl.ds(pl.multiple_of(lax.rem(y + NY - k, NY) * depth, depth), depth)
        mine = mine + dot_general(att_ref[...], wm_ref[span, :], CONTRACT_FIRST)
        other = other + dot_general(att_ref[...], wo_ref[span, :], CONTRACT_FIRST)
    mine = mine + hm_ref[:, s].reshape(rows, half).astype(F32)
    other = other + ho_ref[:, s].reshape(rows, half).astype(F32)
    row = lax.broadcasted_iota(jnp.int32, (rows, half), 0)
    valid = place(row, s) < count
    left = jnp.where(valid, jnp.where(s == 0, mine, other), 0.0).astype(BF16)
    right = jnp.where(valid, jnp.where(s == 0, other, mine), 0.0).astype(BF16)
    span = NZ * tiles
    for y in range(NY):
        for part, lanes in ((left, slice(0, half)), (right, slice(half, 2 * half))):
            out_ref[:, y, :, lanes] = part[y * span : (y + 1) * span].reshape(NZ, tiles, half)


def finish(at, att, wm, wo, hm, ho):
    groups, _, tiles, half = hm.shape
    return pl.pallas_call(
        finish_kernel,
        out_shape=jax.ShapeDtypeStruct((NZ, NY, tiles, 2 * half), BF16),
        in_specs=[SMEM] + [VMEM] * 8,
        out_specs=VMEM,
        compiler_params=params(32),
        cost_estimate=cost(0.6, 4),
        name="finish",
    )(at, *att, wm, wo, hm, ho)


def body(
    head_out,
    proj_weight,
    norm_gain,
    embed_cot,
    tile_counts,
    seg_lengths,
    dilation,
    embed_weight,
    qkv_weight,
    out_weight,
):
    tokens = head_out[0]
    n_rows, aw = tokens.shape
    dt = proj_weight.shape[1]
    half = dt // 2
    tiles = embed_cot.shape[1]
    per_tile = n_rows // tiles
    fsdp = NZ * NY
    f = lax.axis_index("fsdp")
    s = lax.axis_index("seq")
    y = f % NY
    count = tile_counts[0]
    ds = out_weight.shape[1]
    shard_len = fsdp * tiles
    x = lax.axis_index("slide")
    at = jnp.stack([s, y, count, x, f // NY]).astype(jnp.int32)
    dslice = lax.dynamic_slice_in_dim
    heads = ds // HS // NY
    width = heads * HS

    def of_y(v, k):
        return lax.dynamic_index_in_dim(v, (y + k) % NY, 0, keepdims=False)

    bias = biases(at, seg_lengths, dilation, heads, shard_len)

    rows = proj_weight.shape[0]
    w_heads = qkv_weight.reshape(rows, 3, NY, 2, width // 2).transpose(2, 0, 3, 1, 4)
    w_heads = jnp.pad(w_heads, ((0, 0),) * 4 + ((0, 128 - width // 2),)).reshape(NY, rows, 6 * 128)
    w_heads = [of_y(w_heads, 0)] + [shift_y(of_y(w_heads, k), k) for k in range(1, NY)]
    w_heads = jnp.stack([w_heads[-j % NY] for j in range(NY)])
    w_heads = dslice(jnp.concatenate([w_heads, w_heads]), NY - y, NY, 0).reshape(NY * rows, 6 * 128)
    own_heads = w_heads
    w_heads = lax.all_gather(w_heads, "fsdp", axis=0, tiled=True, axis_index_groups=Z_GROUPS)

    quarter = ds // 2
    proj_half = dslice(proj_weight, s * half, half, 1)
    first = jnp.concatenate(
        [proj_half[:, :quarter], proj_half[:, quarter:]]
        + [dslice(w, s * quarter, quarter, 1) for w in (embed_weight, out_weight)]
    )
    first = a2a_z(copies(first, NZ))
    proj_mine = first[:, : 2 * rows]
    proj_mine = a2a_y(copies(after(after(proj_mine, bias), own_heads), NY))
    proj_mine = proj_mine.reshape(NY, NZ, 2, rows, quarter).transpose(1, 0, 3, 2, 4).reshape(aw, half)
    proj_other = swap(proj_mine)
    w_embed = first[:, 2 * rows : 4 * rows]
    w_embed = by_y(at, [w_embed] + [shift_y(w_embed, k) for k in range(1, NY)]).reshape(dt, quarter)

    def halves(v):
        return dslice(v, s * half, half, v.ndim - 1), dslice(v, (1 - s) * half, half, v.ndim - 1)

    gain = halves(norm_gain)
    embed, normed_mine, normed_other, inv_std = forward(at, tokens, proj_mine, proj_other, jnp.stack(gain), tiles)
    embed = embed.astype(BF16)
    embed_other = swap(embed)
    embed = jnp.concatenate([jnp.where(s == 0, embed, embed_other), jnp.where(s == 0, embed_other, embed)])
    hidden = dot(embed, w_embed).astype(BF16)
    local_hidden = hidden
    over_z = a2a_z(copies(hidden, NZ))
    hidden = a2a_y(copies(over_z, NY)).reshape(fsdp, 2, tiles, ds // 2)
    w_out = after(first[:, 4 * rows :], over_z)
    w_out = by_y(at, [w_out] + [shift_y(w_out, k) for k in range(1, NY)]).reshape(ds, quarter)
    w_out_other = swap(w_out)

    base = (s * fsdp + f) * tiles
    valid = (base + jnp.arange(tiles, dtype=jnp.int32) < count).astype(F32)
    valid = after(valid, local_hidden)
    grads = [c * valid[:, None] / per_tile * g for c, g in zip(halves(embed_cot[0].astype(F32)), gain)]
    mixed_mine, mixed_other, term_mine, term_other = backward(tokens, normed_mine, normed_other, inv_std, grads)
    pair = (term_mine.astype(F32) + swap(after(term_other, over_z)).astype(F32)).astype(BF16)
    parts = [of_y(pair, 0)] + [shift_y(of_y(pair, k), k) for k in range(1, NY)]
    share = sum(p.astype(F32) for p in parts).astype(BF16)

    hidden_other = swap(after(after(hidden, pair), w_heads))
    early = attend(0, after(at, w_out_other), hidden, hidden_other, w_heads, bias)
    late = attend(1, after(after(at, share), early), hidden, hidden_other, w_heads, bias)
    share = jnp.sum(a2a_z(after(share, early)).astype(F32), axis=0).astype(BF16)
    attended = jnp.concatenate([early, late])
    head_out_grad = head_out_grad_of(after(at, attended), mixed_mine, mixed_other, proj_mine, proj_other)
    late_share = after(share, attended)
    attended = after(attended, share)
    received = [attended] + [shift_y(attended, k) for k in range(1, NY)]
    share = sum(p.astype(F32) for p in [late_share] + [shift_x(late_share, k) for k in range(1, NX)]).astype(BF16)
    other = swap(share)
    slide_out = finish(after(after(at, share), head_out_grad), received, w_out, w_out_other, hidden, hidden_other)
    slide_out = slide_out.reshape(1, shard_len, ds)
    proj_grad = jnp.concatenate([jnp.where(s == 0, share, other), jnp.where(s == 0, other, share)], axis=1)
    return (slide_out, head_out_grad[None], proj_grad)


def solution(mesh):
    return jax.shard_map(
        body,
        mesh=mesh,
        in_specs=(
            P("slide", ("seq", "fsdp"), None),
            P("fsdp", None),
            P(),
            P("slide", ("seq", "fsdp"), None),
            P("slide"),
            P(),
            P(),
            P("fsdp", None),
            P("fsdp", None),
            P("fsdp", None),
        ),
        out_specs=(P("slide", "seq", None), P("slide", ("seq", "fsdp"), None), P("fsdp", None)),
        check_vma=False,
    )
```

```python
import functools

import jax
import jax.numpy as jnp
from jax import lax
from jax.experimental import pallas as pl
from jax.experimental.pallas import tpu as pltpu
from jax.sharding import PartitionSpec as P

HS = 48
NX, NZ, NY = 4, 8, 4
Z_GROUPS = [[z * NY + y for z in range(NZ)] for y in range(NY)]
Y_GROUPS = [[z * NY + y for y in range(NY)] for z in range(NZ)]
SWAP = [(0, 1), (1, 0)]
F32, BF16 = jnp.float32, jnp.bfloat16
VMEM = pl.BlockSpec(memory_space=pltpu.VMEM)
SMEM = pl.BlockSpec(memory_space=pltpu.SMEM)
CONTRACT_LAST = (((1,), (1,)), ((), ()))
CONTRACT_FIRST = (((0,), (0,)), ((), ()))
dot = functools.partial(jnp.dot, preferred_element_type=F32)
dot_general = functools.partial(lax.dot_general, preferred_element_type=F32)


def a2a_z(v):
    return lax.all_to_all(v, "fsdp", 0, 0, axis_index_groups=Z_GROUPS)


def a2a_y(v):
    return lax.all_to_all(v, "fsdp", 0, 0, axis_index_groups=Y_GROUPS)


def copies(v, n):
    return jnp.broadcast_to(v[None], (n,) + v.shape)


def swap(v):
    return lax.ppermute(v, "seq", SWAP)


def shift_y(v, k):
    return lax.ppermute(
        v, "fsdp", [(z * NY + y, z * NY + (y + k) % NY) for z in range(NZ) for y in range(NY)]
    )


def shift_x(v, k):
    return lax.ppermute(v, "slide", [(x, (x + k) % NX) for x in range(NX)])


def after(v, other):
    return v + (other[(0,) * other.ndim].astype(F32) * 0).astype(v.dtype)


def params(mib):
    return pltpu.CompilerParams(vmem_limit_bytes=mib * 1024 * 1024)


def cost(gflop, mb, mexp=0):
    return pl.CostEstimate(
        flops=int(gflop * 1e9), bytes_accessed=int(mb * 1e6), transcendentals=int(mexp * 1e6)
    )


def forward_kernel(tiles, at_ref, tok_ref, pm_ref, po_ref, gain_ref, out_ref, nm_ref, no_ref, inv_ref):
    tok = tok_ref[...]
    mixed = [dot(tok, pm_ref[...]), dot(tok, po_ref[...])]
    rows, half = mixed[0].shape
    centre = sum(jnp.sum(m, axis=-1, keepdims=True) for m in mixed) * (0.5 / half)
    shifted = [m - centre for m in mixed]
    var = sum(jnp.sum(m * m, axis=-1, keepdims=True) for m in shifted) * (0.5 / half)
    inv_std = lax.rsqrt(var + 1e-06)
    inv_ref[...] = jnp.broadcast_to(inv_std, inv_ref.shape)
    pooled = []
    for i, (m, n_ref) in enumerate(zip(shifted, (nm_ref, no_ref))):
        n = m * inv_std
        n_ref[...] = n
        mean = jnp.sum(n.reshape(tiles, rows // tiles, half), axis=1) * (tiles / rows)
        pooled.append(mean * gain_ref[i : i + 1, :])
    span = pl.ds(pl.multiple_of(pl.program_id(0) * tiles, tiles), tiles)
    for s in range(2):

        @pl.when(at_ref[0] == s)
        def _():
            out_ref[span, :half] = pooled[s]
            out_ref[span, half:] = pooled[1 - s]


def forward(at, tokens, pm, po, gain, tiles):
    rows, aw = tokens.shape
    half = pm.shape[1]
    steps = 2
    spec = pl.BlockSpec((rows // steps, half), lambda i: (i, 0))
    return pl.pallas_call(
        functools.partial(forward_kernel, tiles // steps),
        out_shape=(
            jax.ShapeDtypeStruct((tiles, 2 * half), F32),
            jax.ShapeDtypeStruct((rows, half), F32),
            jax.ShapeDtypeStruct((rows, half), F32),
            jax.ShapeDtypeStruct((rows, 128), F32),
        ),
        grid=(steps,),
        in_specs=[SMEM, pl.BlockSpec((rows // steps, aw), lambda i: (i, 0)), VMEM, VMEM, VMEM],
        out_specs=(
            pl.BlockSpec((tiles, 2 * half), lambda i: (0, 0)),
            spec,
            spec,
            pl.BlockSpec((rows // steps, 128), lambda i: (i, 0)),
        ),
        compiler_params=params(48),
        cost_estimate=cost(2.4, 10),
        name="forward",
    )(at, tokens, pm, po, gain)


def backward_kernel(tok_ref, nm_ref, no_ref, inv_ref, gm_ref, go_ref, xm_ref, xo_ref, tm_ref, to_ref, am_ref, ao_ref):
    step, steps = pl.program_id(0), pl.num_programs(0)
    tok = tok_ref[...]
    normed = [nm_ref[...], no_ref[...]]
    inv_std = inv_ref[:, :1]
    rows, half = normed[0].shape
    tiles = gm_ref.shape[1]
    grads = [gm_ref[0], go_ref[0]]
    mean = sum(jnp.sum(g, axis=-1, keepdims=True) for g in grads) * (0.5 / half)

    def per_token(v):
        return jnp.broadcast_to(v[:, None, :], (tiles, rows // tiles, v.shape[1])).reshape(rows, v.shape[1])

    along = sum(jnp.sum(per_token(g) * n, axis=-1, keepdims=True) for g, n in zip(grads, normed)) * (0.5 / half)
    mixed = [(inv_std * (per_token(g - mean) - n * along)).astype(BF16) for g, n in zip(grads, normed)]
    xm_ref[...] = mixed[0]
    xo_ref[...] = mixed[1]
    for acc_ref, term_ref, m in ((am_ref, tm_ref, mixed[0]), (ao_ref, to_ref, mixed[1])):
        term = dot_general(tok, m, CONTRACT_FIRST)

        @pl.when(step == 0)
        def _():
            acc_ref[...] = term

        @pl.when(step > 0)
        def _():
            acc_ref[...] += term

        @pl.when(step == steps - 1)
        def _():
            block = term_ref.shape[2]
            for z in range(NZ):
                for y in range(NY):
                    term_ref[y, z] = acc_ref[pl.ds((z * NY + y) * block, block), :].astype(BF16)


def backward(tokens, nm, no, inv_std, grads):
    rows, aw = tokens.shape
    half = nm.shape[1]
    tiles = grads[0].shape[0]
    steps = 2
    grads = [g.reshape(steps, tiles // steps, half) for g in grads]
    gspec = pl.BlockSpec((1, tiles // steps, half), lambda i: (i, 0, 0))
    tspec = pl.BlockSpec((NY, NZ, aw // (NY * NZ), half), lambda i: (0, 0, 0, 0))
    term = jax.ShapeDtypeStruct((NY, NZ, aw // (NY * NZ), half), BF16)
    wide = pl.BlockSpec((rows // steps, half), lambda i: (i, 0))
    mixed = jax.ShapeDtypeStruct((rows, half), BF16)
    return pl.pallas_call(
        backward_kernel,
        out_shape=(mixed, mixed, term, term),
        grid=(steps,),
        in_specs=[
            pl.BlockSpec((rows // steps, aw), lambda i: (i, 0)),
            wide,
            wide,
            pl.BlockSpec((rows // steps, 128), lambda i: (i, 0)),
            gspec,
            gspec,
        ],
        out_specs=(wide, wide, tspec, tspec),
        scratch_shapes=[pltpu.VMEM((aw, half), F32), pltpu.VMEM((aw, half), F32)],
        compiler_params=params(56),
        cost_estimate=cost(2.4, 16),
        name="backward",
    )(tokens, nm, no, inv_std, *grads)


def head_out_grad_kernel(at_ref, xm_ref, xo_ref, pm_ref, po_ref, out_ref):
    grad = dot_general(xm_ref[...], pm_ref[...], CONTRACT_LAST) + dot_general(xo_ref[...], po_ref[...], CONTRACT_LAST)
    out_ref[...] = grad.astype(BF16)


def head_out_grad_of(at, xm, xo, pm, po):
    rows, half = xm.shape
    aw = pm.shape[0]
    steps = 2
    spec = pl.BlockSpec((rows // steps, half), lambda i: (i, 0))
    return pl.pallas_call(
        head_out_grad_kernel,
        out_shape=jax.ShapeDtypeStruct((rows, aw), BF16),
        grid=(steps,),
        in_specs=[SMEM, spec, spec, VMEM, VMEM],
        out_specs=pl.BlockSpec((rows // steps, aw), lambda i: (i, 0)),
        compiler_params=params(32),
        cost_estimate=cost(2.4, 7),
        name="head_out_grad",
    )(at, xm, xo, pm, po)


def pair_sum_kernel(at_ref, mine_ref, other_ref, *out_refs):
    for k, out_ref in enumerate(out_refs):
        y = lax.rem(at_ref[1] + k, NY)
        for z in range(NZ):
            out_ref[z] = (mine_ref[y, z].astype(F32) + other_ref[y, z].astype(F32)).astype(BF16)


def pair_sum(at, mine, other):
    return pl.pallas_call(
        pair_sum_kernel,
        out_shape=[jax.ShapeDtypeStruct(mine.shape[1:], BF16)] * NY,
        in_specs=[SMEM, VMEM, VMEM],
        out_specs=[VMEM] * NY,
        compiler_params=params(32),
        cost_estimate=cost(0.01, 3),
        name="pair_sum",
    )(at, mine, other)


def by_y_kernel(at_ref, *refs):
    out_ref = refs[-1]
    for k, ref in enumerate(refs[:-1]):
        y = lax.rem(at_ref[1] + NY - k, NY)
        for z in range(NZ):
            out_ref[z, y] = ref[z]


def by_y(at, pieces):
    zs, rows, cols = pieces[0].shape
    return pl.pallas_call(
        by_y_kernel,
        out_shape=jax.ShapeDtypeStruct((zs, NY, rows, cols), BF16),
        in_specs=[SMEM] + [VMEM] * NY,
        out_specs=VMEM,
        compiler_params=params(32),
        cost_estimate=cost(0.01, 3),
        name="by_y",
    )(at, *pieces)


def place(row, s):
    return s * 512 + ((row // 16) % NZ * NY + row // (16 * NZ)) * 16 + row % 16


def bias_kernel(heads, at_ref, seg_ref, dil_ref, out_ref, done_ref, q_ref, k_ref):
    s, y, count = at_ref[0], at_ref[1], at_ref[2]
    rows = q_ref.shape[1]

    def fill(ref, pos, valid):
        lane = lax.broadcasted_iota(jnp.int32, pos.shape, 1)
        hits, residues = [], []
        for c in range(seg_ref.shape[0]):
            width = seg_ref[c]
            bits = 6 + sum((width > 64 << b).astype(jnp.int32) for b in range(4))
            ids = lax.shift_right_logical(jnp.full_like(pos, 2 * rows), jnp.full_like(pos, bits))
            ids = ids + lax.shift_right_logical(pos, jnp.full_like(pos, bits))
            hits.append((ids == lane) & valid)
            residues.append(pos & (dil_ref[c] - 1))
        for h in range(heads):
            head = y * heads + h
            any_hit = None
            for c, (hit, residue) in enumerate(zip(hits, residues)):
                hit = hit & (residue == (head & (dil_ref[c] - 1)))
                any_hit = hit if any_hit is None else any_hit | hit
            ref[h] = jnp.where(any_hit, 1.0, 0.0).astype(BF16)

    @pl.when(pl.program_id(0) == 0)
    def _():
        row = lax.broadcasted_iota(jnp.int32, (rows, 128), 0)
        pos = place(row, s)
        fill(q_ref, pos, pos >= 0)
        row = lax.broadcasted_iota(jnp.int32, (2 * rows, 128), 0)
        pos = place(row % rows, row // rows)
        fill(k_ref, pos, pos < count)
        done_ref[...] = jnp.zeros_like(done_ref)

    h = pl.program_id(0)
    block = 128
    for start in range(0, rows, block):
        span = pl.ds(start, block)
        counted = dot_general(q_ref[h, span, :], k_ref[h], CONTRACT_LAST)
        bias = jnp.full(counted.shape, -1e30, F32)
        for n, log2 in enumerate((0.0, 1.0, 1.584962500721156, 2.0, 2.321928094887362)):
            bias = jnp.where(counted > n + 0.5, log2, bias)
        out_ref[0, span, :] = bias


def biases(at, seg_lengths, dilation, heads, rows):
    return pl.pallas_call(
        functools.partial(bias_kernel, heads),
        out_shape=(jax.ShapeDtypeStruct((heads, rows, 2 * rows), F32), jax.ShapeDtypeStruct((8, 128), F32)),
        grid=(heads,),
        in_specs=[SMEM] * 3,
        out_specs=(
            pl.BlockSpec((1, rows, 2 * rows), lambda h: (h, 0, 0)),
            pl.BlockSpec((8, 128), lambda h: (0, 0)),
        ),
        scratch_shapes=[pltpu.VMEM((heads, rows, 128), BF16), pltpu.VMEM((heads, 2 * rows, 128), BF16)],
        compiler_params=params(40),
        cost_estimate=cost(1, 1),
        name="biases",
    )(at, seg_lengths, dilation)


def attend_kernel(at_ref, hm_ref, ho_ref, wm_ref, wo_ref, bias_ref, out_ref, w_ref, q_ref, k_ref, v_ref):
    s = at_ref[0]
    rows = hm_ref.shape[0]
    half = hm_ref.shape[1] // 2
    heads, block, keys = bias_ref.shape
    seg = q_ref.shape[2]

    @pl.when(pl.program_id(0) == 0)
    def _():
        for z in range(NZ):
            w_ref[z, s] = wm_ref[z]
            w_ref[z, 1 - s] = wo_ref[z]
        w_mine = w_ref[pl.ds(s * (NZ // 2), NZ // 2)].reshape(half, w_ref.shape[3])
        w_other = w_ref[pl.ds((1 - s) * (NZ // 2), NZ // 2)].reshape(half, w_ref.shape[3])
        for core in range(2):
            lanes = slice(core * half, (core + 1) * half)
            all_parts = dot(hm_ref[:, lanes], w_mine) + dot(ho_ref[:, lanes], w_other)
            span = pl.ds(core * rows, rows)
            q_ref[core] = all_parts[:, :seg].astype(BF16)
            k_ref[span, :] = all_parts[:, seg : 2 * seg].astype(BF16)
            v_ref[span, :] = all_parts[:, 2 * seg :].astype(BF16)

    lane_head = lax.broadcasted_iota(jnp.int32, (1, seg), 1) // HS
    scale = HS ** (-0.5) * 1.4426950408889634
    queries = q_ref[s, pl.ds(pl.multiple_of(pl.program_id(0) * block, block), block), :]
    queries = jnp.concatenate([jnp.where(lane_head == h, queries, 0).astype(BF16) for h in range(heads)])
    scores = dot_general(queries, k_ref[...], CONTRACT_LAST)
    scores = scores * scale + bias_ref[...].reshape(heads * block, keys)
    weights = jnp.exp2(scores - jnp.max(scores, axis=-1, keepdims=True))
    total = jnp.sum(weights, axis=-1, keepdims=True)
    part = dot(weights.astype(BF16), v_ref[...]) * (1.0 / total)
    for h in range(heads):
        turned = part[h * block : (h + 1) * block].T
        out_ref[h * HS : (h + 1) * HS, :] = turned[h * HS : (h + 1) * HS].astype(BF16)


def attend(at, hm, ho, wm, wo, bias):
    heads, rows, keys = bias.shape
    seg = wm.shape[2] // 3
    block = 128
    return pl.pallas_call(
        attend_kernel,
        out_shape=jax.ShapeDtypeStruct((heads * HS, rows), BF16),
        grid=(rows // block,),
        in_specs=[SMEM] + [VMEM] * 4 + [pl.BlockSpec((heads, block, keys), lambda i: (0, i, 0))],
        out_specs=pl.BlockSpec((heads * HS, block), lambda i: (0, i)),
        scratch_shapes=[
            pltpu.VMEM((NZ, 2) + wm.shape[1:], BF16),
            pltpu.VMEM((2, rows, seg), BF16),
            pltpu.VMEM((keys, seg), BF16),
            pltpu.VMEM((keys, seg), BF16),
        ],
        compiler_params=params(48),
        cost_estimate=cost(8, 12, 2),
        name="attend",
    )(at, hm, ho, wm, wo, bias)


def finish_kernel(at_ref, a0_ref, a1_ref, a2_ref, a3_ref, wm_ref, wo_ref, hm_ref, ho_ref, out_ref):
    s, y, count = at_ref[0], at_ref[1], at_ref[2]
    rows, half = hm_ref.shape[0], hm_ref.shape[1] // 2
    tiles = out_ref.shape[2]
    mine = other = 0.0
    for k, att_ref in enumerate((a0_ref, a1_ref, a2_ref, a3_ref)):
        depth = att_ref.shape[0]
        span = pl.ds(pl.multiple_of(lax.rem(y + NY - k, NY) * depth, depth), depth)
        mine = mine + dot_general(att_ref[...], wm_ref[span, :], CONTRACT_FIRST)
        other = other + dot_general(att_ref[...], wo_ref[span, :], CONTRACT_FIRST)
    lanes = pl.ds(pl.multiple_of(s * half, half), half)
    mine = mine + hm_ref[:, lanes].astype(F32)
    other = other + ho_ref[:, lanes].astype(F32)
    row = lax.broadcasted_iota(jnp.int32, (rows, half), 0)
    valid = place(row, s) < count
    left = jnp.where(valid, jnp.where(s == 0, mine, other), 0.0).astype(BF16)
    right = jnp.where(valid, jnp.where(s == 0, other, mine), 0.0).astype(BF16)
    span = NZ * tiles
    for y in range(NY):
        for part, lanes in ((left, slice(0, half)), (right, slice(half, 2 * half))):
            out_ref[:, y, :, lanes] = part[y * span : (y + 1) * span].reshape(NZ, tiles, half)


def finish(at, att, wm, wo, hm, ho, tiles):
    return pl.pallas_call(
        finish_kernel,
        out_shape=jax.ShapeDtypeStruct((NZ, NY, tiles, hm.shape[1]), BF16),
        in_specs=[SMEM] + [VMEM] * 8,
        out_specs=VMEM,
        compiler_params=params(32),
        cost_estimate=cost(0.6, 4),
        name="finish",
    )(at, *att, wm, wo, hm, ho)


def body(
    head_out,
    proj_weight,
    norm_gain,
    embed_cot,
    tile_counts,
    seg_lengths,
    dilation,
    embed_weight,
    qkv_weight,
    out_weight,
):
    tokens = head_out[0]
    n_rows, aw = tokens.shape
    dt = proj_weight.shape[1]
    half = dt // 2
    tiles = embed_cot.shape[1]
    per_tile = n_rows // tiles
    fsdp = NZ * NY
    f = lax.axis_index("fsdp")
    s = lax.axis_index("seq")
    y = f % NY
    count = tile_counts[0]
    ds = out_weight.shape[1]
    shard_len = fsdp * tiles
    x = lax.axis_index("slide")
    at = jnp.stack([s, y, count, x, f // NY]).astype(jnp.int32)
    dslice = lax.dynamic_slice_in_dim
    heads = ds // HS // NY
    width = heads * HS

    def of_y(v, k):
        return lax.dynamic_index_in_dim(v, (y + k) % NY, 0, keepdims=False)

    bias, zero = biases(at, seg_lengths, dilation, heads, shard_len)

    rows = proj_weight.shape[0]
    w_heads = qkv_weight.reshape(rows, 3, NY, width).transpose(2, 0, 1, 3)
    w_heads = jnp.pad(w_heads, ((0, 0), (0, 0), (0, 0), (0, 256 - width))).reshape(NY, rows, 3 * 256)
    w_heads = [of_y(w_heads, 0)] + [shift_y(of_y(w_heads, k), k) for k in range(1, NY)]
    w_heads = jnp.stack([w_heads[-j % NY] for j in range(NY)])
    w_heads = dslice(jnp.concatenate([w_heads, w_heads]), (NY - y + 2 * s) % NY, 2, 0).reshape(2 * rows, 3 * 256)

    quarter = ds // 2
    proj_half = dslice(proj_weight, s * half, half, 1)
    first = jnp.concatenate(
        [proj_half[:, :quarter], proj_half[:, quarter:]]
        + [dslice(w, s * quarter, quarter, 1) for w in (embed_weight, out_weight)]
    )
    first = a2a_z(copies(first, NZ))
    proj_mine = first[:, : 2 * rows]
    proj_mine = a2a_y(copies(after(after(proj_mine, zero), w_heads), NY))
    proj_mine = proj_mine.reshape(NY, NZ, 2, rows, quarter).transpose(1, 0, 3, 2, 4).reshape(aw, half)
    proj_other = swap(proj_mine)
    w_embed = first[:, 2 * rows : 4 * rows]
    w_embed = by_y(at, [w_embed] + [shift_y(w_embed, k) for k in range(1, NY)]).reshape(dt, quarter)

    def halves(v):
        return dslice(v, s * half, half, v.ndim - 1), dslice(v, (1 - s) * half, half, v.ndim - 1)

    gain = halves(norm_gain)
    embed, normed_mine, normed_other, inv_std = forward(at, tokens, proj_mine, proj_other, jnp.stack(gain), tiles)
    embed = embed.astype(BF16)
    embed_other = swap(embed)
    embed = jnp.concatenate([jnp.where(s == 0, embed, embed_other), jnp.where(s == 0, embed_other, embed)])
    hidden = dot(embed, w_embed).astype(BF16)
    hidden = jnp.concatenate([hidden[:tiles], hidden[tiles:]], axis=1)
    local_hidden = hidden
    w_out = after(first[:, 4 * rows :], local_hidden)
    w_out = by_y(at, [w_out] + [shift_y(w_out, k) for k in range(1, NY)]).reshape(ds, quarter)
    w_out_other = swap(w_out)
    second = a2a_z(copies(jnp.concatenate([hidden, w_heads]), NZ))
    w_heads = second[:, tiles:]
    w_heads_other = swap(w_heads)
    hidden = a2a_y(copies(after(second[:, :tiles], w_out), NY)).reshape(shard_len, ds)
    hidden_other = swap(hidden)

    base = (s * fsdp + f) * tiles
    valid = (base + jnp.arange(tiles, dtype=jnp.int32) < count).astype(F32)
    valid = after(valid, local_hidden)
    grads = [c * valid[:, None] / per_tile * g for c, g in zip(halves(embed_cot[0].astype(F32)), gain)]
    mixed_mine, mixed_other, term_mine, term_other = backward(tokens, normed_mine, normed_other, inv_std, grads)
    parts = pair_sum(after(at, second), term_mine, swap(term_other))
    parts = [parts[0]] + [shift_y(parts[k], k) for k in range(1, NY)]
    share = sum(p.astype(F32) for p in parts).astype(BF16)

    attended = attend(after(at, share), hidden, hidden_other, w_heads, w_heads_other, bias)
    share = a2a_z(after(share, hidden)).astype(F32)
    share = jnp.sum(after(share, attended), axis=0).astype(BF16)
    attended = after(attended, share)
    attended = after(attended, share)
    received = [attended] + [shift_y(attended, k) for k in range(1, NY)]
    share = sum(p.astype(F32) for p in [share] + [shift_x(share, k) for k in range(1, NX)]).astype(BF16)
    other = swap(share)
    head_out_grad = head_out_grad_of(after(at, share), mixed_mine, mixed_other, proj_mine, proj_other)
    slide_out = finish(after(at, head_out_grad), received, w_out, w_out_other, hidden, hidden_other, tiles)
    slide_out = slide_out.reshape(1, shard_len, ds)
    proj_grad = jnp.concatenate([jnp.where(s == 0, share, other), jnp.where(s == 0, other, share)], axis=1)
    return (slide_out, head_out_grad[None], proj_grad)


def solution(mesh):
    return jax.shard_map(
        body,
        mesh=mesh,
        in_specs=(
            P("slide", ("seq", "fsdp"), None),
            P("fsdp", None),
            P(),
            P("slide", ("seq", "fsdp"), None),
            P("slide"),
            P(),
            P(),
            P("fsdp", None),
            P("fsdp", None),
            P("fsdp", None),
        ),
        out_specs=(P("slide", "seq", None), P("slide", ("seq", "fsdp"), None), P("fsdp", None)),
        check_vma=False,
    )
```

```python
import functools

import jax
import jax.numpy as jnp
from jax import lax
from jax.experimental import pallas as pl
from jax.experimental.pallas import tpu as pltpu
from jax.sharding import PartitionSpec as P

HS = 48
NX, NZ, NY = 4, 8, 4
Z_GROUPS = [[z * NY + y for z in range(NZ)] for y in range(NY)]
Y_GROUPS = [[z * NY + y for y in range(NY)] for z in range(NZ)]
SWAP = [(0, 1), (1, 0)]
F32, BF16 = jnp.float32, jnp.bfloat16
VMEM = pl.BlockSpec(memory_space=pltpu.VMEM)
SMEM = pl.BlockSpec(memory_space=pltpu.SMEM)
CONTRACT_LAST = (((1,), (1,)), ((), ()))
CONTRACT_FIRST = (((0,), (0,)), ((), ()))
dot = functools.partial(jnp.dot, preferred_element_type=F32)
dot_general = functools.partial(lax.dot_general, preferred_element_type=F32)


def a2a_z(v):
    return lax.all_to_all(v, "fsdp", 0, 0, axis_index_groups=Z_GROUPS)


def a2a_y(v):
    return lax.all_to_all(v, "fsdp", 0, 0, axis_index_groups=Y_GROUPS)


def copies(v, n):
    return jnp.broadcast_to(v[None], (n,) + v.shape)


def swap(v):
    return lax.ppermute(v, "seq", SWAP)


def shift_y(v, k):
    return lax.ppermute(
        v, "fsdp", [(z * NY + y, z * NY + (y + k) % NY) for z in range(NZ) for y in range(NY)]
    )


def shift_z(v, k):
    return lax.ppermute(
        v, "fsdp", [(z * NY + y, (z + k) % NZ * NY + y) for z in range(NZ) for y in range(NY)]
    )


def shift_x(v, k):
    return lax.ppermute(v, "slide", [(x, (x + k) % NX) for x in range(NX)])


def after(v, other):
    return v + (other[(0,) * other.ndim].astype(F32) * 0).astype(v.dtype)


def params(mib):
    return pltpu.CompilerParams(vmem_limit_bytes=mib * 1024 * 1024)


def cost(gflop, mb, mexp=0):
    return pl.CostEstimate(
        flops=int(gflop * 1e9), bytes_accessed=int(mb * 1e6), transcendentals=int(mexp * 1e6)
    )


def forward_kernel(tiles, at_ref, tok_ref, pm_ref, po_ref, gain_ref, out_ref, nm_ref, no_ref, inv_ref):
    tok = tok_ref[...]
    mixed = [dot(tok, pm_ref[...]), dot(tok, po_ref[...])]
    rows, half = mixed[0].shape
    centre = sum(jnp.sum(m, axis=-1, keepdims=True) for m in mixed) * (0.5 / half)
    shifted = [m - centre for m in mixed]
    var = sum(jnp.sum(m * m, axis=-1, keepdims=True) for m in shifted) * (0.5 / half)
    inv_std = lax.rsqrt(var + 1e-06)
    inv_ref[...] = jnp.broadcast_to(inv_std, inv_ref.shape)
    pooled = []
    for i, (m, n_ref) in enumerate(zip(shifted, (nm_ref, no_ref))):
        n = m * inv_std
        n_ref[...] = n
        mean = jnp.sum(n.reshape(tiles, rows // tiles, half), axis=1) * (tiles / rows)
        pooled.append(mean * gain_ref[i : i + 1, :])
    span = pl.ds(pl.multiple_of(pl.program_id(0) * tiles, tiles), tiles)
    for s in range(2):

        @pl.when(at_ref[0] == s)
        def _():
            out_ref[span, :half] = pooled[s]
            out_ref[span, half:] = pooled[1 - s]


def forward(at, tokens, pm, po, gain, tiles):
    rows, aw = tokens.shape
    half = pm.shape[1]
    steps = 2
    spec = pl.BlockSpec((rows // steps, half), lambda i: (i, 0))
    return pl.pallas_call(
        functools.partial(forward_kernel, tiles // steps),
        out_shape=(
            jax.ShapeDtypeStruct((tiles, 2 * half), F32),
            jax.ShapeDtypeStruct((rows, half), F32),
            jax.ShapeDtypeStruct((rows, half), F32),
            jax.ShapeDtypeStruct((rows, 128), F32),
        ),
        grid=(steps,),
        in_specs=[SMEM, pl.BlockSpec((rows // steps, aw), lambda i: (i, 0)), VMEM, VMEM, VMEM],
        out_specs=(
            pl.BlockSpec((tiles, 2 * half), lambda i: (0, 0)),
            spec,
            spec,
            pl.BlockSpec((rows // steps, 128), lambda i: (i, 0)),
        ),
        compiler_params=params(48),
        cost_estimate=cost(2.4, 10),
        name="forward",
    )(at, tokens, pm, po, gain)


def backward_kernel(tok_ref, nm_ref, no_ref, inv_ref, gm_ref, go_ref, xm_ref, xo_ref, tm_ref, to_ref, done_ref, am_ref, ao_ref):
    step, steps = pl.program_id(0), pl.num_programs(0)
    tok = tok_ref[...]
    normed = [nm_ref[...], no_ref[...]]
    inv_std = inv_ref[:, :1]
    rows, half = normed[0].shape
    tiles = gm_ref.shape[1]
    grads = [gm_ref[0], go_ref[0]]
    mean = sum(jnp.sum(g, axis=-1, keepdims=True) for g in grads) * (0.5 / half)

    def per_token(v):
        return jnp.broadcast_to(v[:, None, :], (tiles, rows // tiles, v.shape[1])).reshape(rows, v.shape[1])

    along = sum(jnp.sum(per_token(g) * n, axis=-1, keepdims=True) for g, n in zip(grads, normed)) * (0.5 / half)
    mixed = [(inv_std * (per_token(g - mean) - n * along)).astype(BF16) for g, n in zip(grads, normed)]
    done_ref[...] = jnp.zeros_like(done_ref)
    xm_ref[...] = mixed[0]
    xo_ref[...] = mixed[1]
    for acc_ref, term_ref, m in ((am_ref, tm_ref, mixed[0]), (ao_ref, to_ref, mixed[1])):
        term = dot_general(tok, m, CONTRACT_FIRST)

        @pl.when(step == 0)
        def _():
            acc_ref[...] = term

        @pl.when(step > 0)
        def _():
            acc_ref[...] += term

        @pl.when(step == steps - 1)
        def _():
            block = term_ref.shape[2]
            for z in range(NZ):
                for y in range(NY):
                    term_ref[y, z] = acc_ref[pl.ds((z * NY + y) * block, block), :].astype(BF16)


def backward(tokens, nm, no, inv_std, grads):
    rows, aw = tokens.shape
    half = nm.shape[1]
    tiles = grads[0].shape[0]
    steps = 2
    grads = [g.reshape(steps, tiles // steps, half) for g in grads]
    gspec = pl.BlockSpec((1, tiles // steps, half), lambda i: (i, 0, 0))
    tspec = pl.BlockSpec((NY, NZ, aw // (NY * NZ), half), lambda i: (0, 0, 0, 0))
    term = jax.ShapeDtypeStruct((NY, NZ, aw // (NY * NZ), half), BF16)
    wide = pl.BlockSpec((rows // steps, half), lambda i: (i, 0))
    mixed = jax.ShapeDtypeStruct((rows, half), BF16)
    return pl.pallas_call(
        backward_kernel,
        out_shape=(mixed, mixed, term, term, jax.ShapeDtypeStruct((8, 128), F32)),
        grid=(steps,),
        in_specs=[
            pl.BlockSpec((rows // steps, aw), lambda i: (i, 0)),
            wide,
            wide,
            pl.BlockSpec((rows // steps, 128), lambda i: (i, 0)),
            gspec,
            gspec,
        ],
        out_specs=(wide, wide, tspec, tspec, pl.BlockSpec((8, 128), lambda i: (0, 0))),
        scratch_shapes=[pltpu.VMEM((aw, half), F32), pltpu.VMEM((aw, half), F32)],
        compiler_params=params(56),
        cost_estimate=cost(2.4, 16),
        name="backward",
    )(tokens, nm, no, inv_std, *grads)


def head_out_grad_kernel(at_ref, xm_ref, xo_ref, pm_ref, po_ref, out_ref, done_ref):
    done_ref[...] = jnp.zeros_like(done_ref)
    grad = dot_general(xm_ref[...], pm_ref[...], CONTRACT_LAST) + dot_general(xo_ref[...], po_ref[...], CONTRACT_LAST)
    out_ref[...] = grad.astype(BF16)


def head_out_grad_of(at, xm, xo, pm, po):
    rows, half = xm.shape
    aw = pm.shape[0]
    steps = 2
    spec = pl.BlockSpec((rows // steps, half), lambda i: (i, 0))
    return pl.pallas_call(
        head_out_grad_kernel,
        out_shape=(jax.ShapeDtypeStruct((rows, aw), BF16), jax.ShapeDtypeStruct((8, 128), F32)),
        grid=(steps,),
        in_specs=[SMEM, spec, spec, VMEM, VMEM],
        out_specs=(
            pl.BlockSpec((rows // steps, aw), lambda i: (i, 0)),
            pl.BlockSpec((8, 128), lambda i: (0, 0)),
        ),
        compiler_params=params(32),
        cost_estimate=cost(0.01, 0.1),
        name="head_out_grad",
    )(at, xm, xo, pm, po)


def pair_sum_kernel(at_ref, mine_ref, other_ref, *out_refs):
    for k, out_ref in enumerate(out_refs):
        y = lax.rem(at_ref[1] + k, NY)
        for z in range(NZ):
            out_ref[z] = (mine_ref[y, z].astype(F32) + other_ref[y, z].astype(F32)).astype(BF16)


def pair_sum(at, mine, other):
    return pl.pallas_call(
        pair_sum_kernel,
        out_shape=[jax.ShapeDtypeStruct(mine.shape[1:], BF16)] * NY,
        in_specs=[SMEM, VMEM, VMEM],
        out_specs=[VMEM] * NY,
        compiler_params=params(32),
        cost_estimate=cost(0.001, 0.1),
        name="pair_sum",
    )(at, mine, other)


def y_sum_kernel(at_ref, *refs):
    for k, out_ref in enumerate(refs[NY:]):
        z = lax.rem(at_ref[4] + k, NZ)
        out_ref[...] = sum(ref[z].astype(F32) for ref in refs[:NY]).astype(BF16)


def y_sum(at, parts):
    return pl.pallas_call(
        y_sum_kernel,
        out_shape=[jax.ShapeDtypeStruct(parts[0].shape[1:], BF16)] * NZ,
        in_specs=[SMEM] + [VMEM] * NY,
        out_specs=[VMEM] * NZ,
        compiler_params=params(32),
        cost_estimate=cost(0.001, 0.1),
        name="y_sum",
    )(at, *parts)


def by_y_kernel(cuts, at_ref, *refs):
    for k, ref in enumerate(refs[:NY]):
        y = lax.rem(at_ref[1] + NY - k, NY)
        for (start, stop), out_ref in zip(cuts, refs[NY:]):
            for z in range(NZ):
                out_ref[z, y] = ref[z, start:stop, :]


def by_y(at, pieces, *sizes):
    zs, _, cols = pieces[0].shape
    stops = [sum(sizes[: i + 1]) for i in range(len(sizes))]
    cuts = [(stop - size, stop) for stop, size in zip(stops, sizes)]
    return pl.pallas_call(
        functools.partial(by_y_kernel, cuts),
        out_shape=[jax.ShapeDtypeStruct((zs, NY, size, cols), BF16) for size in sizes],
        in_specs=[SMEM] + [VMEM] * NY,
        out_specs=[VMEM] * len(sizes),
        compiler_params=params(32),
        cost_estimate=cost(0.01, 1),
        name="by_y",
    )(at, *pieces)


def place(row, s):
    return s * 512 + ((row // 16) % NZ * NY + row // (16 * NZ)) * 16 + row % 16


def bias_kernel(heads, at_ref, seg_ref, dil_ref, out_ref, done_ref, q_ref, k_ref):
    s, y, count = at_ref[0], at_ref[1], at_ref[2]
    rows = q_ref.shape[1]

    def fill(ref, pos, valid):
        lane = lax.broadcasted_iota(jnp.int32, pos.shape, 1)
        hits, residues = [], []
        for c in range(seg_ref.shape[0]):
            width = seg_ref[c]
            bits = 6 + sum((width > 64 << b).astype(jnp.int32) for b in range(4))
            ids = lax.shift_right_logical(jnp.full_like(pos, 2 * rows), jnp.full_like(pos, bits))
            ids = ids + lax.shift_right_logical(pos, jnp.full_like(pos, bits))
            hits.append((ids == lane) & valid)
            residues.append(pos & (dil_ref[c] - 1))
        for h in range(heads):
            head = y * heads + h
            any_hit = None
            for c, (hit, residue) in enumerate(zip(hits, residues)):
                hit = hit & (residue == (head & (dil_ref[c] - 1)))
                any_hit = hit if any_hit is None else any_hit | hit
            ref[h] = jnp.where(any_hit, 1.0, 0.0).astype(BF16)

    @pl.when(pl.program_id(0) == 0)
    def _():
        row = lax.broadcasted_iota(jnp.int32, (rows, 128), 0)
        pos = place(row, s)
        fill(q_ref, pos, pos >= 0)
        row = lax.broadcasted_iota(jnp.int32, (2 * rows, 128), 0)
        pos = place(row % rows, row // rows)
        fill(k_ref, pos, pos < count)
        done_ref[...] = jnp.zeros_like(done_ref)

    h = pl.program_id(0)
    block = 128
    for start in range(0, rows, block):
        span = pl.ds(start, block)
        counted = dot_general(q_ref[h, span, :], k_ref[h], CONTRACT_LAST)
        bias = jnp.full(counted.shape, -1e30, F32)
        for n, log2 in enumerate((0.0, 1.0, 1.584962500721156, 2.0, 2.321928094887362)):
            bias = jnp.where(counted > n + 0.5, log2, bias)
        out_ref[0, span, :] = bias


def biases(at, seg_lengths, dilation, heads, rows):
    return pl.pallas_call(
        functools.partial(bias_kernel, heads),
        out_shape=(jax.ShapeDtypeStruct((heads, rows, 2 * rows), F32), jax.ShapeDtypeStruct((8, 128), F32)),
        grid=(heads,),
        in_specs=[SMEM] * 3,
        out_specs=(
            pl.BlockSpec((1, rows, 2 * rows), lambda h: (h, 0, 0)),
            pl.BlockSpec((8, 128), lambda h: (0, 0)),
        ),
        scratch_shapes=[pltpu.VMEM((heads, rows, 128), BF16), pltpu.VMEM((heads, 2 * rows, 128), BF16)],
        compiler_params=params(40),
        cost_estimate=cost(1, 1),
        name="biases",
    )(at, seg_lengths, dilation)


def attend_kernel(at_ref, hm_ref, ho_ref, wm_ref, wo_ref, bias_ref, out_ref, w_ref, q_ref, k_ref, v_ref):
    s = at_ref[0]
    rows = hm_ref.shape[0]
    half = hm_ref.shape[1] // 2
    heads, block, keys = bias_ref.shape
    seg = q_ref.shape[2]

    @pl.when(pl.program_id(0) == 0)
    def _():
        for z in range(NZ):
            w_ref[z, s] = wm_ref[z]
            w_ref[z, 1 - s] = wo_ref[z]
        w_mine = w_ref[pl.ds(s * (NZ // 2), NZ // 2)].reshape(half, w_ref.shape[3])
        w_other = w_ref[pl.ds((1 - s) * (NZ // 2), NZ // 2)].reshape(half, w_ref.shape[3])
        for core in range(2):
            lanes = slice(core * half, (core + 1) * half)
            all_parts = dot(hm_ref[:, lanes], w_mine) + dot(ho_ref[:, lanes], w_other)
            span = pl.ds(core * rows, rows)
            q_ref[core] = all_parts[:, :seg].astype(BF16)
            k_ref[span, :] = all_parts[:, seg : 2 * seg].astype(BF16)
            v_ref[span, :] = all_parts[:, 2 * seg :].astype(BF16)

    lane_head = lax.broadcasted_iota(jnp.int32, (1, seg), 1) // HS
    scale = HS ** (-0.5) * 1.4426950408889634
    queries = q_ref[s, pl.ds(pl.multiple_of(pl.program_id(0) * block, block), block), :]
    queries = jnp.concatenate([jnp.where(lane_head == h, queries, 0).astype(BF16) for h in range(heads)])
    scores = dot_general(queries, k_ref[...], CONTRACT_LAST)
    scores = scores * scale + bias_ref[...].reshape(heads * block, keys)
    weights = jnp.exp2(scores - jnp.max(scores, axis=-1, keepdims=True))
    total = jnp.sum(weights, axis=-1, keepdims=True)
    part = dot(weights.astype(BF16), v_ref[...]) * (1.0 / total)
    for h in range(heads):
        turned = part[h * block : (h + 1) * block].T
        out_ref[h * HS : (h + 1) * HS, :] = turned[h * HS : (h + 1) * HS].astype(BF16)


def attend(at, hm, ho, wm, wo, bias):
    heads, rows, keys = bias.shape
    seg = wm.shape[2] // 3
    block = 128
    return pl.pallas_call(
        attend_kernel,
        out_shape=jax.ShapeDtypeStruct((heads * HS, rows), BF16),
        grid=(rows // block,),
        in_specs=[SMEM] + [VMEM] * 4 + [pl.BlockSpec((heads, block, keys), lambda i: (0, i, 0))],
        out_specs=pl.BlockSpec((heads * HS, block), lambda i: (0, i)),
        scratch_shapes=[
            pltpu.VMEM((NZ, 2) + wm.shape[1:], BF16),
            pltpu.VMEM((2, rows, seg), BF16),
            pltpu.VMEM((keys, seg), BF16),
            pltpu.VMEM((keys, seg), BF16),
        ],
        compiler_params=params(48),
        cost_estimate=cost(8, 12, 2),
        name="attend",
    )(at, hm, ho, wm, wo, bias)


def finish_kernel(at_ref, a0_ref, a1_ref, a2_ref, a3_ref, wm_ref, wo_ref, hm_ref, ho_ref, out_ref):
    s, y, count = at_ref[0], at_ref[1], at_ref[2]
    rows, half = hm_ref.shape[0], hm_ref.shape[1] // 2
    tiles = out_ref.shape[2]
    mine = other = 0.0
    for k, att_ref in enumerate((a0_ref, a1_ref, a2_ref, a3_ref)):
        depth = att_ref.shape[0]
        span = pl.ds(pl.multiple_of(lax.rem(y + NY - k, NY) * depth, depth), depth)
        mine = mine + dot_general(att_ref[...], wm_ref[span, :], CONTRACT_FIRST)
        other = other + dot_general(att_ref[...], wo_ref[span, :], CONTRACT_FIRST)
    lanes = pl.ds(pl.multiple_of(s * half, half), half)
    mine = mine + hm_ref[:, lanes].astype(F32)
    other = other + ho_ref[:, lanes].astype(F32)
    row = lax.broadcasted_iota(jnp.int32, (rows, half), 0)
    valid = place(row, s) < count
    left = jnp.where(valid, jnp.where(s == 0, mine, other), 0.0).astype(BF16)
    right = jnp.where(valid, jnp.where(s == 0, other, mine), 0.0).astype(BF16)
    span = NZ * tiles
    for y in range(NY):
        for part, lanes in ((left, slice(0, half)), (right, slice(half, 2 * half))):
            out_ref[:, y, :, lanes] = part[y * span : (y + 1) * span].reshape(NZ, tiles, half)


def finish(at, att, wm, wo, hm, ho, tiles):
    return pl.pallas_call(
        finish_kernel,
        out_shape=jax.ShapeDtypeStruct((NZ, NY, tiles, hm.shape[1]), BF16),
        in_specs=[SMEM] + [VMEM] * 8,
        out_specs=VMEM,
        compiler_params=params(32),
        cost_estimate=cost(0.6, 4),
        name="finish",
    )(at, *att, wm, wo, hm, ho)


def body(
    head_out,
    proj_weight,
    norm_gain,
    embed_cot,
    tile_counts,
    seg_lengths,
    dilation,
    embed_weight,
    qkv_weight,
    out_weight,
):
    tokens = head_out[0]
    n_rows, aw = tokens.shape
    dt = proj_weight.shape[1]
    half = dt // 2
    tiles = embed_cot.shape[1]
    per_tile = n_rows // tiles
    fsdp = NZ * NY
    f = lax.axis_index("fsdp")
    s = lax.axis_index("seq")
    y = f % NY
    count = tile_counts[0]
    ds = out_weight.shape[1]
    shard_len = fsdp * tiles
    x = lax.axis_index("slide")
    at = jnp.stack([s, y, count, x, f // NY]).astype(jnp.int32)
    dslice = lax.dynamic_slice_in_dim
    heads = ds // HS // NY
    width = heads * HS

    def of_y(v, k):
        return lax.dynamic_index_in_dim(v, (y + k) % NY, 0, keepdims=False)

    bias, zero = biases(at, seg_lengths, dilation, heads, shard_len)

    rows = proj_weight.shape[0]
    w_heads = qkv_weight.reshape(rows, 3, NY, width).transpose(2, 0, 1, 3)
    w_heads = jnp.pad(w_heads, ((0, 0), (0, 0), (0, 0), (0, 256 - width))).reshape(NY, rows, 3 * 256)

    quarter = ds // 2
    proj_half = dslice(proj_weight, s * half, half, 1)
    first = jnp.concatenate(
        [proj_half[:, :quarter], proj_half[:, quarter:]]
        + [dslice(w, s * quarter, quarter, 1) for w in (embed_weight, out_weight)]
    )
    first = a2a_z(copies(first, NZ))
    w_heads = jnp.concatenate([w_heads[..., :quarter], w_heads[..., quarter:]], axis=1)
    proj_mine = jnp.concatenate([copies(first[:, : 2 * rows], NY), after(w_heads, zero)[:, None]], axis=1)
    proj_mine = a2a_y(proj_mine)
    w_heads = dslice(proj_mine[:, NZ], 2 * s, 2, 0).reshape(2, 2, rows, quarter)
    w_heads = jnp.concatenate([w_heads[:, 0], w_heads[:, 1]], axis=2).reshape(2 * rows, 3 * 256)
    proj_mine = proj_mine[:, :NZ].reshape(NY, NZ, 2, rows, quarter).transpose(1, 0, 3, 2, 4).reshape(aw, half)
    proj_other = swap(proj_mine)
    others = first[:, 2 * rows :]
    others = [others] + [shift_y(others, k) for k in range(1, NY)]

    def halves(v):
        return dslice(v, s * half, half, v.ndim - 1), dslice(v, (1 - s) * half, half, v.ndim - 1)

    gain = halves(norm_gain)
    embed, normed_mine, normed_other, inv_std = forward(at, tokens, proj_mine, proj_other, jnp.stack(gain), tiles)
    embed = embed.astype(BF16)
    embed_other = swap(embed)
    embed = jnp.concatenate([jnp.where(s == 0, embed, embed_other), jnp.where(s == 0, embed_other, embed)])

    base = (s * fsdp + f) * tiles
    valid = (base + jnp.arange(tiles, dtype=jnp.int32) < count).astype(F32)
    grads = [c * valid[:, None] / per_tile * g for c, g in zip(halves(embed_cot[0].astype(F32)), gain)]
    mixed_mine, mixed_other, term_mine, term_other, zero = backward(tokens, normed_mine, normed_other, inv_std, grads)

    w_embed, w_out = by_y(after(at, zero), others, 2 * rows, rows)
    w_embed, w_out = w_embed.reshape(dt, quarter), w_out.reshape(ds, quarter)
    w_out_other = swap(w_out)
    hidden = dot(embed, w_embed).astype(BF16)
    hidden = jnp.concatenate([hidden[:tiles], hidden[tiles:]], axis=1)
    second = a2a_z(copies(jnp.concatenate([hidden, w_heads]), NZ))
    w_heads = second[:, tiles:]

    parts = pair_sum(at, term_mine, swap(term_other))
    parts = [parts[0]] + [shift_y(parts[k], k) for k in range(1, NY)]
    parts = y_sum(at, parts)
    head_out_grad, zero = head_out_grad_of(at, mixed_mine, mixed_other, proj_mine, proj_other)
    hidden = a2a_y(copies(after(after(second[:, :tiles], parts[0]), zero), NY)).reshape(shard_len, ds)
    hidden_other = swap(hidden)
    parts = [parts[0]] + [shift_z(parts[k], k) for k in range(1, NZ)]
    share = sum(p.astype(F32) for p in parts).astype(BF16)
    w_heads_other = swap(after(w_heads, share))

    attended = attend(at, hidden, hidden_other, w_heads, w_heads_other, bias)
    received = [attended] + [shift_y(attended, k) for k in range(1, NY)]
    share = after(share, attended)
    share = sum(p.astype(F32) for p in [share] + [shift_x(share, k) for k in range(1, NX)]).astype(BF16)
    other = swap(share)
    slide_out = finish(at, received, w_out, w_out_other, hidden, hidden_other, tiles)
    slide_out = slide_out.reshape(1, shard_len, ds)
    proj_grad = jnp.concatenate([jnp.where(s == 0, share, other), jnp.where(s == 0, other, share)], axis=1)
    return (slide_out, head_out_grad[None], proj_grad)


def solution(mesh):
    return jax.shard_map(
        body,
        mesh=mesh,
        in_specs=(
            P("slide", ("seq", "fsdp"), None),
            P("fsdp", None),
            P(),
            P("slide", ("seq", "fsdp"), None),
            P("slide"),
            P(),
            P(),
            P("fsdp", None),
            P("fsdp", None),
            P("fsdp", None),
        ),
        out_specs=(P("slide", "seq", None), P("slide", ("seq", "fsdp"), None), P("fsdp", None)),
        check_vma=False,
    )
```

```python
import functools

import jax
import jax.numpy as jnp
from jax import lax
from jax.experimental import pallas as pl
from jax.experimental.pallas import tpu as pltpu
from jax.sharding import PartitionSpec as P

HS = 48
NX, NZ, NY = 4, 8, 4
Z_GROUPS = [[z * NY + y for z in range(NZ)] for y in range(NY)]
Y_GROUPS = [[z * NY + y for y in range(NY)] for z in range(NZ)]
SWAP = [(0, 1), (1, 0)]
F32, BF16 = jnp.float32, jnp.bfloat16
VMEM = pl.BlockSpec(memory_space=pltpu.VMEM)
SMEM = pl.BlockSpec(memory_space=pltpu.SMEM)
ANY = pl.BlockSpec(memory_space=pl.ANY)
CONTRACT_LAST = (((1,), (1,)), ((), ()))
CONTRACT_FIRST = (((0,), (0,)), ((), ()))
dot = functools.partial(jnp.dot, preferred_element_type=F32)
dot_general = functools.partial(lax.dot_general, preferred_element_type=F32)


def a2a_z(v):
    return lax.all_to_all(v, "fsdp", 0, 0, axis_index_groups=Z_GROUPS)


def a2a_y(v):
    return lax.all_to_all(v, "fsdp", 0, 0, axis_index_groups=Y_GROUPS)


def copies(v, n):
    return jnp.broadcast_to(v[None], (n,) + v.shape)


def swap(v):
    return lax.ppermute(v, "seq", SWAP)


def shift_y(v, k):
    return lax.ppermute(
        v, "fsdp", [(z * NY + y, z * NY + (y + k) % NY) for z in range(NZ) for y in range(NY)]
    )


def shift_z(v, k):
    return lax.ppermute(
        v, "fsdp", [(z * NY + y, (z + k) % NZ * NY + y) for z in range(NZ) for y in range(NY)]
    )


def shift_x(v, k):
    return lax.ppermute(v, "slide", [(x, (x + k) % NX) for x in range(NX)])


def after(v, other):
    return v + (other[(0,) * other.ndim].astype(F32) * 0).astype(v.dtype)


def params(mib):
    return pltpu.CompilerParams(vmem_limit_bytes=mib * 1024 * 1024)


def cost(gflop, mb, mexp=0):
    return pl.CostEstimate(
        flops=int(gflop * 1e9), bytes_accessed=int(mb * 1e6), transcendentals=int(mexp * 1e6)
    )


def forward_kernel(tiles, at_ref, tok_ref, pm_ref, po_ref, gain_ref, out_ref, nm_ref, no_ref, inv_ref):
    tok = tok_ref[...]
    mixed = [dot(tok, pm_ref[...]), dot(tok, po_ref[...])]
    rows, half = mixed[0].shape
    centre = sum(jnp.sum(m, axis=-1, keepdims=True) for m in mixed) * (0.5 / half)
    shifted = [m - centre for m in mixed]
    var = sum(jnp.sum(m * m, axis=-1, keepdims=True) for m in shifted) * (0.5 / half)
    inv_std = lax.rsqrt(var + 1e-06)
    inv_ref[...] = jnp.broadcast_to(inv_std, inv_ref.shape)
    pooled = []
    for i, (m, n_ref) in enumerate(zip(shifted, (nm_ref, no_ref))):
        n = m * inv_std
        n_ref[...] = n
        mean = jnp.sum(n.reshape(tiles, rows // tiles, half), axis=1) * (tiles / rows)
        pooled.append(mean * gain_ref[i : i + 1, :])
    span = pl.ds(pl.multiple_of(pl.program_id(0) * tiles, tiles), tiles)
    for s in range(2):

        @pl.when(at_ref[0] == s)
        def _():
            out_ref[span, :half] = pooled[s]
            out_ref[span, half:] = pooled[1 - s]


def forward(at, tokens, pm, po, gain, tiles):
    rows, aw = tokens.shape
    half = pm.shape[1]
    steps = 2
    spec = pl.BlockSpec((rows // steps, half), lambda i: (i, 0))
    return pl.pallas_call(
        functools.partial(forward_kernel, tiles // steps),
        out_shape=(
            jax.ShapeDtypeStruct((tiles, 2 * half), F32),
            jax.ShapeDtypeStruct((rows, half), F32),
            jax.ShapeDtypeStruct((rows, half), F32),
            jax.ShapeDtypeStruct((rows, 128), F32),
        ),
        grid=(steps,),
        in_specs=[SMEM, pl.BlockSpec((rows // steps, aw), lambda i: (i, 0)), VMEM, VMEM, VMEM],
        out_specs=(
            pl.BlockSpec((tiles, 2 * half), lambda i: (0, 0)),
            spec,
            spec,
            pl.BlockSpec((rows // steps, 128), lambda i: (i, 0)),
        ),
        compiler_params=params(48),
        cost_estimate=cost(2.4, 10),
        name="forward",
    )(at, tokens, pm, po, gain)


def backward_kernel(tok_ref, nm_ref, no_ref, inv_ref, gm_ref, go_ref, xm_ref, xo_ref, tm_ref, to_ref, done_ref, am_ref, ao_ref):
    step, steps = pl.program_id(0), pl.num_programs(0)
    tok = tok_ref[...]
    normed = [nm_ref[...], no_ref[...]]
    inv_std = inv_ref[:, :1]
    rows, half = normed[0].shape
    tiles = gm_ref.shape[1]
    grads = [gm_ref[0], go_ref[0]]
    mean = sum(jnp.sum(g, axis=-1, keepdims=True) for g in grads) * (0.5 / half)

    def per_token(v):
        return jnp.broadcast_to(v[:, None, :], (tiles, rows // tiles, v.shape[1])).reshape(rows, v.shape[1])

    along = sum(jnp.sum(per_token(g) * n, axis=-1, keepdims=True) for g, n in zip(grads, normed)) * (0.5 / half)
    mixed = [(inv_std * (per_token(g - mean) - n * along)).astype(BF16) for g, n in zip(grads, normed)]
    done_ref[...] = jnp.zeros_like(done_ref)
    xm_ref[...] = mixed[0]
    xo_ref[...] = mixed[1]
    for acc_ref, term_ref, m in ((am_ref, tm_ref, mixed[0]), (ao_ref, to_ref, mixed[1])):
        term = dot_general(tok, m, CONTRACT_FIRST)

        @pl.when(step == 0)
        def _():
            acc_ref[...] = term

        @pl.when(step > 0)
        def _():
            acc_ref[...] += term

        @pl.when(step == steps - 1)
        def _():
            block = term_ref.shape[2]
            for z in range(NZ):
                for y in range(NY):
                    term_ref[y, z] = acc_ref[pl.ds((z * NY + y) * block, block), :].astype(BF16)


def backward(tokens, nm, no, inv_std, grads):
    rows, aw = tokens.shape
    half = nm.shape[1]
    tiles = grads[0].shape[0]
    steps = 2
    grads = [g.reshape(steps, tiles // steps, half) for g in grads]
    gspec = pl.BlockSpec((1, tiles // steps, half), lambda i: (i, 0, 0))
    tspec = pl.BlockSpec((NY, NZ, aw // (NY * NZ), half), lambda i: (0, 0, 0, 0))
    term = jax.ShapeDtypeStruct((NY, NZ, aw // (NY * NZ), half), BF16)
    wide = pl.BlockSpec((rows // steps, half), lambda i: (i, 0))
    mixed = jax.ShapeDtypeStruct((rows, half), BF16)
    return pl.pallas_call(
        backward_kernel,
        out_shape=(mixed, mixed, term, term, jax.ShapeDtypeStruct((8, 128), F32)),
        grid=(steps,),
        in_specs=[
            pl.BlockSpec((rows // steps, aw), lambda i: (i, 0)),
            wide,
            wide,
            pl.BlockSpec((rows // steps, 128), lambda i: (i, 0)),
            gspec,
            gspec,
        ],
        out_specs=(wide, wide, tspec, tspec, pl.BlockSpec((8, 128), lambda i: (0, 0))),
        scratch_shapes=[pltpu.VMEM((aw, half), F32), pltpu.VMEM((aw, half), F32)],
        compiler_params=params(56),
        cost_estimate=cost(2.4, 16),
        name="backward",
    )(tokens, nm, no, inv_std, *grads)


def head_out_grad_kernel(at_ref, xm_ref, xo_ref, pm_ref, po_ref, out_ref, done_ref):
    done_ref[...] = jnp.zeros_like(done_ref)
    grad = dot_general(xm_ref[...], pm_ref[...], CONTRACT_LAST) + dot_general(xo_ref[...], po_ref[...], CONTRACT_LAST)
    out_ref[...] = grad.astype(BF16)


def head_out_grad_of(at, xm, xo, pm, po):
    rows, half = xm.shape
    aw = pm.shape[0]
    steps = 2
    spec = pl.BlockSpec((rows // steps, half), lambda i: (i, 0))
    return pl.pallas_call(
        head_out_grad_kernel,
        out_shape=(jax.ShapeDtypeStruct((rows, aw), BF16), jax.ShapeDtypeStruct((8, 128), F32)),
        grid=(steps,),
        in_specs=[SMEM, spec, spec, VMEM, VMEM],
        out_specs=(
            pl.BlockSpec((rows // steps, aw), lambda i: (i, 0)),
            pl.BlockSpec((8, 128), lambda i: (0, 0)),
        ),
        compiler_params=params(32),
        cost_estimate=cost(0.01, 0.1),
        name="head_out_grad",
    )(at, xm, xo, pm, po)


def pair_sum_kernel(at_ref, mine_ref, other_ref, *out_refs):
    for k, out_ref in enumerate(out_refs):
        y = lax.rem(at_ref[1] + k, NY)
        for z in range(NZ):
            out_ref[z] = (mine_ref[y, z].astype(F32) + other_ref[y, z].astype(F32)).astype(BF16)


def pair_sum(at, mine, other):
    return pl.pallas_call(
        pair_sum_kernel,
        out_shape=[jax.ShapeDtypeStruct(mine.shape[1:], BF16)] * NY,
        in_specs=[SMEM, VMEM, VMEM],
        out_specs=[VMEM] * NY,
        compiler_params=params(32),
        cost_estimate=cost(0.001, 0.1),
        name="pair_sum",
    )(at, mine, other)


def y_sum_kernel(at_ref, _, *refs):
    for k, out_ref in enumerate(refs[NY:]):
        z = lax.rem(at_ref[4] + k, NZ)
        out_ref[...] = sum(ref[z].astype(F32) for ref in refs[:NY]).astype(BF16)


def y_sum(at, before, parts):
    return pl.pallas_call(
        y_sum_kernel,
        out_shape=[jax.ShapeDtypeStruct(parts[0].shape[1:], BF16)] * NZ,
        in_specs=[SMEM, ANY] + [VMEM] * NY,
        out_specs=[VMEM] * NZ,
        compiler_params=params(32),
        cost_estimate=cost(0.001, 0.1),
        name="y_sum",
    )(at, before, *parts)


def sum_kernel(n, *refs):
    refs[-1][...] = sum(ref[...].astype(F32) for ref in refs[:n]).astype(BF16)


def sum_of(name, before, parts):
    return pl.pallas_call(
        functools.partial(sum_kernel, len(parts)),
        out_shape=jax.ShapeDtypeStruct(parts[0].shape, BF16),
        in_specs=[VMEM] * len(parts) + [ANY] * len(before),
        out_specs=VMEM,
        compiler_params=params(32),
        cost_estimate=cost(0.001, 0.1),
        name=name,
    )(*parts, *before)


def rest_kernel(skip, in_ref, *refs):
    for z in range(NZ):
        refs[-1][z] = in_ref[z, skip:, :]


def rest_of(gathered, skip, before):
    zs, rows, cols = gathered.shape
    return pl.pallas_call(
        functools.partial(rest_kernel, skip),
        out_shape=jax.ShapeDtypeStruct((zs, rows - skip, cols), BF16),
        in_specs=[VMEM] + [ANY] * len(before),
        out_specs=VMEM,
        compiler_params=params(32),
        cost_estimate=cost(5, 5),
        name="rest",
    )(gathered, *before)


def by_z_kernel(at_ref, *refs):
    for k, ref in enumerate(refs[:-1]):
        refs[-1][lax.rem(at_ref[4] + NZ - k, NZ)] = ref[...]


def by_z(at, pieces):
    return pl.pallas_call(
        by_z_kernel,
        out_shape=jax.ShapeDtypeStruct((NZ,) + pieces[0].shape, BF16),
        in_specs=[SMEM] + [VMEM] * NZ,
        out_specs=VMEM,
        compiler_params=params(32),
        cost_estimate=cost(0.001, 0.1),
        name="by_z",
    )(at, *pieces)


def arrange_kernel(at_ref, in_ref, *refs):
    proj_ref, heads_ref = refs[-2:]
    for y in range(NY):
        for z in range(NZ):
            proj_ref[z, y] = in_ref[y, z]
    for i in range(2):
        heads_ref[i] = in_ref[2 * at_ref[0] + i, NZ]


def arrange(at, gathered, before):
    block = gathered.shape[2:]
    return pl.pallas_call(
        arrange_kernel,
        out_shape=(jax.ShapeDtypeStruct((NZ, NY) + block, BF16), jax.ShapeDtypeStruct((2,) + block, BF16)),
        in_specs=[SMEM, VMEM] + [ANY] * len(before),
        out_specs=(VMEM, VMEM),
        compiler_params=params(32),
        cost_estimate=cost(0.001, 0.1),
        name="arrange",
    )(at, gathered, *before)


def by_y_kernel(cuts, at_ref, _, *refs):
    for k, ref in enumerate(refs[:NY]):
        y = lax.rem(at_ref[1] + NY - k, NY)
        for (start, stop), out_ref in zip(cuts, refs[NY:]):
            for z in range(NZ):
                out_ref[z, y] = ref[z, start:stop, :]


def by_y(at, before, pieces, *sizes):
    zs, _, cols = pieces[0].shape
    stops = [sum(sizes[: i + 1]) for i in range(len(sizes))]
    cuts = [(stop - size, stop) for stop, size in zip(stops, sizes)]
    return pl.pallas_call(
        functools.partial(by_y_kernel, cuts),
        out_shape=[jax.ShapeDtypeStruct((zs, NY, size, cols), BF16) for size in sizes],
        in_specs=[SMEM, ANY] + [VMEM] * NY,
        out_specs=[VMEM] * len(sizes),
        compiler_params=params(32),
        cost_estimate=cost(0.01, 1),
        name="by_y",
    )(at, before, *pieces)


def place(row, s):
    return s * 512 + ((row // 16) % NZ * NY + row // (16 * NZ)) * 16 + row % 16


def bias_kernel(heads, at_ref, seg_ref, dil_ref, out_ref, done_ref, q_ref, k_ref):
    s, y, count = at_ref[0], at_ref[1], at_ref[2]
    rows = q_ref.shape[1]

    def fill(ref, pos, valid):
        lane = lax.broadcasted_iota(jnp.int32, pos.shape, 1)
        hits, residues = [], []
        for c in range(seg_ref.shape[0]):
            width = seg_ref[c]
            bits = 6 + sum((width > 64 << b).astype(jnp.int32) for b in range(4))
            ids = lax.shift_right_logical(jnp.full_like(pos, 2 * rows), jnp.full_like(pos, bits))
            ids = ids + lax.shift_right_logical(pos, jnp.full_like(pos, bits))
            hits.append((ids == lane) & valid)
            residues.append(pos & (dil_ref[c] - 1))
        for h in range(heads):
            head = y * heads + h
            any_hit = None
            for c, (hit, residue) in enumerate(zip(hits, residues)):
                hit = hit & (residue == (head & (dil_ref[c] - 1)))
                any_hit = hit if any_hit is None else any_hit | hit
            ref[h] = jnp.where(any_hit, 1.0, 0.0).astype(BF16)

    @pl.when(pl.program_id(0) == 0)
    def _():
        row = lax.broadcasted_iota(jnp.int32, (rows, 128), 0)
        pos = place(row, s)
        fill(q_ref, pos, pos >= 0)
        row = lax.broadcasted_iota(jnp.int32, (2 * rows, 128), 0)
        pos = place(row % rows, row // rows)
        fill(k_ref, pos, pos < count)
        done_ref[...] = jnp.zeros_like(done_ref)

    h = pl.program_id(0)
    block = 128
    for start in range(0, rows, block):
        span = pl.ds(start, block)
        counted = dot_general(q_ref[h, span, :], k_ref[h], CONTRACT_LAST)
        bias = jnp.full(counted.shape, -1e30, F32)
        for n, log2 in enumerate((0.0, 1.0, 1.584962500721156, 2.0, 2.321928094887362)):
            bias = jnp.where(counted > n + 0.5, log2, bias)
        out_ref[0, span, :] = bias


def biases(at, seg_lengths, dilation, heads, rows):
    return pl.pallas_call(
        functools.partial(bias_kernel, heads),
        out_shape=(jax.ShapeDtypeStruct((heads, rows, 2 * rows), F32), jax.ShapeDtypeStruct((8, 128), F32)),
        grid=(heads,),
        in_specs=[SMEM] * 3,
        out_specs=(
            pl.BlockSpec((1, rows, 2 * rows), lambda h: (h, 0, 0)),
            pl.BlockSpec((8, 128), lambda h: (0, 0)),
        ),
        scratch_shapes=[pltpu.VMEM((heads, rows, 128), BF16), pltpu.VMEM((heads, 2 * rows, 128), BF16)],
        compiler_params=params(60),
        cost_estimate=cost(1, 1),
        name="biases",
    )(at, seg_lengths, dilation)


def attend_kernel(at_ref, hm_ref, ho_ref, wm_ref, wo_ref, bias_ref, *refs):
    out_ref, w_ref, q_ref, k_ref, v_ref = refs[-5:]
    s = at_ref[0]
    rows = hm_ref.shape[0]
    half = hm_ref.shape[1] // 2
    heads, block, keys = bias_ref.shape
    seg = q_ref.shape[2]

    @pl.when(pl.program_id(0) == 0)
    def _():
        for z in range(NZ):
            w_ref[z, s] = wm_ref[z]
            w_ref[z, 1 - s] = wo_ref[z]
        w_mine = w_ref[pl.ds(s * (NZ // 2), NZ // 2)].reshape(half, w_ref.shape[3])
        w_other = w_ref[pl.ds((1 - s) * (NZ // 2), NZ // 2)].reshape(half, w_ref.shape[3])
        for core in range(2):
            lanes = slice(core * half, (core + 1) * half)
            all_parts = dot(hm_ref[:, lanes], w_mine) + dot(ho_ref[:, lanes], w_other)
            span = pl.ds(core * rows, rows)
            q_ref[core] = all_parts[:, :seg].astype(BF16)
            k_ref[span, :] = all_parts[:, seg : 2 * seg].astype(BF16)
            v_ref[span, :] = all_parts[:, 2 * seg :].astype(BF16)

    lane_head = lax.broadcasted_iota(jnp.int32, (1, seg), 1) // HS
    scale = HS ** (-0.5) * 1.4426950408889634
    queries = q_ref[s, pl.ds(pl.multiple_of(pl.program_id(0) * block, block), block), :]
    queries = jnp.concatenate([jnp.where(lane_head == h, queries, 0).astype(BF16) for h in range(heads)])
    scores = dot_general(queries, k_ref[...], CONTRACT_LAST)
    scores = scores * scale + bias_ref[...].reshape(heads * block, keys)
    weights = jnp.exp2(scores - jnp.max(scores, axis=-1, keepdims=True))
    total = jnp.sum(weights, axis=-1, keepdims=True)
    part = dot(weights.astype(BF16), v_ref[...]) * (1.0 / total)
    for h in range(heads):
        turned = part[h * block : (h + 1) * block].T
        out_ref[h * HS : (h + 1) * HS, :] = turned[h * HS : (h + 1) * HS].astype(BF16)


def attend(at, hm, ho, wm, wo, bias, before):
    heads, rows, keys = bias.shape
    seg = wm.shape[2] // 3
    block = 128
    return pl.pallas_call(
        attend_kernel,
        out_shape=jax.ShapeDtypeStruct((heads * HS, rows), BF16),
        grid=(rows // block,),
        in_specs=[SMEM] + [VMEM] * 4 + [pl.BlockSpec((heads, block, keys), lambda i: (0, i, 0))] + [ANY] * len(before),
        out_specs=pl.BlockSpec((heads * HS, block), lambda i: (0, i)),
        scratch_shapes=[
            pltpu.VMEM((NZ, 2) + wm.shape[1:], BF16),
            pltpu.VMEM((2, rows, seg), BF16),
            pltpu.VMEM((keys, seg), BF16),
            pltpu.VMEM((keys, seg), BF16),
        ],
        compiler_params=params(48),
        cost_estimate=cost(8, 12, 2),
        name="attend",
    )(at, hm, ho, wm, wo, bias, *before)


def finish_kernel(at_ref, a0_ref, a1_ref, a2_ref, a3_ref, wm_ref, wo_ref, hm_ref, ho_ref, out_ref):
    s, y, count = at_ref[0], at_ref[1], at_ref[2]
    rows, half = hm_ref.shape[0], hm_ref.shape[1] // 2
    tiles = out_ref.shape[2]
    mine = other = 0.0
    for k, att_ref in enumerate((a0_ref, a1_ref, a2_ref, a3_ref)):
        depth = att_ref.shape[0]
        span = pl.ds(pl.multiple_of(lax.rem(y + NY - k, NY) * depth, depth), depth)
        mine = mine + dot_general(att_ref[...], wm_ref[span, :], CONTRACT_FIRST)
        other = other + dot_general(att_ref[...], wo_ref[span, :], CONTRACT_FIRST)
    lanes = pl.ds(pl.multiple_of(s * half, half), half)
    mine = mine + hm_ref[:, lanes].astype(F32)
    other = other + ho_ref[:, lanes].astype(F32)
    row = lax.broadcasted_iota(jnp.int32, (rows, half), 0)
    valid = place(row, s) < count
    left = jnp.where(valid, jnp.where(s == 0, mine, other), 0.0).astype(BF16)
    right = jnp.where(valid, jnp.where(s == 0, other, mine), 0.0).astype(BF16)
    span = NZ * tiles
    for y in range(NY):
        for part, lanes in ((left, slice(0, half)), (right, slice(half, 2 * half))):
            out_ref[:, y, :, lanes] = part[y * span : (y + 1) * span].reshape(NZ, tiles, half)


def finish(at, att, wm, wo, hm, ho, tiles):
    return pl.pallas_call(
        finish_kernel,
        out_shape=jax.ShapeDtypeStruct((NZ, NY, tiles, hm.shape[1]), BF16),
        in_specs=[SMEM] + [VMEM] * 8,
        out_specs=VMEM,
        compiler_params=params(32),
        cost_estimate=cost(0.6, 4),
        name="finish",
    )(at, *att, wm, wo, hm, ho)


def body(
    head_out,
    proj_weight,
    norm_gain,
    embed_cot,
    tile_counts,
    seg_lengths,
    dilation,
    embed_weight,
    qkv_weight,
    out_weight,
):
    tokens = head_out[0]
    n_rows, aw = tokens.shape
    dt = proj_weight.shape[1]
    half = dt // 2
    tiles = embed_cot.shape[1]
    per_tile = n_rows // tiles
    fsdp = NZ * NY
    f = lax.axis_index("fsdp")
    s = lax.axis_index("seq")
    y = f % NY
    count = tile_counts[0]
    ds = out_weight.shape[1]
    shard_len = fsdp * tiles
    x = lax.axis_index("slide")
    at = jnp.stack([s, y, count, x, f // NY]).astype(jnp.int32)
    dslice = lax.dynamic_slice_in_dim
    heads = ds // HS // NY
    width = heads * HS

    def of_y(v, k):
        return lax.dynamic_index_in_dim(v, (y + k) % NY, 0, keepdims=False)

    bias, zero = biases(at, seg_lengths, dilation, heads, shard_len)

    rows = proj_weight.shape[0]
    w_heads = qkv_weight.reshape(rows, 3, NY, width).transpose(2, 0, 1, 3)
    w_heads = jnp.pad(w_heads, ((0, 0), (0, 0), (0, 0), (0, 256 - width))).reshape(NY, rows, 3 * 256)

    quarter = ds // 2
    first = a2a_z(copies(dslice(proj_weight, s * half, half, 1), NZ))
    others = jnp.concatenate([dslice(w, s * quarter, quarter, 1) for w in (embed_weight, out_weight)])
    others = after(others, first)
    others = [others] + [shift_z(others, k) for k in range(1, NZ)]
    gathered = a2a_y(jnp.concatenate([copies(first, NY), after(w_heads, zero)[:, None]], axis=1))
    proj_mine, w_heads = arrange(at, gathered, others[1:])
    proj_mine, w_heads = proj_mine.reshape(aw, half), w_heads.reshape(2 * rows, half)
    proj_other = swap(proj_mine)
    others = by_z(at, others)
    others = [others] + [shift_y(others, k) for k in range(1, NY)]

    def halves(v):
        return dslice(v, s * half, half, v.ndim - 1), dslice(v, (1 - s) * half, half, v.ndim - 1)

    gain = halves(norm_gain)
    embed, normed_mine, normed_other, inv_std = forward(at, tokens, proj_mine, proj_other, jnp.stack(gain), tiles)
    embed = embed.astype(BF16)
    embed_other = swap(embed)
    embed = jnp.concatenate([jnp.where(s == 0, embed, embed_other), jnp.where(s == 0, embed_other, embed)])

    base = (s * fsdp + f) * tiles
    valid = (base + jnp.arange(tiles, dtype=jnp.int32) < count).astype(F32)
    grads = [c * valid[:, None] / per_tile * g for c, g in zip(halves(embed_cot[0].astype(F32)), gain)]
    mixed_mine, mixed_other, term_mine, term_other, zero = backward(tokens, normed_mine, normed_other, inv_std, grads)

    w_embed, w_out = by_y(at, zero, others, 2 * rows, rows)
    w_embed, w_out = w_embed.reshape(dt, quarter), w_out.reshape(ds, quarter)
    w_out_other = swap(w_out)
    hidden = dot(embed, w_embed).astype(BF16)
    hidden = jnp.concatenate([hidden[:tiles], hidden[tiles:]], axis=1)
    second = a2a_z(copies(jnp.concatenate([hidden, w_heads]), NZ))

    parts = pair_sum(at, term_mine, swap(term_other))
    parts = [parts[0]] + [shift_y(parts[k], k) for k in range(1, NY)]
    head_out_grad, zero = head_out_grad_of(at, mixed_mine, mixed_other, proj_mine, proj_other)
    parts = y_sum(at, zero, parts)
    hidden = a2a_y(copies(after(second[:, :tiles], parts[0]), NY)).reshape(shard_len, ds)
    hidden_other = swap(hidden)
    parts = [parts[0]] + [shift_z(parts[k], k) for k in range(1, NZ)]
    share = sum_of("z_sum", [], parts)
    w_heads = rest_of(second, tiles, [share])
    w_heads_other = swap(w_heads)

    attended = attend(at, hidden, hidden_other, w_heads, w_heads_other, bias, [])
    received = [attended] + [shift_y(attended, k) for k in range(1, NY)]
    share = sum_of("hold", received[1:], [share])
    parts = [share] + [shift_x(share, k) for k in range(1, NX)]
    slide_out = finish(at, received, w_out, w_out_other, hidden, hidden_other, tiles)
    share = sum_of("x_sum", [slide_out], parts)
    other = swap(share)
    slide_out = slide_out.reshape(1, shard_len, ds)
    proj_grad = jnp.concatenate([jnp.where(s == 0, share, other), jnp.where(s == 0, other, share)], axis=1)
    return (slide_out, head_out_grad[None], proj_grad)


def solution(mesh):
    return jax.shard_map(
        body,
        mesh=mesh,
        in_specs=(
            P("slide", ("seq", "fsdp"), None),
            P("fsdp", None),
            P(),
            P("slide", ("seq", "fsdp"), None),
            P("slide"),
            P(),
            P(),
            P("fsdp", None),
            P("fsdp", None),
            P("fsdp", None),
        ),
        out_specs=(P("slide", "seq", None), P("slide", ("seq", "fsdp"), None), P("fsdp", None)),
        check_vma=False,
    )
```

```python
import functools

import jax
import jax.numpy as jnp
from jax import lax
from jax.experimental import pallas as pl
from jax.experimental.pallas import tpu as pltpu
from jax.sharding import PartitionSpec as P

HS = 48
NX, NZ, NY = 4, 8, 4
Z_GROUPS = [[z * NY + y for z in range(NZ)] for y in range(NY)]
Y_GROUPS = [[z * NY + y for y in range(NY)] for z in range(NZ)]
SWAP = [(0, 1), (1, 0)]
F32, BF16 = jnp.float32, jnp.bfloat16
VMEM = pl.BlockSpec(memory_space=pltpu.VMEM)
SMEM = pl.BlockSpec(memory_space=pltpu.SMEM)
ANY = pl.BlockSpec(memory_space=pl.ANY)
CONTRACT_LAST = (((1,), (1,)), ((), ()))
CONTRACT_FIRST = (((0,), (0,)), ((), ()))
dot = functools.partial(jnp.dot, preferred_element_type=F32)
dot_general = functools.partial(lax.dot_general, preferred_element_type=F32)


def a2a_z(v):
    return lax.all_to_all(v, "fsdp", 0, 0, axis_index_groups=Z_GROUPS)


def a2a_y(v):
    return lax.all_to_all(v, "fsdp", 0, 0, axis_index_groups=Y_GROUPS)


def copies(v, n):
    return jnp.broadcast_to(v[None], (n,) + v.shape)


def swap(v):
    return lax.ppermute(v, "seq", SWAP)


def shift_y(v, k):
    return lax.ppermute(
        v, "fsdp", [(z * NY + y, z * NY + (y + k) % NY) for z in range(NZ) for y in range(NY)]
    )


def shift_z(v, k):
    return lax.ppermute(
        v, "fsdp", [(z * NY + y, (z + k) % NZ * NY + y) for z in range(NZ) for y in range(NY)]
    )


def shift_x(v, k):
    return lax.ppermute(v, "slide", [(x, (x + k) % NX) for x in range(NX)])


def after(v, other):
    return v + (other[(0,) * other.ndim].astype(F32) * 0).astype(v.dtype)


def params(mib):
    return pltpu.CompilerParams(vmem_limit_bytes=mib * 1024 * 1024)


def cost(gflop, mb, mexp=0):
    return pl.CostEstimate(
        flops=int(gflop * 1e9), bytes_accessed=int(mb * 1e6), transcendentals=int(mexp * 1e6)
    )


def forward_kernel(tiles, at_ref, tok_ref, pm_ref, po_ref, gain_ref, out_ref, nm_ref, no_ref, inv_ref):
    tok = tok_ref[...]
    mixed = [dot(tok, pm_ref[...]), dot(tok, po_ref[...])]
    rows, half = mixed[0].shape
    centre = sum(jnp.sum(m, axis=-1, keepdims=True) for m in mixed) * (0.5 / half)
    shifted = [m - centre for m in mixed]
    var = sum(jnp.sum(m * m, axis=-1, keepdims=True) for m in shifted) * (0.5 / half)
    inv_std = lax.rsqrt(var + 1e-06)
    inv_ref[...] = jnp.broadcast_to(inv_std, inv_ref.shape)
    pooled = []
    for i, (m, n_ref) in enumerate(zip(shifted, (nm_ref, no_ref))):
        n = m * inv_std
        n_ref[...] = n
        mean = jnp.sum(n.reshape(tiles, rows // tiles, half), axis=1) * (tiles / rows)
        pooled.append(mean * gain_ref[i : i + 1, :])
    span = pl.ds(pl.multiple_of(pl.program_id(0) * tiles, tiles), tiles)
    for s in range(2):

        @pl.when(at_ref[0] == s)
        def _():
            out_ref[span, :half] = pooled[s]
            out_ref[span, half:] = pooled[1 - s]


def forward(at, tokens, pm, po, gain, tiles):
    rows, aw = tokens.shape
    half = pm.shape[1]
    steps = 2
    spec = pl.BlockSpec((rows // steps, half), lambda i: (i, 0))
    return pl.pallas_call(
        functools.partial(forward_kernel, tiles // steps),
        out_shape=(
            jax.ShapeDtypeStruct((tiles, 2 * half), F32),
            jax.ShapeDtypeStruct((rows, half), F32),
            jax.ShapeDtypeStruct((rows, half), F32),
            jax.ShapeDtypeStruct((rows, 128), F32),
        ),
        grid=(steps,),
        in_specs=[SMEM, pl.BlockSpec((rows // steps, aw), lambda i: (i, 0)), VMEM, VMEM, VMEM],
        out_specs=(
            pl.BlockSpec((tiles, 2 * half), lambda i: (0, 0)),
            spec,
            spec,
            pl.BlockSpec((rows // steps, 128), lambda i: (i, 0)),
        ),
        compiler_params=params(32),
        cost_estimate=cost(2.4, 10),
        name="forward",
    )(at, tokens, pm, po, gain)


def backward_kernel(_, tok_ref, nm_ref, no_ref, inv_ref, gm_ref, go_ref, xm_ref, xo_ref, tm_ref, to_ref, am_ref, ao_ref):
    step, steps = pl.program_id(0), pl.num_programs(0)
    tok = tok_ref[...]
    normed = [nm_ref[...], no_ref[...]]
    inv_std = inv_ref[:, :1]
    rows, half = normed[0].shape
    tiles = gm_ref.shape[1]
    grads = [gm_ref[0], go_ref[0]]
    mean = sum(jnp.sum(g, axis=-1, keepdims=True) for g in grads) * (0.5 / half)

    def per_token(v):
        return jnp.broadcast_to(v[:, None, :], (tiles, rows // tiles, v.shape[1])).reshape(rows, v.shape[1])

    along = sum(jnp.sum(per_token(g) * n, axis=-1, keepdims=True) for g, n in zip(grads, normed)) * (0.5 / half)
    mixed = [(inv_std * (per_token(g - mean) - n * along)).astype(BF16) for g, n in zip(grads, normed)]
    xm_ref[...] = mixed[0]
    xo_ref[...] = mixed[1]
    for acc_ref, term_ref, m in ((am_ref, tm_ref, mixed[0]), (ao_ref, to_ref, mixed[1])):
        term = dot_general(tok, m, CONTRACT_FIRST)

        @pl.when(step == 0)
        def _():
            acc_ref[...] = term

        @pl.when(step > 0)
        def _():
            acc_ref[...] += term

        @pl.when(step == steps - 1)
        def _():
            block = term_ref.shape[2]
            for z in range(NZ):
                for y in range(NY):
                    term_ref[y, z] = acc_ref[pl.ds((z * NY + y) * block, block), :].astype(BF16)


def backward(before, tokens, nm, no, inv_std, grads):
    rows, aw = tokens.shape
    half = nm.shape[1]
    tiles = grads[0].shape[0]
    steps = 2
    grads = [g.reshape(steps, tiles // steps, half) for g in grads]
    gspec = pl.BlockSpec((1, tiles // steps, half), lambda i: (i, 0, 0))
    tspec = pl.BlockSpec((NY, NZ, aw // (NY * NZ), half), lambda i: (0, 0, 0, 0))
    term = jax.ShapeDtypeStruct((NY, NZ, aw // (NY * NZ), half), BF16)
    wide = pl.BlockSpec((rows // steps, half), lambda i: (i, 0))
    mixed = jax.ShapeDtypeStruct((rows, half), BF16)
    return pl.pallas_call(
        backward_kernel,
        out_shape=(mixed, mixed, term, term),
        grid=(steps,),
        in_specs=[
            ANY,
            pl.BlockSpec((rows // steps, aw), lambda i: (i, 0)),
            wide,
            wide,
            pl.BlockSpec((rows // steps, 128), lambda i: (i, 0)),
            gspec,
            gspec,
        ],
        out_specs=(wide, wide, tspec, tspec),
        scratch_shapes=[pltpu.VMEM((aw, half), F32), pltpu.VMEM((aw, half), F32)],
        compiler_params=params(40),
        cost_estimate=cost(2.4, 16),
        name="backward",
    )(before, tokens, nm, no, inv_std, *grads)


def head_out_grad_kernel(at_ref, xm_ref, xo_ref, pm_ref, po_ref, out_ref, done_ref):
    done_ref[...] = jnp.zeros_like(done_ref)
    grad = dot_general(xm_ref[...], pm_ref[...], CONTRACT_LAST) + dot_general(xo_ref[...], po_ref[...], CONTRACT_LAST)
    out_ref[...] = grad.astype(BF16)


def head_out_grad_of(at, xm, xo, pm, po):
    rows, half = xm.shape
    aw = pm.shape[0]
    steps = 2
    spec = pl.BlockSpec((rows // steps, half), lambda i: (i, 0))
    return pl.pallas_call(
        head_out_grad_kernel,
        out_shape=(jax.ShapeDtypeStruct((rows, aw), BF16), jax.ShapeDtypeStruct((8, 128), F32)),
        grid=(steps,),
        in_specs=[SMEM, spec, spec, VMEM, VMEM],
        out_specs=(
            pl.BlockSpec((rows // steps, aw), lambda i: (i, 0)),
            pl.BlockSpec((8, 128), lambda i: (0, 0)),
        ),
        compiler_params=params(32),
        cost_estimate=cost(0.01, 0.1),
        name="head_out_grad",
    )(at, xm, xo, pm, po)


def pair_sum_kernel(at_ref, mine_ref, other_ref, *out_refs):
    for k, out_ref in enumerate(out_refs):
        y = lax.rem(at_ref[1] + k, NY)
        for z in range(NZ):
            out_ref[z] = (mine_ref[y, z].astype(F32) + other_ref[y, z].astype(F32)).astype(BF16)


def pair_sum(at, mine, other):
    return pl.pallas_call(
        pair_sum_kernel,
        out_shape=[jax.ShapeDtypeStruct(mine.shape[1:], BF16)] * NY,
        in_specs=[SMEM, VMEM, VMEM],
        out_specs=[VMEM] * NY,
        compiler_params=params(32),
        cost_estimate=cost(0.001, 0.1),
        name="pair_sum",
    )(at, mine, other)


def sum_kernel(n, *refs):
    if refs[0].shape == refs[-1].shape:
        parts = [ref[...] for ref in refs[:n]]
    else:
        parts = [refs[0][z] for z in range(refs[0].shape[0])]
    refs[-1][...] = sum(part.astype(F32) for part in parts).astype(BF16)


def sum_of(name, before, parts, gflop=0.001):
    if isinstance(parts, jax.Array):
        parts = [parts]
        shape = parts[0].shape[1:]
    else:
        shape = parts[0].shape
    return pl.pallas_call(
        functools.partial(sum_kernel, len(parts)),
        out_shape=jax.ShapeDtypeStruct(shape, BF16),
        in_specs=[VMEM] * len(parts) + [ANY] * len(before),
        out_specs=VMEM,
        compiler_params=params(32),
        cost_estimate=cost(gflop, 0.1),
        name=name,
    )(*parts, *before)


def by_z_kernel(at_ref, *refs):
    for k, ref in enumerate(refs[:-1]):
        refs[-1][lax.rem(at_ref[4] + NZ - k, NZ)] = ref[...]


def by_z(at, pieces):
    return pl.pallas_call(
        by_z_kernel,
        out_shape=jax.ShapeDtypeStruct((NZ,) + pieces[0].shape, BF16),
        in_specs=[SMEM] + [VMEM] * NZ,
        out_specs=VMEM,
        compiler_params=params(32),
        cost_estimate=cost(0.001, 0.1),
        name="by_z",
    )(at, *pieces)


def arrange_kernel(at_ref, in_ref, *refs):
    proj_ref, heads_ref = refs[-2:]
    for y in range(NY):
        for z in range(NZ):
            proj_ref[z, y] = in_ref[y, z]
    for i in range(2):
        heads_ref[i] = in_ref[2 * at_ref[0] + i, NZ]


def arrange(at, gathered, before):
    block = gathered.shape[2:]
    return pl.pallas_call(
        arrange_kernel,
        out_shape=(jax.ShapeDtypeStruct((NZ, NY) + block, BF16), jax.ShapeDtypeStruct((2,) + block, BF16)),
        in_specs=[SMEM, VMEM] + [ANY] * len(before),
        out_specs=(VMEM, VMEM),
        compiler_params=params(32),
        cost_estimate=cost(0.001, 0.1),
        name="arrange",
    )(at, gathered, *before)


def by_y_kernel(cuts, at_ref, *refs):
    for k, ref in enumerate(refs[:NY]):
        y = lax.rem(at_ref[1] + NY - k, NY)
        for (start, stop), out_ref in zip(cuts, refs[NY:]):
            for z in range(NZ):
                out_ref[z, y] = ref[z, start:stop, :]


def by_y(at, pieces, *sizes):
    zs, _, cols = pieces[0].shape
    stops = [sum(sizes[: i + 1]) for i in range(len(sizes))]
    cuts = [(stop - size, stop) for stop, size in zip(stops, sizes)]
    return pl.pallas_call(
        functools.partial(by_y_kernel, cuts),
        out_shape=[jax.ShapeDtypeStruct((zs, NY, size, cols), BF16) for size in sizes],
        in_specs=[SMEM] + [VMEM] * NY,
        out_specs=[VMEM] * len(sizes),
        compiler_params=params(32),
        cost_estimate=cost(0.01, 1),
        name="by_y",
    )(at, *pieces)


def place(row, s):
    return s * 512 + ((row // 16) % NZ * NY + row // (16 * NZ)) * 16 + row % 16


def bias_kernel(heads, at_ref, seg_ref, dil_ref, out_ref, done_ref, q_ref, k_ref):
    s, y, count = at_ref[0], at_ref[1], at_ref[2]
    rows = q_ref.shape[0]
    span = 128 // heads

    def fill(ref, pos, valid):
        lane = lax.broadcasted_iota(jnp.int32, pos.shape, 1)
        column, head = lane & (span - 1), y * heads + lax.shift_right_logical(lane, jnp.full_like(lane, 5))
        hits = None
        for c in range(seg_ref.shape[0]):
            width = seg_ref[c]
            bits = 6 + sum((width > 64 << b).astype(jnp.int32) for b in range(4))
            first = lax.shift_right_logical(jnp.int32(2 * rows), bits)
            ids = first + lax.shift_right_logical(pos, jnp.full_like(pos, bits))
            hit = (ids == column) & (((pos ^ head) & (dil_ref[c] - 1)) == 0)
            hits = hit if hits is None else hits | hit
        ref[...] = jnp.where(hits & valid, 1.0, 0.0).astype(BF16)

    h = pl.program_id(0)

    @pl.when(h == 0)
    def _():
        row = lax.broadcasted_iota(jnp.int32, (rows, 128), 0)
        pos = place(row, s)
        fill(q_ref, pos, pos >= 0)
        row = lax.broadcasted_iota(jnp.int32, (2 * rows, 128), 0)
        pos = place(row % rows, row // rows)
        fill(k_ref, pos, pos < count)
        done_ref[...] = jnp.zeros_like(done_ref)

    block = 128
    of_head = lax.broadcasted_iota(jnp.int32, (1, 128), 1) // span == h
    for start in range(0, rows, block):
        span_rows = pl.ds(start, block)
        queries = jnp.where(of_head, q_ref[span_rows, :], 0).astype(BF16)
        counted = dot_general(queries, k_ref[...], CONTRACT_LAST)
        out_ref[0, span_rows, :] = jnp.where(counted > 0.5, jnp.log2(jnp.maximum(counted, 1.0)), -1e30)


def biases(at, seg_lengths, dilation, heads, rows):
    return pl.pallas_call(
        functools.partial(bias_kernel, heads),
        out_shape=(jax.ShapeDtypeStruct((heads, rows, 2 * rows), F32), jax.ShapeDtypeStruct((8, 128), F32)),
        grid=(heads,),
        in_specs=[SMEM] * 3,
        out_specs=(
            pl.BlockSpec((1, rows, 2 * rows), lambda h: (h, 0, 0)),
            pl.BlockSpec((8, 128), lambda h: (0, 0)),
        ),
        scratch_shapes=[pltpu.VMEM((rows, 128), BF16), pltpu.VMEM((2 * rows, 128), BF16)],
        compiler_params=params(60),
        cost_estimate=cost(1, 1),
        name="biases",
    )(at, seg_lengths, dilation)


def spread_kernel(common_ref, own_ref, _, out_ref):
    blocks = common_ref.shape[0]
    for y in range(NY):
        out_ref[y, :blocks] = common_ref[...]
        out_ref[y, blocks] = own_ref[y]


def spread(common, own, before):
    return pl.pallas_call(
        spread_kernel,
        out_shape=jax.ShapeDtypeStruct((NY, common.shape[0] + 1) + common.shape[1:], BF16),
        in_specs=[VMEM, VMEM, ANY],
        out_specs=VMEM,
        compiler_params=params(32),
        cost_estimate=cost(0.001, 0.1),
        name="spread",
    )(common, own, before)


def attend_kernel(at_ref, hm_ref, ho_ref, wm_ref, wo_ref, bias_ref, *refs):
    out_ref, w_ref, q_ref, k_ref, v_ref = refs[-5:]
    s = at_ref[0]
    rows = hm_ref.shape[0]
    half = hm_ref.shape[1] // 2
    heads, block, keys = bias_ref.shape
    seg = q_ref.shape[2]

    @pl.when(pl.program_id(0) == 0)
    def _():
        for z in range(NZ):
            w_ref[z, s] = wm_ref[z]
            w_ref[z, 1 - s] = wo_ref[z]
        w_mine = w_ref[pl.ds(s * (NZ // 2), NZ // 2)].reshape(half, w_ref.shape[3])
        w_other = w_ref[pl.ds((1 - s) * (NZ // 2), NZ // 2)].reshape(half, w_ref.shape[3])
        for core in range(2):
            lanes = slice(core * half, (core + 1) * half)
            all_parts = dot(hm_ref[:, lanes], w_mine) + dot(ho_ref[:, lanes], w_other)
            span = pl.ds(core * rows, rows)
            q_ref[core] = all_parts[:, :seg].astype(BF16)
            k_ref[span, :] = all_parts[:, seg : 2 * seg].astype(BF16)
            v_ref[span, :] = all_parts[:, 2 * seg :].astype(BF16)

    lane_head = lax.broadcasted_iota(jnp.int32, (1, seg), 1) // HS
    scale = HS ** (-0.5) * 1.4426950408889634
    queries = q_ref[s, pl.ds(pl.multiple_of(pl.program_id(0) * block, block), block), :]
    queries = jnp.concatenate([jnp.where(lane_head == h, queries, 0).astype(BF16) for h in range(heads)])
    scores = dot_general(queries, k_ref[...], CONTRACT_LAST)
    scores = scores * scale + bias_ref[...].reshape(heads * block, keys)
    weights = jnp.exp2(scores - jnp.max(scores, axis=-1, keepdims=True))
    total = jnp.sum(weights, axis=-1, keepdims=True)
    part = dot(weights.astype(BF16), v_ref[...]) * (1.0 / total)
    for h in range(heads):
        turned = part[h * block : (h + 1) * block].T
        out_ref[h * HS : (h + 1) * HS, :] = turned[h * HS : (h + 1) * HS].astype(BF16)


def attend(at, hm, ho, wm, wo, bias, before):
    heads, rows, keys = bias.shape
    seg = wm.shape[2] // 3
    block = 128
    return pl.pallas_call(
        attend_kernel,
        out_shape=jax.ShapeDtypeStruct((heads * HS, rows), BF16),
        grid=(rows // block,),
        in_specs=[SMEM] + [VMEM] * 4 + [pl.BlockSpec((heads, block, keys), lambda i: (0, i, 0))] + [ANY] * len(before),
        out_specs=pl.BlockSpec((heads * HS, block), lambda i: (0, i)),
        scratch_shapes=[
            pltpu.VMEM((NZ, 2) + wm.shape[1:], BF16),
            pltpu.VMEM((2, rows, seg), BF16),
            pltpu.VMEM((keys, seg), BF16),
            pltpu.VMEM((keys, seg), BF16),
        ],
        compiler_params=params(48),
        cost_estimate=cost(8, 12, 2),
        name="attend",
    )(at, hm, ho, wm, wo, bias, *before)


def finish_kernel(at_ref, a0_ref, a1_ref, a2_ref, a3_ref, wm_ref, wo_ref, hm_ref, ho_ref, out_ref):
    s, y, count = at_ref[0], at_ref[1], at_ref[2]
    rows, half = hm_ref.shape[0], hm_ref.shape[1] // 2
    tiles = out_ref.shape[2]
    mine = other = 0.0
    for k, att_ref in enumerate((a0_ref, a1_ref, a2_ref, a3_ref)):
        depth = att_ref.shape[0]
        span = pl.ds(pl.multiple_of(lax.rem(y + NY - k, NY) * depth, depth), depth)
        mine = mine + dot_general(att_ref[...], wm_ref[span, :], CONTRACT_FIRST)
        other = other + dot_general(att_ref[...], wo_ref[span, :], CONTRACT_FIRST)
    lanes = pl.ds(pl.multiple_of(s * half, half), half)
    mine = mine + hm_ref[:, lanes].astype(F32)
    other = other + ho_ref[:, lanes].astype(F32)
    row = lax.broadcasted_iota(jnp.int32, (rows, half), 0)
    valid = place(row, s) < count
    left = jnp.where(valid, jnp.where(s == 0, mine, other), 0.0).astype(BF16)
    right = jnp.where(valid, jnp.where(s == 0, other, mine), 0.0).astype(BF16)
    span = NZ * tiles
    for y in range(NY):
        for part, lanes in ((left, slice(0, half)), (right, slice(half, 2 * half))):
            out_ref[:, y, :, lanes] = part[y * span : (y + 1) * span].reshape(NZ, tiles, half)


def finish(at, att, wm, wo, hm, ho, tiles):
    return pl.pallas_call(
        finish_kernel,
        out_shape=jax.ShapeDtypeStruct((NZ, NY, tiles, hm.shape[1]), BF16),
        in_specs=[SMEM] + [VMEM] * 8,
        out_specs=VMEM,
        compiler_params=params(32),
        cost_estimate=cost(0.6, 4),
        name="finish",
    )(at, *att, wm, wo, hm, ho)


def body(
    head_out,
    proj_weight,
    norm_gain,
    embed_cot,
    tile_counts,
    seg_lengths,
    dilation,
    embed_weight,
    qkv_weight,
    out_weight,
):
    tokens = head_out[0]
    n_rows, aw = tokens.shape
    dt = proj_weight.shape[1]
    half = dt // 2
    tiles = embed_cot.shape[1]
    per_tile = n_rows // tiles
    fsdp = NZ * NY
    f = lax.axis_index("fsdp")
    s = lax.axis_index("seq")
    y = f % NY
    count = tile_counts[0]
    ds = out_weight.shape[1]
    shard_len = fsdp * tiles
    x = lax.axis_index("slide")
    at = jnp.stack([s, y, count, x, f // NY]).astype(jnp.int32)
    dslice = lax.dynamic_slice_in_dim
    heads = ds // HS // NY
    width = heads * HS

    def of_y(v, k):
        return lax.dynamic_index_in_dim(v, (y + k) % NY, 0, keepdims=False)

    bias, zero = biases(at, seg_lengths, dilation, heads, shard_len)

    rows = proj_weight.shape[0]
    w_heads = qkv_weight.reshape(rows, 3, NY, width).transpose(2, 0, 1, 3)
    w_heads = jnp.pad(w_heads, ((0, 0), (0, 0), (0, 0), (0, 256 - width))).reshape(NY, rows, 3 * 256)

    quarter = ds // 2
    first = a2a_z(copies(dslice(proj_weight, s * half, half, 1), NZ))
    others = jnp.concatenate([dslice(w, s * quarter, quarter, 1) for w in (embed_weight, out_weight)])
    others = after(others, first)
    others = [others] + [shift_z(others, k) for k in range(1, NZ)]
    gathered = a2a_y(spread(first, w_heads, zero))
    proj_mine, w_heads = arrange(at, gathered, others[1:])
    proj_mine, w_heads = proj_mine.reshape(aw, half), w_heads.reshape(2 * rows, half)
    proj_other = swap(proj_mine)
    others = by_z(at, others)
    others = [others] + [shift_y(others, k) for k in range(1, NY)]

    def halves(v):
        return dslice(v, s * half, half, v.ndim - 1), dslice(v, (1 - s) * half, half, v.ndim - 1)

    gain = halves(norm_gain)
    embed, normed_mine, normed_other, inv_std = forward(at, tokens, proj_mine, proj_other, jnp.stack(gain), tiles)
    embed = embed.astype(BF16)
    embed_other = swap(embed)
    embed = jnp.concatenate([jnp.where(s == 0, embed, embed_other), jnp.where(s == 0, embed_other, embed)])

    base = (s * fsdp + f) * tiles
    valid = (base + jnp.arange(tiles, dtype=jnp.int32) < count).astype(F32)
    grads = [c * valid[:, None] / per_tile * g for c, g in zip(halves(embed_cot[0].astype(F32)), gain)]

    w_embed, w_out = by_y(at, others, 2 * rows, rows)
    w_embed, w_out = w_embed.reshape(dt, quarter), w_out.reshape(ds, quarter)
    w_out_other = swap(w_out)
    hidden = dot(embed, w_embed).astype(BF16)
    hidden = jnp.concatenate([hidden[:tiles], hidden[tiles:]], axis=1)
    mixed_mine, mixed_other, term_mine, term_other = backward(
        hidden, tokens, normed_mine, normed_other, inv_std, grads
    )
    second = a2a_z(copies(jnp.concatenate([hidden, w_heads]), NZ))

    parts = pair_sum(at, term_mine, swap(term_other))
    hidden = a2a_y(copies(after(second[:, :tiles], parts[0]), NY)).reshape(shard_len, ds)
    hidden_other = swap(hidden)
    head_out_grad, zero = head_out_grad_of(at, mixed_mine, mixed_other, proj_mine, proj_other)
    parts = [parts[0]] + [shift_y(parts[k], k) for k in range(1, NY)]
    share = a2a_z(sum_of("y_sum", [zero, hidden], parts, 6))

    w_heads = second[:, tiles:]
    w_heads_other = swap(w_heads)
    attended = attend(at, hidden, hidden_other, w_heads, w_heads_other, bias, [])
    received = [attended] + [shift_y(attended, k) for k in range(1, NY)]
    share = sum_of("z_sum", [attended], share)
    parts = [share] + [shift_x(share, k) for k in range(1, NX)]
    slide_out = finish(at, received, w_out, w_out_other, hidden, hidden_other, tiles)
    share = sum_of("x_sum", [slide_out], parts)
    other = swap(share)
    slide_out = slide_out.reshape(1, shard_len, ds)
    proj_grad = jnp.concatenate([jnp.where(s == 0, share, other), jnp.where(s == 0, other, share)], axis=1)
    return (slide_out, head_out_grad[None], proj_grad)


def solution(mesh):
    return jax.shard_map(
        body,
        mesh=mesh,
        in_specs=(
            P("slide", ("seq", "fsdp"), None),
            P("fsdp", None),
            P(),
            P("slide", ("seq", "fsdp"), None),
            P("slide"),
            P(),
            P(),
            P("fsdp", None),
            P("fsdp", None),
            P("fsdp", None),
        ),
        out_specs=(P("slide", "seq", None), P("slide", ("seq", "fsdp"), None), P("fsdp", None)),
        check_vma=False,
    )
```

```python
import functools

import jax
import jax.numpy as jnp
from jax import lax
from jax.experimental import pallas as pl
from jax.experimental.pallas import tpu as pltpu
from jax.sharding import PartitionSpec as P

HS = 48
NX, NZ, NY = 4, 8, 4
Z_GROUPS = [[z * NY + y for z in range(NZ)] for y in range(NY)]
Y_GROUPS = [[z * NY + y for y in range(NY)] for z in range(NZ)]
SWAP = [(0, 1), (1, 0)]
F32, BF16 = jnp.float32, jnp.bfloat16
VMEM = pl.BlockSpec(memory_space=pltpu.VMEM)
SMEM = pl.BlockSpec(memory_space=pltpu.SMEM)
ANY = pl.BlockSpec(memory_space=pl.ANY)
CONTRACT_LAST = (((1,), (1,)), ((), ()))
CONTRACT_FIRST = (((0,), (0,)), ((), ()))
dot = functools.partial(jnp.dot, preferred_element_type=F32)
dot_general = functools.partial(lax.dot_general, preferred_element_type=F32)


def a2a_z(v):
    return lax.all_to_all(v, "fsdp", 0, 0, axis_index_groups=Z_GROUPS)


def a2a_y(v):
    return lax.all_to_all(v, "fsdp", 0, 0, axis_index_groups=Y_GROUPS)


def copies(v, n):
    return jnp.broadcast_to(v[None], (n,) + v.shape)


def swap(v):
    return lax.ppermute(v, "seq", SWAP)


def shift_y(v, k):
    return lax.ppermute(
        v, "fsdp", [(z * NY + y, z * NY + (y + k) % NY) for z in range(NZ) for y in range(NY)]
    )


def shift_z(v, k):
    return lax.ppermute(
        v, "fsdp", [(z * NY + y, (z + k) % NZ * NY + y) for z in range(NZ) for y in range(NY)]
    )


def shift_x(v, k):
    return lax.ppermute(v, "slide", [(x, (x + k) % NX) for x in range(NX)])


def after(v, other):
    return v + (other[(0,) * other.ndim].astype(F32) * 0).astype(v.dtype)


def params(mib):
    return pltpu.CompilerParams(vmem_limit_bytes=mib * 1024 * 1024)


def cost(gflop, mb, mexp=0):
    return pl.CostEstimate(
        flops=int(gflop * 1e9), bytes_accessed=int(mb * 1e6), transcendentals=int(mexp * 1e6)
    )


def forward_kernel(tiles, at_ref, tok_ref, pm_ref, po_ref, gain_ref, out_ref, nm_ref, no_ref, inv_ref):
    tok = tok_ref[...]
    mixed = [dot(tok, pm_ref[...]), dot(tok, po_ref[...])]
    rows, half = mixed[0].shape
    centre = sum(jnp.sum(m, axis=-1, keepdims=True) for m in mixed) * (0.5 / half)
    shifted = [m - centre for m in mixed]
    var = sum(jnp.sum(m * m, axis=-1, keepdims=True) for m in shifted) * (0.5 / half)
    inv_std = lax.rsqrt(var + 1e-06)
    inv_ref[...] = jnp.broadcast_to(inv_std, inv_ref.shape)
    pooled = []
    for i, (m, n_ref) in enumerate(zip(shifted, (nm_ref, no_ref))):
        n = m * inv_std
        n_ref[...] = n
        mean = jnp.sum(n.reshape(tiles, rows // tiles, half), axis=1) * (tiles / rows)
        pooled.append(mean * gain_ref[i : i + 1, :])
    span = pl.ds(pl.multiple_of(pl.program_id(0) * tiles, tiles), tiles)
    for s in range(2):

        @pl.when(at_ref[0] == s)
        def _():
            out_ref[span, :half] = pooled[s]
            out_ref[span, half:] = pooled[1 - s]


def forward(at, tokens, pm, po, gain, tiles):
    rows, aw = tokens.shape
    half = pm.shape[1]
    steps = 2
    spec = pl.BlockSpec((rows // steps, half), lambda i: (i, 0))
    return pl.pallas_call(
        functools.partial(forward_kernel, tiles // steps),
        out_shape=(
            jax.ShapeDtypeStruct((tiles, 2 * half), F32),
            jax.ShapeDtypeStruct((rows, half), F32),
            jax.ShapeDtypeStruct((rows, half), F32),
            jax.ShapeDtypeStruct((rows, 128), F32),
        ),
        grid=(steps,),
        in_specs=[SMEM, pl.BlockSpec((rows // steps, aw), lambda i: (i, 0)), VMEM, VMEM, VMEM],
        out_specs=(
            pl.BlockSpec((tiles, 2 * half), lambda i: (0, 0)),
            spec,
            spec,
            pl.BlockSpec((rows // steps, 128), lambda i: (i, 0)),
        ),
        compiler_params=params(48),
        cost_estimate=cost(2.4, 10),
        name="forward",
    )(at, tokens, pm, po, gain)


def backward_kernel(_, tok_ref, nm_ref, no_ref, inv_ref, gm_ref, go_ref, xm_ref, xo_ref, tm_ref, to_ref, am_ref, ao_ref):
    step, steps = pl.program_id(0), pl.num_programs(0)
    tok = tok_ref[...]
    normed = [nm_ref[...], no_ref[...]]
    inv_std = inv_ref[:, :1]
    rows, half = normed[0].shape
    tiles = gm_ref.shape[1]
    grads = [gm_ref[0], go_ref[0]]
    mean = sum(jnp.sum(g, axis=-1, keepdims=True) for g in grads) * (0.5 / half)

    def per_token(v):
        return jnp.broadcast_to(v[:, None, :], (tiles, rows // tiles, v.shape[1])).reshape(rows, v.shape[1])

    along = sum(jnp.sum(per_token(g) * n, axis=-1, keepdims=True) for g, n in zip(grads, normed)) * (0.5 / half)
    mixed = [(inv_std * (per_token(g - mean) - n * along)).astype(BF16) for g, n in zip(grads, normed)]
    xm_ref[...] = mixed[0]
    xo_ref[...] = mixed[1]
    for acc_ref, term_ref, m in ((am_ref, tm_ref, mixed[0]), (ao_ref, to_ref, mixed[1])):
        term = dot_general(tok, m, CONTRACT_FIRST)

        @pl.when(step == 0)
        def _():
            acc_ref[...] = term

        @pl.when(step > 0)
        def _():
            acc_ref[...] += term

        @pl.when(step == steps - 1)
        def _():
            block = term_ref.shape[2]
            for z in range(NZ):
                for y in range(NY):
                    term_ref[y, z] = acc_ref[pl.ds((z * NY + y) * block, block), :].astype(BF16)


def backward(before, tokens, nm, no, inv_std, grads):
    rows, aw = tokens.shape
    half = nm.shape[1]
    tiles = grads[0].shape[0]
    steps = 2
    grads = [g.reshape(steps, tiles // steps, half) for g in grads]
    gspec = pl.BlockSpec((1, tiles // steps, half), lambda i: (i, 0, 0))
    tspec = pl.BlockSpec((NY, NZ, aw // (NY * NZ), half), lambda i: (0, 0, 0, 0))
    term = jax.ShapeDtypeStruct((NY, NZ, aw // (NY * NZ), half), BF16)
    wide = pl.BlockSpec((rows // steps, half), lambda i: (i, 0))
    mixed = jax.ShapeDtypeStruct((rows, half), BF16)
    return pl.pallas_call(
        backward_kernel,
        out_shape=(mixed, mixed, term, term),
        grid=(steps,),
        in_specs=[
            ANY,
            pl.BlockSpec((rows // steps, aw), lambda i: (i, 0)),
            wide,
            wide,
            pl.BlockSpec((rows // steps, 128), lambda i: (i, 0)),
            gspec,
            gspec,
        ],
        out_specs=(wide, wide, tspec, tspec),
        scratch_shapes=[pltpu.VMEM((aw, half), F32), pltpu.VMEM((aw, half), F32)],
        compiler_params=params(56),
        cost_estimate=cost(2.4, 16),
        name="backward",
    )(before, tokens, nm, no, inv_std, *grads)


def head_out_grad_kernel(at_ref, xm_ref, xo_ref, pm_ref, po_ref, out_ref, done_ref):
    done_ref[...] = jnp.zeros_like(done_ref)
    grad = dot_general(xm_ref[...], pm_ref[...], CONTRACT_LAST) + dot_general(xo_ref[...], po_ref[...], CONTRACT_LAST)
    out_ref[...] = grad.astype(BF16)


def head_out_grad_of(at, xm, xo, pm, po):
    rows, half = xm.shape
    aw = pm.shape[0]
    steps = 2
    spec = pl.BlockSpec((rows // steps, half), lambda i: (i, 0))
    return pl.pallas_call(
        head_out_grad_kernel,
        out_shape=(jax.ShapeDtypeStruct((rows, aw), BF16), jax.ShapeDtypeStruct((8, 128), F32)),
        grid=(steps,),
        in_specs=[SMEM, spec, spec, VMEM, VMEM],
        out_specs=(
            pl.BlockSpec((rows // steps, aw), lambda i: (i, 0)),
            pl.BlockSpec((8, 128), lambda i: (0, 0)),
        ),
        compiler_params=params(32),
        cost_estimate=cost(0.01, 0.1),
        name="head_out_grad",
    )(at, xm, xo, pm, po)


def pair_sum_kernel(at_ref, _, mine_ref, other_ref, *out_refs):
    for k, out_ref in enumerate(out_refs):
        y = lax.rem(at_ref[1] + k, NY)
        for z in range(NZ):
            out_ref[z] = (mine_ref[y, z].astype(F32) + other_ref[y, z].astype(F32)).astype(BF16)


def pair_sum(at, before, mine, other):
    return pl.pallas_call(
        pair_sum_kernel,
        out_shape=[jax.ShapeDtypeStruct(mine.shape[1:], BF16)] * NY,
        in_specs=[SMEM, ANY, VMEM, VMEM],
        out_specs=[VMEM] * NY,
        compiler_params=params(32),
        cost_estimate=cost(0.001, 0.1),
        name="pair_sum",
    )(at, before, mine, other)


def sum_kernel(n, *refs):
    if refs[0].shape == refs[-1].shape:
        parts = [ref[...] for ref in refs[:n]]
    else:
        parts = [refs[0][z] for z in range(refs[0].shape[0])]
    refs[-1][...] = sum(part.astype(F32) for part in parts).astype(BF16)


def sum_of(name, before, parts, gflop=0.001):
    if isinstance(parts, jax.Array):
        parts = [parts]
        shape = parts[0].shape[1:]
    else:
        shape = parts[0].shape
    return pl.pallas_call(
        functools.partial(sum_kernel, len(parts)),
        out_shape=jax.ShapeDtypeStruct(shape, BF16),
        in_specs=[VMEM] * len(parts) + [ANY] * len(before),
        out_specs=VMEM,
        compiler_params=params(32),
        cost_estimate=cost(gflop, 0.1),
        name=name,
    )(*parts, *before)


def by_z_kernel(at_ref, *refs):
    for k, ref in enumerate(refs[:-1]):
        refs[-1][lax.rem(at_ref[4] + NZ - k, NZ)] = ref[...]


def by_z(at, pieces):
    return pl.pallas_call(
        by_z_kernel,
        out_shape=jax.ShapeDtypeStruct((NZ,) + pieces[0].shape, BF16),
        in_specs=[SMEM] + [VMEM] * NZ,
        out_specs=VMEM,
        compiler_params=params(32),
        cost_estimate=cost(0.001, 0.1),
        name="by_z",
    )(at, *pieces)


def arrange_kernel(at_ref, in_ref, *refs):
    proj_ref, heads_ref = refs[-2:]
    for y in range(NY):
        for z in range(NZ):
            proj_ref[z, y] = in_ref[y, z]
    for i in range(2):
        heads_ref[i] = in_ref[2 * at_ref[0] + i, NZ]


def arrange(at, gathered, before):
    block = gathered.shape[2:]
    return pl.pallas_call(
        arrange_kernel,
        out_shape=(jax.ShapeDtypeStruct((NZ, NY) + block, BF16), jax.ShapeDtypeStruct((2,) + block, BF16)),
        in_specs=[SMEM, VMEM] + [ANY] * len(before),
        out_specs=(VMEM, VMEM),
        compiler_params=params(32),
        cost_estimate=cost(0.001, 0.1),
        name="arrange",
    )(at, gathered, *before)


def by_y_kernel(cuts, at_ref, *refs):
    for k, ref in enumerate(refs[:NY]):
        y = lax.rem(at_ref[1] + NY - k, NY)
        for (start, stop), out_ref in zip(cuts, refs[NY:]):
            for z in range(NZ):
                out_ref[z, y] = ref[z, start:stop, :]


def by_y(at, pieces, *sizes):
    zs, _, cols = pieces[0].shape
    stops = [sum(sizes[: i + 1]) for i in range(len(sizes))]
    cuts = [(stop - size, stop) for stop, size in zip(stops, sizes)]
    return pl.pallas_call(
        functools.partial(by_y_kernel, cuts),
        out_shape=[jax.ShapeDtypeStruct((zs, NY, size, cols), BF16) for size in sizes],
        in_specs=[SMEM] + [VMEM] * NY,
        out_specs=[VMEM] * len(sizes),
        compiler_params=params(32),
        cost_estimate=cost(0.01, 1),
        name="by_y",
    )(at, *pieces)


def place(row, s):
    return s * 512 + ((row // 16) % NZ * NY + row // (16 * NZ)) * 16 + row % 16


def bias_kernel(heads, at_ref, seg_ref, dil_ref, out_ref, done_ref, q_ref, k_ref):
    s, y, count = at_ref[0], at_ref[1], at_ref[2]
    rows = q_ref.shape[0]
    span = 128 // heads

    def fill(ref, pos, valid):
        lane = lax.broadcasted_iota(jnp.int32, pos.shape, 1)
        column, head = lane & (span - 1), y * heads + lax.shift_right_logical(lane, jnp.full_like(lane, 5))
        hits = None
        for c in range(seg_ref.shape[0]):
            width = seg_ref[c]
            bits = 6 + sum((width > 64 << b).astype(jnp.int32) for b in range(4))
            first = lax.shift_right_logical(jnp.int32(2 * rows), bits)
            ids = first + lax.shift_right_logical(pos, jnp.full_like(pos, bits))
            hit = (ids == column) & (((pos ^ head) & (dil_ref[c] - 1)) == 0)
            hits = hit if hits is None else hits | hit
        ref[...] = jnp.where(hits & valid, 1.0, 0.0).astype(BF16)

    h = pl.program_id(0)

    @pl.when(h == 0)
    def _():
        row = lax.broadcasted_iota(jnp.int32, (rows, 128), 0)
        pos = place(row, s)
        fill(q_ref, pos, pos >= 0)
        row = lax.broadcasted_iota(jnp.int32, (2 * rows, 128), 0)
        pos = place(row % rows, row // rows)
        fill(k_ref, pos, pos < count)
        done_ref[...] = jnp.zeros_like(done_ref)

    block = 128
    of_head = lax.broadcasted_iota(jnp.int32, (1, 128), 1) // span == h
    for start in range(0, rows, block):
        span_rows = pl.ds(start, block)
        queries = jnp.where(of_head, q_ref[span_rows, :], 0).astype(BF16)
        counted = dot_general(queries, k_ref[...], CONTRACT_LAST)
        out_ref[0, span_rows, :] = jnp.where(counted > 0.5, jnp.log2(jnp.maximum(counted, 1.0)), -1e30)


def biases(at, seg_lengths, dilation, heads, rows):
    return pl.pallas_call(
        functools.partial(bias_kernel, heads),
        out_shape=(jax.ShapeDtypeStruct((heads, rows, 2 * rows), F32), jax.ShapeDtypeStruct((8, 128), F32)),
        grid=(heads,),
        in_specs=[SMEM] * 3,
        out_specs=(
            pl.BlockSpec((1, rows, 2 * rows), lambda h: (h, 0, 0)),
            pl.BlockSpec((8, 128), lambda h: (0, 0)),
        ),
        scratch_shapes=[pltpu.VMEM((rows, 128), BF16), pltpu.VMEM((2 * rows, 128), BF16)],
        compiler_params=params(60),
        cost_estimate=cost(1, 1),
        name="biases",
    )(at, seg_lengths, dilation)


def spread_kernel(common_ref, own_ref, _, out_ref):
    blocks = common_ref.shape[0]
    for y in range(NY):
        out_ref[y, :blocks] = common_ref[...]
        out_ref[y, blocks] = own_ref[y]


def spread(common, own, before):
    return pl.pallas_call(
        spread_kernel,
        out_shape=jax.ShapeDtypeStruct((NY, common.shape[0] + 1) + common.shape[1:], BF16),
        in_specs=[VMEM, VMEM, ANY],
        out_specs=VMEM,
        compiler_params=params(32),
        cost_estimate=cost(0.001, 0.1),
        name="spread",
    )(common, own, before)


def attend_kernel(at_ref, hm_ref, ho_ref, wm_ref, wo_ref, bias_ref, *refs):
    out_ref, w_ref, q_ref, k_ref, v_ref = refs[-5:]
    s = at_ref[0]
    rows = hm_ref.shape[0]
    half = hm_ref.shape[1] // 2
    heads, block, keys = bias_ref.shape
    seg = q_ref.shape[2]

    @pl.when(pl.program_id(0) == 0)
    def _():
        for z in range(NZ):
            w_ref[z, s] = wm_ref[z]
            w_ref[z, 1 - s] = wo_ref[z]
        w_mine = w_ref[pl.ds(s * (NZ // 2), NZ // 2)].reshape(half, w_ref.shape[3])
        w_other = w_ref[pl.ds((1 - s) * (NZ // 2), NZ // 2)].reshape(half, w_ref.shape[3])
        for core in range(2):
            lanes = slice(core * half, (core + 1) * half)
            all_parts = dot(hm_ref[:, lanes], w_mine) + dot(ho_ref[:, lanes], w_other)
            span = pl.ds(core * rows, rows)
            q_ref[core] = all_parts[:, :seg].astype(BF16)
            k_ref[span, :] = all_parts[:, seg : 2 * seg].astype(BF16)
            v_ref[span, :] = all_parts[:, 2 * seg :].astype(BF16)

    lane_head = lax.broadcasted_iota(jnp.int32, (1, seg), 1) // HS
    scale = HS ** (-0.5) * 1.4426950408889634
    queries = q_ref[s, pl.ds(pl.multiple_of(pl.program_id(0) * block, block), block), :]
    queries = jnp.concatenate([jnp.where(lane_head == h, queries, 0).astype(BF16) for h in range(heads)])
    scores = dot_general(queries, k_ref[...], CONTRACT_LAST)
    scores = scores * scale + bias_ref[...].reshape(heads * block, keys)
    weights = jnp.exp2(scores - jnp.max(scores, axis=-1, keepdims=True))
    total = jnp.sum(weights, axis=-1, keepdims=True)
    part = dot(weights.astype(BF16), v_ref[...]) * (1.0 / total)
    for h in range(heads):
        turned = part[h * block : (h + 1) * block].T
        out_ref[h * HS : (h + 1) * HS, :] = turned[h * HS : (h + 1) * HS].astype(BF16)


def attend(at, hm, ho, wm, wo, bias, before):
    heads, rows, keys = bias.shape
    seg = wm.shape[2] // 3
    block = 128
    return pl.pallas_call(
        attend_kernel,
        out_shape=jax.ShapeDtypeStruct((heads * HS, rows), BF16),
        grid=(rows // block,),
        in_specs=[SMEM] + [VMEM] * 4 + [pl.BlockSpec((heads, block, keys), lambda i: (0, i, 0))] + [ANY] * len(before),
        out_specs=pl.BlockSpec((heads * HS, block), lambda i: (0, i)),
        scratch_shapes=[
            pltpu.VMEM((NZ, 2) + wm.shape[1:], BF16),
            pltpu.VMEM((2, rows, seg), BF16),
            pltpu.VMEM((keys, seg), BF16),
            pltpu.VMEM((keys, seg), BF16),
        ],
        compiler_params=params(48),
        cost_estimate=cost(8, 12, 2),
        name="attend",
    )(at, hm, ho, wm, wo, bias, *before)


def finish_kernel(at_ref, a0_ref, a1_ref, a2_ref, a3_ref, wm_ref, wo_ref, hm_ref, ho_ref, out_ref):
    s, y, count = at_ref[0], at_ref[1], at_ref[2]
    rows, half = hm_ref.shape[0], hm_ref.shape[1] // 2
    tiles = out_ref.shape[2]
    mine = other = 0.0
    for k, att_ref in enumerate((a0_ref, a1_ref, a2_ref, a3_ref)):
        depth = att_ref.shape[0]
        span = pl.ds(pl.multiple_of(lax.rem(y + NY - k, NY) * depth, depth), depth)
        mine = mine + dot_general(att_ref[...], wm_ref[span, :], CONTRACT_FIRST)
        other = other + dot_general(att_ref[...], wo_ref[span, :], CONTRACT_FIRST)
    lanes = pl.ds(pl.multiple_of(s * half, half), half)
    mine = mine + hm_ref[:, lanes].astype(F32)
    other = other + ho_ref[:, lanes].astype(F32)
    row = lax.broadcasted_iota(jnp.int32, (rows, half), 0)
    valid = place(row, s) < count
    left = jnp.where(valid, jnp.where(s == 0, mine, other), 0.0).astype(BF16)
    right = jnp.where(valid, jnp.where(s == 0, other, mine), 0.0).astype(BF16)
    span = NZ * tiles
    for y in range(NY):
        for part, lanes in ((left, slice(0, half)), (right, slice(half, 2 * half))):
            out_ref[:, y, :, lanes] = part[y * span : (y + 1) * span].reshape(NZ, tiles, half)


def finish(at, att, wm, wo, hm, ho, tiles):
    return pl.pallas_call(
        finish_kernel,
        out_shape=jax.ShapeDtypeStruct((NZ, NY, tiles, hm.shape[1]), BF16),
        in_specs=[SMEM] + [VMEM] * 8,
        out_specs=VMEM,
        compiler_params=params(32),
        cost_estimate=cost(0.6, 4),
        name="finish",
    )(at, *att, wm, wo, hm, ho)


def body(
    head_out,
    proj_weight,
    norm_gain,
    embed_cot,
    tile_counts,
    seg_lengths,
    dilation,
    embed_weight,
    qkv_weight,
    out_weight,
):
    tokens = head_out[0]
    n_rows, aw = tokens.shape
    dt = proj_weight.shape[1]
    half = dt // 2
    tiles = embed_cot.shape[1]
    per_tile = n_rows // tiles
    fsdp = NZ * NY
    f = lax.axis_index("fsdp")
    s = lax.axis_index("seq")
    y = f % NY
    count = tile_counts[0]
    ds = out_weight.shape[1]
    shard_len = fsdp * tiles
    x = lax.axis_index("slide")
    at = jnp.stack([s, y, count, x, f // NY]).astype(jnp.int32)
    dslice = lax.dynamic_slice_in_dim
    heads = ds // HS // NY
    width = heads * HS

    def of_y(v, k):
        return lax.dynamic_index_in_dim(v, (y + k) % NY, 0, keepdims=False)

    bias, zero = biases(at, seg_lengths, dilation, heads, shard_len)

    rows = proj_weight.shape[0]
    w_heads = qkv_weight.reshape(rows, 3, NY, width).transpose(2, 0, 1, 3)
    w_heads = jnp.pad(w_heads, ((0, 0), (0, 0), (0, 0), (0, 256 - width))).reshape(NY, rows, 3 * 256)

    quarter = ds // 2
    first = a2a_z(copies(dslice(proj_weight, s * half, half, 1), NZ))
    others = jnp.concatenate([dslice(w, s * quarter, quarter, 1) for w in (embed_weight, out_weight)])
    others = after(others, first)
    others = [others] + [shift_z(others, k) for k in range(1, NZ)]
    gathered = a2a_y(spread(first, w_heads, zero))
    proj_mine, w_heads = arrange(at, gathered, others[1:])
    proj_mine, w_heads = proj_mine.reshape(aw, half), w_heads.reshape(2 * rows, half)
    proj_other = swap(proj_mine)
    others = by_z(at, others)
    others = [others] + [shift_y(others, k) for k in range(1, NY)]

    def halves(v):
        return dslice(v, s * half, half, v.ndim - 1), dslice(v, (1 - s) * half, half, v.ndim - 1)

    gain = halves(norm_gain)
    embed, normed_mine, normed_other, inv_std = forward(at, tokens, proj_mine, proj_other, jnp.stack(gain), tiles)
    embed = embed.astype(BF16)
    embed_other = swap(embed)
    embed = jnp.concatenate([jnp.where(s == 0, embed, embed_other), jnp.where(s == 0, embed_other, embed)])

    base = (s * fsdp + f) * tiles
    valid = (base + jnp.arange(tiles, dtype=jnp.int32) < count).astype(F32)
    grads = [c * valid[:, None] / per_tile * g for c, g in zip(halves(embed_cot[0].astype(F32)), gain)]

    w_embed, w_out = by_y(at, others, 2 * rows, rows)
    w_embed, w_out = w_embed.reshape(dt, quarter), w_out.reshape(ds, quarter)
    w_out_other = swap(w_out)
    hidden = dot(embed, w_embed).astype(BF16)
    hidden = jnp.concatenate([hidden[:tiles], hidden[tiles:]], axis=1)
    mixed_mine, mixed_other, term_mine, term_other = backward(
        hidden, tokens, normed_mine, normed_other, inv_std, grads
    )
    second = a2a_z(copies(jnp.concatenate([hidden, w_heads]), NZ))

    head_out_grad, zero = head_out_grad_of(at, mixed_mine, mixed_other, proj_mine, proj_other)
    parts = pair_sum(at, zero, term_mine, swap(term_other))
    hidden = a2a_y(copies(after(second[:, :tiles], parts[0]), NY)).reshape(shard_len, ds)
    hidden_other = swap(hidden)
    parts = [parts[0]] + [shift_y(parts[k], k) for k in range(1, NY)]

    w_heads = second[:, tiles:]
    w_heads_other = swap(w_heads)
    attended = attend(at, hidden, hidden_other, w_heads, w_heads_other, bias, [])
    share = a2a_z(sum_of("y_sum", [attended], parts, 0.001))
    received = [attended] + [shift_y(attended, k) for k in range(1, NY)]
    share = sum_of("z_sum", [], share)
    parts = [share] + [shift_x(share, k) for k in range(1, NX)]
    slide_out = finish(at, received, w_out, w_out_other, hidden, hidden_other, tiles)
    share = sum_of("x_sum", [slide_out], parts)
    other = swap(share)
    slide_out = slide_out.reshape(1, shard_len, ds)
    proj_grad = jnp.concatenate([jnp.where(s == 0, share, other), jnp.where(s == 0, other, share)], axis=1)
    return (slide_out, head_out_grad[None], proj_grad)


def solution(mesh):
    return jax.shard_map(
        body,
        mesh=mesh,
        in_specs=(
            P("slide", ("seq", "fsdp"), None),
            P("fsdp", None),
            P(),
            P("slide", ("seq", "fsdp"), None),
            P("slide"),
            P(),
            P(),
            P("fsdp", None),
            P("fsdp", None),
            P("fsdp", None),
        ),
        out_specs=(P("slide", "seq", None), P("slide", ("seq", "fsdp"), None), P("fsdp", None)),
        check_vma=False,
    )
```

```python
import functools

import jax
import jax.numpy as jnp
from jax import lax
from jax.experimental import pallas as pl
from jax.experimental.pallas import tpu as pltpu
from jax.sharding import PartitionSpec as P

HS = 48
NX, NZ, NY = 4, 8, 4
Z_GROUPS = [[z * NY + y for z in range(NZ)] for y in range(NY)]
Y_GROUPS = [[z * NY + y for y in range(NY)] for z in range(NZ)]
SWAP = [(0, 1), (1, 0)]
F32, BF16 = jnp.float32, jnp.bfloat16
VMEM = pl.BlockSpec(memory_space=pltpu.VMEM)
SMEM = pl.BlockSpec(memory_space=pltpu.SMEM)
ANY = pl.BlockSpec(memory_space=pl.ANY)
CONTRACT_LAST = (((1,), (1,)), ((), ()))
CONTRACT_FIRST = (((0,), (0,)), ((), ()))
dot = functools.partial(jnp.dot, preferred_element_type=F32)
dot_general = functools.partial(lax.dot_general, preferred_element_type=F32)


def a2a_z(v):
    return lax.all_to_all(v, "fsdp", 0, 0, axis_index_groups=Z_GROUPS)


def a2a_y(v):
    return lax.all_to_all(v, "fsdp", 0, 0, axis_index_groups=Y_GROUPS)


def copies(v, n):
    return jnp.broadcast_to(v[None], (n,) + v.shape)


def swap(v):
    return lax.ppermute(v, "seq", SWAP)


def shift_y(v, k):
    return lax.ppermute(
        v, "fsdp", [(z * NY + y, z * NY + (y + k) % NY) for z in range(NZ) for y in range(NY)]
    )


def shift_z(v, k):
    return lax.ppermute(
        v, "fsdp", [(z * NY + y, (z + k) % NZ * NY + y) for z in range(NZ) for y in range(NY)]
    )


def shift_x(v, k):
    return lax.ppermute(v, "slide", [(x, (x + k) % NX) for x in range(NX)])


def after(v, other):
    return v + (other[(0,) * other.ndim].astype(F32) * 0).astype(v.dtype)


def params(mib):
    return pltpu.CompilerParams(vmem_limit_bytes=mib * 1024 * 1024)


def cost(gflop, mb, mexp=0):
    return pl.CostEstimate(
        flops=int(gflop * 1e9), bytes_accessed=int(mb * 1e6), transcendentals=int(mexp * 1e6)
    )


def forward_kernel(tiles, at_ref, tok_ref, pm_ref, po_ref, gain_ref, out_ref, nm_ref, no_ref, inv_ref):
    tok = tok_ref[...]
    mixed = [dot(tok, pm_ref[...]), dot(tok, po_ref[...])]
    rows, half = mixed[0].shape
    centre = sum(jnp.sum(m, axis=-1, keepdims=True) for m in mixed) * (0.5 / half)
    shifted = [m - centre for m in mixed]
    var = sum(jnp.sum(m * m, axis=-1, keepdims=True) for m in shifted) * (0.5 / half)
    inv_std = lax.rsqrt(var + 1e-06)
    inv_ref[...] = jnp.broadcast_to(inv_std, inv_ref.shape)
    pooled = []
    for i, (m, n_ref) in enumerate(zip(shifted, (nm_ref, no_ref))):
        n = m * inv_std
        n_ref[...] = n
        mean = jnp.sum(n.reshape(tiles, rows // tiles, half), axis=1) * (tiles / rows)
        pooled.append(mean * gain_ref[i : i + 1, :])
    span = pl.ds(pl.multiple_of(pl.program_id(0) * tiles, tiles), tiles)
    for s in range(2):

        @pl.when(at_ref[0] == s)
        def _():
            out_ref[span, :half] = pooled[s]
            out_ref[span, half:] = pooled[1 - s]


def forward(at, tokens, pm, po, gain, tiles):
    rows, aw = tokens.shape
    half = pm.shape[1]
    steps = 2
    spec = pl.BlockSpec((rows // steps, half), lambda i: (i, 0))
    return pl.pallas_call(
        functools.partial(forward_kernel, tiles // steps),
        out_shape=(
            jax.ShapeDtypeStruct((tiles, 2 * half), F32),
            jax.ShapeDtypeStruct((rows, half), F32),
            jax.ShapeDtypeStruct((rows, half), F32),
            jax.ShapeDtypeStruct((rows, 128), F32),
        ),
        grid=(steps,),
        in_specs=[SMEM, pl.BlockSpec((rows // steps, aw), lambda i: (i, 0)), VMEM, VMEM, VMEM],
        out_specs=(
            pl.BlockSpec((tiles, 2 * half), lambda i: (0, 0)),
            spec,
            spec,
            pl.BlockSpec((rows // steps, 128), lambda i: (i, 0)),
        ),
        compiler_params=params(48),
        cost_estimate=cost(2.4, 10),
        name="forward",
    )(at, tokens, pm, po, gain)


def backward_kernel(_, tok_ref, nm_ref, no_ref, inv_ref, gm_ref, go_ref, xm_ref, xo_ref, tm_ref, to_ref, am_ref, ao_ref):
    step, steps = pl.program_id(0), pl.num_programs(0)
    tok = tok_ref[...]
    normed = [nm_ref[...], no_ref[...]]
    inv_std = inv_ref[:, :1]
    rows, half = normed[0].shape
    tiles = gm_ref.shape[1]
    grads = [gm_ref[0], go_ref[0]]
    mean = sum(jnp.sum(g, axis=-1, keepdims=True) for g in grads) * (0.5 / half)

    def per_token(v):
        return jnp.broadcast_to(v[:, None, :], (tiles, rows // tiles, v.shape[1])).reshape(rows, v.shape[1])

    along = sum(jnp.sum(per_token(g) * n, axis=-1, keepdims=True) for g, n in zip(grads, normed)) * (0.5 / half)
    mixed = [(inv_std * (per_token(g - mean) - n * along)).astype(BF16) for g, n in zip(grads, normed)]
    xm_ref[...] = mixed[0]
    xo_ref[...] = mixed[1]
    for acc_ref, term_ref, m in ((am_ref, tm_ref, mixed[0]), (ao_ref, to_ref, mixed[1])):
        term = dot_general(tok, m, CONTRACT_FIRST)

        @pl.when(step == 0)
        def _():
            acc_ref[...] = term

        @pl.when(step > 0)
        def _():
            acc_ref[...] += term

        @pl.when(step == steps - 1)
        def _():
            block = term_ref.shape[2]
            for z in range(NZ):
                for y in range(NY):
                    term_ref[y, z] = acc_ref[pl.ds((z * NY + y) * block, block), :].astype(BF16)


def backward(before, tokens, nm, no, inv_std, grads):
    rows, aw = tokens.shape
    half = nm.shape[1]
    tiles = grads[0].shape[0]
    steps = 2
    grads = [g.reshape(steps, tiles // steps, half) for g in grads]
    gspec = pl.BlockSpec((1, tiles // steps, half), lambda i: (i, 0, 0))
    tspec = pl.BlockSpec((NY, NZ, aw // (NY * NZ), half), lambda i: (0, 0, 0, 0))
    term = jax.ShapeDtypeStruct((NY, NZ, aw // (NY * NZ), half), BF16)
    wide = pl.BlockSpec((rows // steps, half), lambda i: (i, 0))
    mixed = jax.ShapeDtypeStruct((rows, half), BF16)
    return pl.pallas_call(
        backward_kernel,
        out_shape=(mixed, mixed, term, term),
        grid=(steps,),
        in_specs=[
            ANY,
            pl.BlockSpec((rows // steps, aw), lambda i: (i, 0)),
            wide,
            wide,
            pl.BlockSpec((rows // steps, 128), lambda i: (i, 0)),
            gspec,
            gspec,
        ],
        out_specs=(wide, wide, tspec, tspec),
        scratch_shapes=[pltpu.VMEM((aw, half), F32), pltpu.VMEM((aw, half), F32)],
        compiler_params=params(56),
        cost_estimate=cost(2.4, 16),
        name="backward",
    )(before, tokens, nm, no, inv_std, *grads)


def head_out_grad_kernel(at_ref, xm_ref, xo_ref, pm_ref, po_ref, out_ref, done_ref):
    done_ref[...] = jnp.zeros_like(done_ref)
    grad = dot_general(xm_ref[...], pm_ref[...], CONTRACT_LAST) + dot_general(xo_ref[...], po_ref[...], CONTRACT_LAST)
    out_ref[...] = grad.astype(BF16)


def head_out_grad_of(at, xm, xo, pm, po):
    rows, half = xm.shape
    aw = pm.shape[0]
    steps = 2
    spec = pl.BlockSpec((rows // steps, half), lambda i: (i, 0))
    return pl.pallas_call(
        head_out_grad_kernel,
        out_shape=(jax.ShapeDtypeStruct((rows, aw), BF16), jax.ShapeDtypeStruct((8, 128), F32)),
        grid=(steps,),
        in_specs=[SMEM, spec, spec, VMEM, VMEM],
        out_specs=(
            pl.BlockSpec((rows // steps, aw), lambda i: (i, 0)),
            pl.BlockSpec((8, 128), lambda i: (0, 0)),
        ),
        compiler_params=params(32),
        cost_estimate=cost(0.01, 0.1),
        name="head_out_grad",
    )(at, xm, xo, pm, po)


def pair_sum_kernel(at_ref, _, mine_ref, other_ref, *out_refs):
    for k, out_ref in enumerate(out_refs):
        y = lax.rem(at_ref[1] + k, NY)
        for z in range(NZ):
            out_ref[z] = (mine_ref[y, z].astype(F32) + other_ref[y, z].astype(F32)).astype(BF16)


def pair_sum(at, before, mine, other):
    return pl.pallas_call(
        pair_sum_kernel,
        out_shape=[jax.ShapeDtypeStruct(mine.shape[1:], BF16)] * NY,
        in_specs=[SMEM, ANY, VMEM, VMEM],
        out_specs=[VMEM] * NY,
        compiler_params=params(32),
        cost_estimate=cost(0.001, 0.1),
        name="pair_sum",
    )(at, before, mine, other)


def sum_kernel(n, *refs):
    if refs[0].shape == refs[-1].shape:
        parts = [ref[...] for ref in refs[:n]]
    else:
        parts = [refs[0][z] for z in range(refs[0].shape[0])]
    refs[-1][...] = sum(part.astype(F32) for part in parts).astype(BF16)


def sum_of(name, before, parts, gflop=0.001):
    if isinstance(parts, jax.Array):
        parts = [parts]
        shape = parts[0].shape[1:]
    else:
        shape = parts[0].shape
    return pl.pallas_call(
        functools.partial(sum_kernel, len(parts)),
        out_shape=jax.ShapeDtypeStruct(shape, BF16),
        in_specs=[VMEM] * len(parts) + [ANY] * len(before),
        out_specs=VMEM,
        compiler_params=params(32),
        cost_estimate=cost(gflop, 0.1),
        name=name,
    )(*parts, *before)


def rest_kernel(skip, in_ref, *refs):
    for z in range(NZ):
        refs[-1][z] = in_ref[z, skip:, :]


def rest_of(gathered, skip, before):
    zs, rows, cols = gathered.shape
    return pl.pallas_call(
        functools.partial(rest_kernel, skip),
        out_shape=jax.ShapeDtypeStruct((zs, rows - skip, cols), BF16),
        in_specs=[VMEM] + [ANY] * len(before),
        out_specs=VMEM,
        compiler_params=params(32),
        cost_estimate=cost(5, 0.1),
        name="rest",
    )(gathered, *before)


def by_z_kernel(at_ref, *refs):
    for k, ref in enumerate(refs[:-1]):
        refs[-1][lax.rem(at_ref[4] + NZ - k, NZ)] = ref[...]


def by_z(at, pieces):
    return pl.pallas_call(
        by_z_kernel,
        out_shape=jax.ShapeDtypeStruct((NZ,) + pieces[0].shape, BF16),
        in_specs=[SMEM] + [VMEM] * NZ,
        out_specs=VMEM,
        compiler_params=params(32),
        cost_estimate=cost(0.001, 0.1),
        name="by_z",
    )(at, *pieces)


def arrange_kernel(at_ref, in_ref, *refs):
    proj_ref, heads_ref = refs[-2:]
    for y in range(NY):
        for z in range(NZ):
            proj_ref[z, y] = in_ref[y, z]
    for i in range(2):
        heads_ref[i] = in_ref[2 * at_ref[0] + i, NZ]


def arrange(at, gathered, before):
    block = gathered.shape[2:]
    return pl.pallas_call(
        arrange_kernel,
        out_shape=(jax.ShapeDtypeStruct((NZ, NY) + block, BF16), jax.ShapeDtypeStruct((2,) + block, BF16)),
        in_specs=[SMEM, VMEM] + [ANY] * len(before),
        out_specs=(VMEM, VMEM),
        compiler_params=params(32),
        cost_estimate=cost(0.001, 0.1),
        name="arrange",
    )(at, gathered, *before)


def by_y_kernel(cuts, at_ref, *refs):
    for k, ref in enumerate(refs[:NY]):
        y = lax.rem(at_ref[1] + NY - k, NY)
        for (start, stop), out_ref in zip(cuts, refs[NY:]):
            for z in range(NZ):
                out_ref[z, y] = ref[z, start:stop, :]


def by_y(at, pieces, *sizes, gflop=0.01):
    zs, _, cols = pieces[0].shape
    stops = [sum(sizes[: i + 1]) for i in range(len(sizes))]
    cuts = [(stop - size, stop) for stop, size in zip(stops, sizes)]
    return pl.pallas_call(
        functools.partial(by_y_kernel, cuts),
        out_shape=[jax.ShapeDtypeStruct((zs, NY, size, cols), BF16) for size in sizes],
        in_specs=[SMEM] + [VMEM] * NY,
        out_specs=[VMEM] * len(sizes),
        compiler_params=params(32),
        cost_estimate=cost(gflop, 1),
        name="by_y",
    )(at, *pieces)


def place(row, s):
    return s * 512 + ((row // 16) % NZ * NY + row // (16 * NZ)) * 16 + row % 16


def bias_kernel(heads, at_ref, seg_ref, dil_ref, out_ref, done_ref, q_ref, k_ref):
    s, y, count = at_ref[0], at_ref[1], at_ref[2]
    rows = q_ref.shape[0]
    span = 128 // heads

    def fill(ref, pos, valid):
        lane = lax.broadcasted_iota(jnp.int32, pos.shape, 1)
        column, head = lane & (span - 1), y * heads + lax.shift_right_logical(lane, jnp.full_like(lane, 5))
        hits = None
        for c in range(seg_ref.shape[0]):
            width = seg_ref[c]
            bits = 6 + sum((width > 64 << b).astype(jnp.int32) for b in range(4))
            first = lax.shift_right_logical(jnp.int32(2 * rows), bits)
            ids = first + lax.shift_right_logical(pos, jnp.full_like(pos, bits))
            hit = (ids == column) & (((pos ^ head) & (dil_ref[c] - 1)) == 0)
            hits = hit if hits is None else hits | hit
        ref[...] = jnp.where(hits & valid, 1.0, 0.0).astype(BF16)

    h = pl.program_id(0)

    @pl.when(h == 0)
    def _():
        row = lax.broadcasted_iota(jnp.int32, (rows, 128), 0)
        pos = place(row, s)
        fill(q_ref, pos, pos >= 0)
        row = lax.broadcasted_iota(jnp.int32, (2 * rows, 128), 0)
        pos = place(row % rows, row // rows)
        fill(k_ref, pos, pos < count)
        done_ref[...] = jnp.zeros_like(done_ref)

    block = 128
    of_head = lax.broadcasted_iota(jnp.int32, (1, 128), 1) // span == h
    for start in range(0, rows, block):
        span_rows = pl.ds(start, block)
        queries = jnp.where(of_head, q_ref[span_rows, :], 0).astype(BF16)
        counted = dot_general(queries, k_ref[...], CONTRACT_LAST)
        out_ref[0, span_rows, :] = jnp.where(counted > 0.5, jnp.log2(jnp.maximum(counted, 1.0)), -1e30)


def biases(at, seg_lengths, dilation, heads, rows):
    return pl.pallas_call(
        functools.partial(bias_kernel, heads),
        out_shape=(jax.ShapeDtypeStruct((heads, rows, 2 * rows), F32), jax.ShapeDtypeStruct((8, 128), F32)),
        grid=(heads,),
        in_specs=[SMEM] * 3,
        out_specs=(
            pl.BlockSpec((1, rows, 2 * rows), lambda h: (h, 0, 0)),
            pl.BlockSpec((8, 128), lambda h: (0, 0)),
        ),
        scratch_shapes=[pltpu.VMEM((rows, 128), BF16), pltpu.VMEM((2 * rows, 128), BF16)],
        compiler_params=params(60),
        cost_estimate=cost(1, 1),
        name="biases",
    )(at, seg_lengths, dilation)


def spread_kernel(common_ref, own_ref, _, out_ref):
    blocks = common_ref.shape[0]
    for y in range(NY):
        out_ref[y, :blocks] = common_ref[...]
        out_ref[y, blocks] = own_ref[y]


def spread(common, own, before):
    return pl.pallas_call(
        spread_kernel,
        out_shape=jax.ShapeDtypeStruct((NY, common.shape[0] + 1) + common.shape[1:], BF16),
        in_specs=[VMEM, VMEM, ANY],
        out_specs=VMEM,
        compiler_params=params(32),
        cost_estimate=cost(0.001, 0.1),
        name="spread",
    )(common, own, before)


def attend_kernel(at_ref, hm_ref, ho_ref, wm_ref, wo_ref, bias_ref, *refs):
    out_ref, w_ref, q_ref, k_ref, v_ref = refs[-5:]
    s = at_ref[0]
    rows = hm_ref.shape[0]
    half = hm_ref.shape[1] // 2
    heads, block, keys = bias_ref.shape
    seg = q_ref.shape[2]

    @pl.when(pl.program_id(0) == 0)
    def _():
        for z in range(NZ):
            w_ref[z, s] = wm_ref[z]
            w_ref[z, 1 - s] = wo_ref[z]
        w_mine = w_ref[pl.ds(s * (NZ // 2), NZ // 2)].reshape(half, w_ref.shape[3])
        w_other = w_ref[pl.ds((1 - s) * (NZ // 2), NZ // 2)].reshape(half, w_ref.shape[3])
        for core in range(2):
            lanes = slice(core * half, (core + 1) * half)
            all_parts = dot(hm_ref[:, lanes], w_mine) + dot(ho_ref[:, lanes], w_other)
            span = pl.ds(core * rows, rows)
            q_ref[core] = all_parts[:, :seg].astype(BF16)
            k_ref[span, :] = all_parts[:, seg : 2 * seg].astype(BF16)
            v_ref[span, :] = all_parts[:, 2 * seg :].astype(BF16)

    lane_head = lax.broadcasted_iota(jnp.int32, (1, seg), 1) // HS
    scale = HS ** (-0.5) * 1.4426950408889634
    queries = q_ref[s, pl.ds(pl.multiple_of(pl.program_id(0) * block, block), block), :]
    queries = jnp.concatenate([jnp.where(lane_head == h, queries, 0).astype(BF16) for h in range(heads)])
    scores = dot_general(queries, k_ref[...], CONTRACT_LAST)
    scores = scores * scale + bias_ref[...].reshape(heads * block, keys)
    weights = jnp.exp2(scores - jnp.max(scores, axis=-1, keepdims=True))
    total = jnp.sum(weights, axis=-1, keepdims=True)
    part = dot(weights.astype(BF16), v_ref[...]) * (1.0 / total)
    for h in range(heads):
        turned = part[h * block : (h + 1) * block].T
        out_ref[h * HS : (h + 1) * HS, :] = turned[h * HS : (h + 1) * HS].astype(BF16)


def attend(at, hm, ho, wm, wo, bias, before):
    heads, rows, keys = bias.shape
    seg = wm.shape[2] // 3
    block = 128
    return pl.pallas_call(
        attend_kernel,
        out_shape=jax.ShapeDtypeStruct((heads * HS, rows), BF16),
        grid=(rows // block,),
        in_specs=[SMEM] + [VMEM] * 4 + [pl.BlockSpec((heads, block, keys), lambda i: (0, i, 0))] + [ANY] * len(before),
        out_specs=pl.BlockSpec((heads * HS, block), lambda i: (0, i)),
        scratch_shapes=[
            pltpu.VMEM((NZ, 2) + wm.shape[1:], BF16),
            pltpu.VMEM((2, rows, seg), BF16),
            pltpu.VMEM((keys, seg), BF16),
            pltpu.VMEM((keys, seg), BF16),
        ],
        compiler_params=params(48),
        cost_estimate=cost(8, 12, 2),
        name="attend",
    )(at, hm, ho, wm, wo, bias, *before)


def finish_kernel(at_ref, a0_ref, a1_ref, a2_ref, a3_ref, wm_ref, wo_ref, hm_ref, ho_ref, out_ref):
    s, y, count = at_ref[0], at_ref[1], at_ref[2]
    rows, half = hm_ref.shape[0], hm_ref.shape[1] // 2
    tiles = out_ref.shape[2]
    mine = other = 0.0
    for k, att_ref in enumerate((a0_ref, a1_ref, a2_ref, a3_ref)):
        depth = att_ref.shape[0]
        span = pl.ds(pl.multiple_of(lax.rem(y + NY - k, NY) * depth, depth), depth)
        mine = mine + dot_general(att_ref[...], wm_ref[span, :], CONTRACT_FIRST)
        other = other + dot_general(att_ref[...], wo_ref[span, :], CONTRACT_FIRST)
    lanes = pl.ds(pl.multiple_of(s * half, half), half)
    mine = mine + hm_ref[:, lanes].astype(F32)
    other = other + ho_ref[:, lanes].astype(F32)
    row = lax.broadcasted_iota(jnp.int32, (rows, half), 0)
    valid = place(row, s) < count
    left = jnp.where(valid, jnp.where(s == 0, mine, other), 0.0).astype(BF16)
    right = jnp.where(valid, jnp.where(s == 0, other, mine), 0.0).astype(BF16)
    span = NZ * tiles
    for y in range(NY):
        for part, lanes in ((left, slice(0, half)), (right, slice(half, 2 * half))):
            out_ref[:, y, :, lanes] = part[y * span : (y + 1) * span].reshape(NZ, tiles, half)


def finish(at, att, wm, wo, hm, ho, tiles):
    return pl.pallas_call(
        finish_kernel,
        out_shape=jax.ShapeDtypeStruct((NZ, NY, tiles, hm.shape[1]), BF16),
        in_specs=[SMEM] + [VMEM] * 8,
        out_specs=VMEM,
        compiler_params=params(32),
        cost_estimate=cost(0.6, 4),
        name="finish",
    )(at, *att, wm, wo, hm, ho)


def body(
    head_out,
    proj_weight,
    norm_gain,
    embed_cot,
    tile_counts,
    seg_lengths,
    dilation,
    embed_weight,
    qkv_weight,
    out_weight,
):
    tokens = head_out[0]
    n_rows, aw = tokens.shape
    dt = proj_weight.shape[1]
    half = dt // 2
    tiles = embed_cot.shape[1]
    per_tile = n_rows // tiles
    fsdp = NZ * NY
    f = lax.axis_index("fsdp")
    s = lax.axis_index("seq")
    y = f % NY
    count = tile_counts[0]
    ds = out_weight.shape[1]
    shard_len = fsdp * tiles
    x = lax.axis_index("slide")
    at = jnp.stack([s, y, count, x, f // NY]).astype(jnp.int32)
    dslice = lax.dynamic_slice_in_dim
    heads = ds // HS // NY
    width = heads * HS

    def of_y(v, k):
        return lax.dynamic_index_in_dim(v, (y + k) % NY, 0, keepdims=False)

    bias, zero = biases(at, seg_lengths, dilation, heads, shard_len)

    rows = proj_weight.shape[0]
    w_heads = qkv_weight.reshape(rows, 3, NY, width).transpose(2, 0, 1, 3)
    w_heads = jnp.pad(w_heads, ((0, 0), (0, 0), (0, 0), (0, 256 - width))).reshape(NY, rows, 3 * 256)

    quarter = ds // 2
    first = a2a_z(copies(dslice(proj_weight, s * half, half, 1), NZ))
    others = jnp.concatenate([dslice(w, s * quarter, quarter, 1) for w in (embed_weight, out_weight)])
    others = after(others, first)
    others = [others] + [shift_z(others, k) for k in range(1, NZ)]
    gathered = a2a_y(spread(first, w_heads, zero))
    proj_mine, w_heads = arrange(at, gathered, others[1:])
    proj_mine, w_heads = proj_mine.reshape(aw, half), w_heads.reshape(2 * rows, half)
    proj_other = swap(proj_mine)
    others = by_z(at, others)
    w_out = others[:, 2 * rows :]
    others = others[:, : 2 * rows]
    others = [others] + [shift_y(others, k) for k in range(1, NY)]

    def halves(v):
        return dslice(v, s * half, half, v.ndim - 1), dslice(v, (1 - s) * half, half, v.ndim - 1)

    gain = halves(norm_gain)
    embed, normed_mine, normed_other, inv_std = forward(at, tokens, proj_mine, proj_other, jnp.stack(gain), tiles)
    embed = embed.astype(BF16)
    embed_other = swap(embed)
    embed = jnp.concatenate([jnp.where(s == 0, embed, embed_other), jnp.where(s == 0, embed_other, embed)])

    base = (s * fsdp + f) * tiles
    valid = (base + jnp.arange(tiles, dtype=jnp.int32) < count).astype(F32)
    grads = [c * valid[:, None] / per_tile * g for c, g in zip(halves(embed_cot[0].astype(F32)), gain)]

    (w_embed,) = by_y(at, others, 2 * rows)
    w_embed = w_embed.reshape(dt, quarter)
    hidden = dot(embed, w_embed).astype(BF16)
    hidden = jnp.concatenate([hidden[:tiles], hidden[tiles:]], axis=1)
    mixed_mine, mixed_other, term_mine, term_other = backward(
        hidden, tokens, normed_mine, normed_other, inv_std, grads
    )
    w_out = after(w_out, hidden)
    (w_out,) = by_y(at, [w_out] + [shift_y(w_out, k) for k in range(1, NY)], rows, gflop=5)
    w_out = w_out.reshape(ds, quarter)
    w_out_other = swap(w_out)
    second = a2a_z(copies(jnp.concatenate([hidden, w_heads]), NZ))

    parts = pair_sum(at, w_out, term_mine, swap(term_other))
    hidden = a2a_y(copies(after(second[:, :tiles], parts[0]), NY)).reshape(shard_len, ds)
    hidden_other = swap(hidden)
    head_out_grad, zero = head_out_grad_of(at, mixed_mine, mixed_other, proj_mine, proj_other)
    parts = [parts[0]] + [shift_y(parts[k], k) for k in range(1, NY)]
    w_heads = rest_of(second, tiles, [])
    w_heads_other = swap(w_heads)
    share = a2a_z(sum_of("y_sum", [hidden], parts, 6))

    attended = attend(at, hidden, hidden_other, w_heads, w_heads_other, bias, [zero])
    received = [attended] + [shift_y(attended, k) for k in range(1, NY)]
    share = sum_of("z_sum", [attended], share)
    parts = [share] + [shift_x(share, k) for k in range(1, NX)]
    slide_out = finish(at, received, w_out, w_out_other, hidden, hidden_other, tiles)
    share = sum_of("x_sum", [slide_out], parts)
    other = swap(share)
    slide_out = slide_out.reshape(1, shard_len, ds)
    proj_grad = jnp.concatenate([jnp.where(s == 0, share, other), jnp.where(s == 0, other, share)], axis=1)
    return (slide_out, head_out_grad[None], proj_grad)


def solution(mesh):
    return jax.shard_map(
        body,
        mesh=mesh,
        in_specs=(
            P("slide", ("seq", "fsdp"), None),
            P("fsdp", None),
            P(),
            P("slide", ("seq", "fsdp"), None),
            P("slide"),
            P(),
            P(),
            P("fsdp", None),
            P("fsdp", None),
            P("fsdp", None),
        ),
        out_specs=(P("slide", "seq", None), P("slide", ("seq", "fsdp"), None), P("fsdp", None)),
        check_vma=False,
    )
```

```python
import functools

import jax
import jax.numpy as jnp
from jax import lax
from jax.experimental import pallas as pl
from jax.experimental.pallas import tpu as pltpu
from jax.sharding import PartitionSpec as P

HS = 48
NX, NZ, NY = 4, 8, 4
Z_GROUPS = [[z * NY + y for z in range(NZ)] for y in range(NY)]
Y_GROUPS = [[z * NY + y for y in range(NY)] for z in range(NZ)]
SWAP = [(0, 1), (1, 0)]
F32, BF16 = jnp.float32, jnp.bfloat16
VMEM = pl.BlockSpec(memory_space=pltpu.VMEM)
SMEM = pl.BlockSpec(memory_space=pltpu.SMEM)
ANY = pl.BlockSpec(memory_space=pl.ANY)
CONTRACT_LAST = (((1,), (1,)), ((), ()))
CONTRACT_FIRST = (((0,), (0,)), ((), ()))
dot = functools.partial(jnp.dot, preferred_element_type=F32)
dot_general = functools.partial(lax.dot_general, preferred_element_type=F32)


def a2a_z(v):
    return lax.all_to_all(v, "fsdp", 0, 0, axis_index_groups=Z_GROUPS)


def a2a_y(v):
    return lax.all_to_all(v, "fsdp", 0, 0, axis_index_groups=Y_GROUPS)


def copies(v, n):
    return jnp.broadcast_to(v[None], (n,) + v.shape)


def swap(v):
    return lax.ppermute(v, "seq", SWAP)


def shift_y(v, k):
    return lax.ppermute(
        v, "fsdp", [(z * NY + y, z * NY + (y + k) % NY) for z in range(NZ) for y in range(NY)]
    )


def shift_z(v, k):
    return lax.ppermute(
        v, "fsdp", [(z * NY + y, (z + k) % NZ * NY + y) for z in range(NZ) for y in range(NY)]
    )


def shift_x(v, k):
    return lax.ppermute(v, "slide", [(x, (x + k) % NX) for x in range(NX)])


def after(v, other):
    return v + (other[(0,) * other.ndim].astype(F32) * 0).astype(v.dtype)


def params(mib):
    return pltpu.CompilerParams(vmem_limit_bytes=mib * 1024 * 1024)


def cost(gflop, mb, mexp=0):
    return pl.CostEstimate(
        flops=int(gflop * 1e9), bytes_accessed=int(mb * 1e6), transcendentals=int(mexp * 1e6)
    )


def forward_kernel(tiles, at_ref, tok_ref, pm_ref, po_ref, gain_ref, out_ref, nm_ref, no_ref, inv_ref):
    tok = tok_ref[...]
    mixed = [dot(tok, pm_ref[...]), dot(tok, po_ref[...])]
    rows, half = mixed[0].shape
    centre = sum(jnp.sum(m, axis=-1, keepdims=True) for m in mixed) * (0.5 / half)
    shifted = [m - centre for m in mixed]
    var = sum(jnp.sum(m * m, axis=-1, keepdims=True) for m in shifted) * (0.5 / half)
    inv_std = lax.rsqrt(var + 1e-06)
    inv_ref[...] = jnp.broadcast_to(inv_std, inv_ref.shape)
    pooled = []
    for i, (m, n_ref) in enumerate(zip(shifted, (nm_ref, no_ref))):
        n = m * inv_std
        n_ref[...] = n
        mean = jnp.sum(n.reshape(tiles, rows // tiles, half), axis=1) * (tiles / rows)
        pooled.append(mean * gain_ref[i : i + 1, :])
    span = pl.ds(pl.multiple_of(pl.program_id(0) * tiles, tiles), tiles)
    for s in range(2):

        @pl.when(at_ref[0] == s)
        def _():
            out_ref[span, :half] = pooled[s]
            out_ref[span, half:] = pooled[1 - s]


def forward(at, tokens, pm, po, gain, tiles):
    rows, aw = tokens.shape
    half = pm.shape[1]
    steps = 2
    spec = pl.BlockSpec((rows // steps, half), lambda i: (i, 0))
    return pl.pallas_call(
        functools.partial(forward_kernel, tiles // steps),
        out_shape=(
            jax.ShapeDtypeStruct((tiles, 2 * half), F32),
            jax.ShapeDtypeStruct((rows, half), F32),
            jax.ShapeDtypeStruct((rows, half), F32),
            jax.ShapeDtypeStruct((rows, 128), F32),
        ),
        grid=(steps,),
        in_specs=[SMEM, pl.BlockSpec((rows // steps, aw), lambda i: (i, 0)), VMEM, VMEM, VMEM],
        out_specs=(
            pl.BlockSpec((tiles, 2 * half), lambda i: (0, 0)),
            spec,
            spec,
            pl.BlockSpec((rows // steps, 128), lambda i: (i, 0)),
        ),
        compiler_params=params(48),
        cost_estimate=cost(2.4, 10),
        name="forward",
    )(at, tokens, pm, po, gain)


def backward_kernel(_, tok_ref, nm_ref, no_ref, inv_ref, gm_ref, go_ref, pm_ref, po_ref, grad_ref, tm_ref, to_ref, am_ref, ao_ref):
    step, steps = pl.program_id(0), pl.num_programs(0)
    tok = tok_ref[...]
    normed = [nm_ref[...], no_ref[...]]
    inv_std = inv_ref[:, :1]
    rows, half = normed[0].shape
    tiles = gm_ref.shape[1]
    grads = [gm_ref[0], go_ref[0]]
    mean = sum(jnp.sum(g, axis=-1, keepdims=True) for g in grads) * (0.5 / half)

    def per_token(v):
        return jnp.broadcast_to(v[:, None, :], (tiles, rows // tiles, v.shape[1])).reshape(rows, v.shape[1])

    along = sum(jnp.sum(per_token(g) * n, axis=-1, keepdims=True) for g, n in zip(grads, normed)) * (0.5 / half)
    mixed = [(inv_std * (per_token(g - mean) - n * along)).astype(BF16) for g, n in zip(grads, normed)]
    for acc_ref, term_ref, m in ((am_ref, tm_ref, mixed[0]), (ao_ref, to_ref, mixed[1])):
        term = dot_general(tok, m, CONTRACT_FIRST)

        @pl.when(step == 0)
        def _():
            acc_ref[...] = term

        @pl.when(step > 0)
        def _():
            acc_ref[...] += term

        @pl.when(step == steps - 1)
        def _():
            block = term_ref.shape[2]
            for z in range(NZ):
                for y in range(NY):
                    term_ref[y, z] = acc_ref[pl.ds((z * NY + y) * block, block), :].astype(BF16)

    grad = dot_general(mixed[0], pm_ref[...], CONTRACT_LAST) + dot_general(mixed[1], po_ref[...], CONTRACT_LAST)
    grad_ref[...] = grad.astype(BF16)


def backward(before, tokens, nm, no, inv_std, grads, pm, po):
    rows, aw = tokens.shape
    half = nm.shape[1]
    tiles = grads[0].shape[0]
    steps = 2
    grads = [g.reshape(steps, tiles // steps, half) for g in grads]
    gspec = pl.BlockSpec((1, tiles // steps, half), lambda i: (i, 0, 0))
    tspec = pl.BlockSpec((NY, NZ, aw // (NY * NZ), half), lambda i: (0, 0, 0, 0))
    term = jax.ShapeDtypeStruct((NY, NZ, aw // (NY * NZ), half), BF16)
    wide = pl.BlockSpec((rows // steps, half), lambda i: (i, 0))
    return pl.pallas_call(
        backward_kernel,
        out_shape=(jax.ShapeDtypeStruct((rows, aw), BF16), term, term),
        grid=(steps,),
        in_specs=[
            ANY,
            pl.BlockSpec((rows // steps, aw), lambda i: (i, 0)),
            wide,
            wide,
            pl.BlockSpec((rows // steps, 128), lambda i: (i, 0)),
            gspec,
            gspec,
            VMEM,
            VMEM,
        ],
        out_specs=(pl.BlockSpec((rows // steps, aw), lambda i: (i, 0)), tspec, tspec),
        scratch_shapes=[pltpu.VMEM((aw, half), F32), pltpu.VMEM((aw, half), F32)],
        compiler_params=params(56),
        cost_estimate=cost(2.4, 16),
        name="backward",
    )(before, tokens, nm, no, inv_std, *grads, pm, po)


def pair_sum_kernel(at_ref, mine_ref, other_ref, *out_refs):
    for k, out_ref in enumerate(out_refs):
        y = lax.rem(at_ref[1] + k, NY)
        for z in range(NZ):
            out_ref[z] = (mine_ref[y, z].astype(F32) + other_ref[y, z].astype(F32)).astype(BF16)


def pair_sum(at, mine, other):
    return pl.pallas_call(
        pair_sum_kernel,
        out_shape=[jax.ShapeDtypeStruct(mine.shape[1:], BF16)] * NY,
        in_specs=[SMEM, VMEM, VMEM],
        out_specs=[VMEM] * NY,
        compiler_params=params(32),
        cost_estimate=cost(0.001, 0.1),
        name="pair_sum",
    )(at, mine, other)


def sum_kernel(n, *refs):
    if refs[0].shape == refs[-1].shape:
        parts = [ref[...] for ref in refs[:n]]
    else:
        parts = [refs[0][z] for z in range(refs[0].shape[0])]
    refs[-1][...] = sum(part.astype(F32) for part in parts).astype(BF16)


def sum_of(name, before, parts, gflop=0.001):
    if isinstance(parts, jax.Array):
        parts = [parts]
        shape = parts[0].shape[1:]
    else:
        shape = parts[0].shape
    return pl.pallas_call(
        functools.partial(sum_kernel, len(parts)),
        out_shape=jax.ShapeDtypeStruct(shape, BF16),
        in_specs=[VMEM] * len(parts) + [ANY] * len(before),
        out_specs=VMEM,
        compiler_params=params(32),
        cost_estimate=cost(gflop, 0.1),
        name=name,
    )(*parts, *before)


def by_z_kernel(at_ref, *refs):
    for k, ref in enumerate(refs[:-1]):
        refs[-1][lax.rem(at_ref[4] + NZ - k, NZ)] = ref[...]


def by_z(at, pieces):
    return pl.pallas_call(
        by_z_kernel,
        out_shape=jax.ShapeDtypeStruct((NZ,) + pieces[0].shape, BF16),
        in_specs=[SMEM] + [VMEM] * NZ,
        out_specs=VMEM,
        compiler_params=params(32),
        cost_estimate=cost(0.001, 0.1),
        name="by_z",
    )(at, *pieces)


def arrange_kernel(at_ref, in_ref, *refs):
    proj_ref, heads_ref = refs[-2:]
    for y in range(NY):
        for z in range(NZ):
            proj_ref[z, y] = in_ref[y, z]
    for i in range(2):
        heads_ref[i] = in_ref[2 * at_ref[0] + i, NZ]


def arrange(at, gathered, before):
    block = gathered.shape[2:]
    return pl.pallas_call(
        arrange_kernel,
        out_shape=(jax.ShapeDtypeStruct((NZ, NY) + block, BF16), jax.ShapeDtypeStruct((2,) + block, BF16)),
        in_specs=[SMEM, VMEM] + [ANY] * len(before),
        out_specs=(VMEM, VMEM),
        compiler_params=params(32),
        cost_estimate=cost(0.001, 0.1),
        name="arrange",
    )(at, gathered, *before)


def by_y_kernel(cuts, at_ref, *refs):
    for k, ref in enumerate(refs[:NY]):
        y = lax.rem(at_ref[1] + NY - k, NY)
        for (start, stop), out_ref in zip(cuts, refs[NY:]):
            for z in range(NZ):
                out_ref[z, y] = ref[z, start:stop, :]


def by_y(at, pieces, *sizes):
    zs, _, cols = pieces[0].shape
    stops = [sum(sizes[: i + 1]) for i in range(len(sizes))]
    cuts = [(stop - size, stop) for stop, size in zip(stops, sizes)]
    return pl.pallas_call(
        functools.partial(by_y_kernel, cuts),
        out_shape=[jax.ShapeDtypeStruct((zs, NY, size, cols), BF16) for size in sizes],
        in_specs=[SMEM] + [VMEM] * NY,
        out_specs=[VMEM] * len(sizes),
        compiler_params=params(32),
        cost_estimate=cost(0.01, 1),
        name="by_y",
    )(at, *pieces)


def place(row, s):
    return s * 512 + ((row // 16) % NZ * NY + row // (16 * NZ)) * 16 + row % 16


def bias_kernel(heads, at_ref, seg_ref, dil_ref, out_ref, done_ref, q_ref, k_ref):
    s, y, count = at_ref[0], at_ref[1], at_ref[2]
    rows = q_ref.shape[0]
    span = 128 // heads

    def fill(ref, pos, valid):
        lane = lax.broadcasted_iota(jnp.int32, pos.shape, 1)
        column, head = lane & (span - 1), y * heads + lax.shift_right_logical(lane, jnp.full_like(lane, 5))
        hits = None
        for c in range(seg_ref.shape[0]):
            width = seg_ref[c]
            bits = 6 + sum((width > 64 << b).astype(jnp.int32) for b in range(4))
            first = lax.shift_right_logical(jnp.int32(2 * rows), bits)
            ids = first + lax.shift_right_logical(pos, jnp.full_like(pos, bits))
            hit = (ids == column) & (((pos ^ head) & (dil_ref[c] - 1)) == 0)
            hits = hit if hits is None else hits | hit
        ref[...] = jnp.where(hits & valid, 1.0, 0.0).astype(BF16)

    h = pl.program_id(0)

    @pl.when(h == 0)
    def _():
        row = lax.broadcasted_iota(jnp.int32, (rows, 128), 0)
        pos = place(row, s)
        fill(q_ref, pos, pos >= 0)
        row = lax.broadcasted_iota(jnp.int32, (2 * rows, 128), 0)
        pos = place(row % rows, row // rows)
        fill(k_ref, pos, pos < count)
        done_ref[...] = jnp.zeros_like(done_ref)

    block = 128
    of_head = lax.broadcasted_iota(jnp.int32, (1, 128), 1) // span == h
    for start in range(0, rows, block):
        span_rows = pl.ds(start, block)
        queries = jnp.where(of_head, q_ref[span_rows, :], 0).astype(BF16)
        counted = dot_general(queries, k_ref[...], CONTRACT_LAST)
        out_ref[0, span_rows, :] = jnp.where(counted > 0.5, jnp.log2(jnp.maximum(counted, 1.0)), -1e30)


def biases(at, seg_lengths, dilation, heads, rows):
    return pl.pallas_call(
        functools.partial(bias_kernel, heads),
        out_shape=(jax.ShapeDtypeStruct((heads, rows, 2 * rows), F32), jax.ShapeDtypeStruct((8, 128), F32)),
        grid=(heads,),
        in_specs=[SMEM] * 3,
        out_specs=(
            pl.BlockSpec((1, rows, 2 * rows), lambda h: (h, 0, 0)),
            pl.BlockSpec((8, 128), lambda h: (0, 0)),
        ),
        scratch_shapes=[pltpu.VMEM((rows, 128), BF16), pltpu.VMEM((2 * rows, 128), BF16)],
        compiler_params=params(60),
        cost_estimate=cost(1, 1),
        name="biases",
    )(at, seg_lengths, dilation)


def spread_kernel(common_ref, own_ref, _, out_ref):
    blocks = common_ref.shape[0]
    for y in range(NY):
        out_ref[y, :blocks] = common_ref[...]
        out_ref[y, blocks] = own_ref[y]


def spread(common, own, before):
    return pl.pallas_call(
        spread_kernel,
        out_shape=jax.ShapeDtypeStruct((NY, common.shape[0] + 1) + common.shape[1:], BF16),
        in_specs=[VMEM, VMEM, ANY],
        out_specs=VMEM,
        compiler_params=params(32),
        cost_estimate=cost(0.001, 0.1),
        name="spread",
    )(common, own, before)


def attend_kernel(at_ref, hm_ref, ho_ref, wm_ref, wo_ref, bias_ref, *refs):
    out_ref, w_ref, q_ref, k_ref, v_ref = refs[-5:]
    s = at_ref[0]
    rows = hm_ref.shape[0]
    half = hm_ref.shape[1] // 2
    heads, block, keys = bias_ref.shape
    seg = q_ref.shape[2]

    @pl.when(pl.program_id(0) == 0)
    def _():
        for z in range(NZ):
            w_ref[z, s] = wm_ref[z]
            w_ref[z, 1 - s] = wo_ref[z]
        w_mine = w_ref[pl.ds(s * (NZ // 2), NZ // 2)].reshape(half, w_ref.shape[3])
        w_other = w_ref[pl.ds((1 - s) * (NZ // 2), NZ // 2)].reshape(half, w_ref.shape[3])
        for core in range(2):
            lanes = slice(core * half, (core + 1) * half)
            all_parts = dot(hm_ref[:, lanes], w_mine) + dot(ho_ref[:, lanes], w_other)
            span = pl.ds(core * rows, rows)
            q_ref[core] = all_parts[:, :seg].astype(BF16)
            k_ref[span, :] = all_parts[:, seg : 2 * seg].astype(BF16)
            v_ref[span, :] = all_parts[:, 2 * seg :].astype(BF16)

    lane_head = lax.broadcasted_iota(jnp.int32, (1, seg), 1) // HS
    scale = HS ** (-0.5) * 1.4426950408889634
    queries = q_ref[s, pl.ds(pl.multiple_of(pl.program_id(0) * block, block), block), :]
    queries = jnp.concatenate([jnp.where(lane_head == h, queries, 0).astype(BF16) for h in range(heads)])
    scores = dot_general(queries, k_ref[...], CONTRACT_LAST)
    scores = scores * scale + bias_ref[...].reshape(heads * block, keys)
    weights = jnp.exp2(scores - jnp.max(scores, axis=-1, keepdims=True))
    total = jnp.sum(weights, axis=-1, keepdims=True)
    part = dot(weights.astype(BF16), v_ref[...]) * (1.0 / total)
    for h in range(heads):
        turned = part[h * block : (h + 1) * block].T
        out_ref[h * HS : (h + 1) * HS, :] = turned[h * HS : (h + 1) * HS].astype(BF16)


def attend(at, hm, ho, wm, wo, bias, before):
    heads, rows, keys = bias.shape
    seg = wm.shape[2] // 3
    block = 128
    return pl.pallas_call(
        attend_kernel,
        out_shape=jax.ShapeDtypeStruct((heads * HS, rows), BF16),
        grid=(rows // block,),
        in_specs=[SMEM] + [VMEM] * 4 + [pl.BlockSpec((heads, block, keys), lambda i: (0, i, 0))] + [ANY] * len(before),
        out_specs=pl.BlockSpec((heads * HS, block), lambda i: (0, i)),
        scratch_shapes=[
            pltpu.VMEM((NZ, 2) + wm.shape[1:], BF16),
            pltpu.VMEM((2, rows, seg), BF16),
            pltpu.VMEM((keys, seg), BF16),
            pltpu.VMEM((keys, seg), BF16),
        ],
        compiler_params=params(48),
        cost_estimate=cost(8, 12, 2),
        name="attend",
    )(at, hm, ho, wm, wo, bias, *before)


def finish_kernel(at_ref, a0_ref, a1_ref, a2_ref, a3_ref, wm_ref, wo_ref, hm_ref, ho_ref, out_ref):
    s, y, count = at_ref[0], at_ref[1], at_ref[2]
    rows, half = hm_ref.shape[0], hm_ref.shape[1] // 2
    tiles = out_ref.shape[2]
    mine = other = 0.0
    for k, att_ref in enumerate((a0_ref, a1_ref, a2_ref, a3_ref)):
        depth = att_ref.shape[0]
        span = pl.ds(pl.multiple_of(lax.rem(y + NY - k, NY) * depth, depth), depth)
        mine = mine + dot_general(att_ref[...], wm_ref[span, :], CONTRACT_FIRST)
        other = other + dot_general(att_ref[...], wo_ref[span, :], CONTRACT_FIRST)
    lanes = pl.ds(pl.multiple_of(s * half, half), half)
    mine = mine + hm_ref[:, lanes].astype(F32)
    other = other + ho_ref[:, lanes].astype(F32)
    row = lax.broadcasted_iota(jnp.int32, (rows, half), 0)
    valid = place(row, s) < count
    left = jnp.where(valid, jnp.where(s == 0, mine, other), 0.0).astype(BF16)
    right = jnp.where(valid, jnp.where(s == 0, other, mine), 0.0).astype(BF16)
    span = NZ * tiles
    for y in range(NY):
        for part, lanes in ((left, slice(0, half)), (right, slice(half, 2 * half))):
            out_ref[:, y, :, lanes] = part[y * span : (y + 1) * span].reshape(NZ, tiles, half)


def finish(at, att, wm, wo, hm, ho, tiles):
    return pl.pallas_call(
        finish_kernel,
        out_shape=jax.ShapeDtypeStruct((NZ, NY, tiles, hm.shape[1]), BF16),
        in_specs=[SMEM] + [VMEM] * 8,
        out_specs=VMEM,
        compiler_params=params(32),
        cost_estimate=cost(0.6, 4),
        name="finish",
    )(at, *att, wm, wo, hm, ho)


def body(
    head_out,
    proj_weight,
    norm_gain,
    embed_cot,
    tile_counts,
    seg_lengths,
    dilation,
    embed_weight,
    qkv_weight,
    out_weight,
):
    tokens = head_out[0]
    n_rows, aw = tokens.shape
    dt = proj_weight.shape[1]
    half = dt // 2
    tiles = embed_cot.shape[1]
    per_tile = n_rows // tiles
    fsdp = NZ * NY
    f = lax.axis_index("fsdp")
    s = lax.axis_index("seq")
    y = f % NY
    count = tile_counts[0]
    ds = out_weight.shape[1]
    shard_len = fsdp * tiles
    x = lax.axis_index("slide")
    at = jnp.stack([s, y, count, x, f // NY]).astype(jnp.int32)
    dslice = lax.dynamic_slice_in_dim
    heads = ds // HS // NY
    width = heads * HS

    def of_y(v, k):
        return lax.dynamic_index_in_dim(v, (y + k) % NY, 0, keepdims=False)

    bias, zero = biases(at, seg_lengths, dilation, heads, shard_len)

    rows = proj_weight.shape[0]
    w_heads = qkv_weight.reshape(rows, 3, NY, width).transpose(2, 0, 1, 3)
    w_heads = jnp.pad(w_heads, ((0, 0), (0, 0), (0, 0), (0, 256 - width))).reshape(NY, rows, 3 * 256)

    quarter = ds // 2
    first = a2a_z(copies(dslice(proj_weight, s * half, half, 1), NZ))
    others = jnp.concatenate([dslice(w, s * quarter, quarter, 1) for w in (embed_weight, out_weight)])
    others = after(others, first)
    others = [others] + [shift_z(others, k) for k in range(1, NZ)]
    gathered = a2a_y(spread(first, w_heads, zero))
    proj_mine, w_heads = arrange(at, gathered, others[1:])
    proj_mine, w_heads = proj_mine.reshape(aw, half), w_heads.reshape(2 * rows, half)
    proj_other = swap(proj_mine)
    others = by_z(at, others)
    others = [others] + [shift_y(others, k) for k in range(1, NY)]

    def halves(v):
        return dslice(v, s * half, half, v.ndim - 1), dslice(v, (1 - s) * half, half, v.ndim - 1)

    gain = halves(norm_gain)
    embed, normed_mine, normed_other, inv_std = forward(at, tokens, proj_mine, proj_other, jnp.stack(gain), tiles)
    embed = embed.astype(BF16)
    embed_other = swap(embed)
    embed = jnp.concatenate([jnp.where(s == 0, embed, embed_other), jnp.where(s == 0, embed_other, embed)])

    base = (s * fsdp + f) * tiles
    valid = (base + jnp.arange(tiles, dtype=jnp.int32) < count).astype(F32)
    grads = [c * valid[:, None] / per_tile * g for c, g in zip(halves(embed_cot[0].astype(F32)), gain)]

    w_embed, w_out = by_y(at, others, 2 * rows, rows)
    w_embed, w_out = w_embed.reshape(dt, quarter), w_out.reshape(ds, quarter)
    w_out_other = swap(w_out)
    hidden = dot(embed, w_embed).astype(BF16)
    hidden = jnp.concatenate([hidden[:tiles], hidden[tiles:]], axis=1)
    head_out_grad, term_mine, term_other = backward(
        hidden, tokens, normed_mine, normed_other, inv_std, grads, proj_mine, proj_other
    )
    second = a2a_z(copies(jnp.concatenate([hidden, w_heads]), NZ))

    parts = pair_sum(at, term_mine, swap(term_other))
    hidden = a2a_y(copies(after(second[:, :tiles], parts[0]), NY)).reshape(shard_len, ds)
    hidden_other = swap(hidden)
    parts = [parts[0]] + [shift_y(parts[k], k) for k in range(1, NY)]
    share = a2a_z(sum_of("y_sum", [hidden], parts, 6))

    w_heads = second[:, tiles:]
    w_heads_other = swap(w_heads)
    attended = attend(at, hidden, hidden_other, w_heads, w_heads_other, bias, [])
    received = [attended] + [shift_y(attended, k) for k in range(1, NY)]
    share = sum_of("z_sum", [attended], share)
    parts = [share] + [shift_x(share, k) for k in range(1, NX)]
    slide_out = finish(at, received, w_out, w_out_other, hidden, hidden_other, tiles)
    share = sum_of("x_sum", [slide_out], parts)
    other = swap(share)
    slide_out = slide_out.reshape(1, shard_len, ds)
    proj_grad = jnp.concatenate([jnp.where(s == 0, share, other), jnp.where(s == 0, other, share)], axis=1)
    return (slide_out, head_out_grad[None], proj_grad)


def solution(mesh):
    return jax.shard_map(
        body,
        mesh=mesh,
        in_specs=(
            P("slide", ("seq", "fsdp"), None),
            P("fsdp", None),
            P(),
            P("slide", ("seq", "fsdp"), None),
            P("slide"),
            P(),
            P(),
            P("fsdp", None),
            P("fsdp", None),
            P("fsdp", None),
        ),
        out_specs=(P("slide", "seq", None), P("slide", ("seq", "fsdp"), None), P("fsdp", None)),
        check_vma=False,
    )
```

```python
import functools

import jax
import jax.numpy as jnp
from jax import lax
from jax.experimental import pallas as pl
from jax.experimental.pallas import tpu as pltpu
from jax.sharding import PartitionSpec as P

HS = 48
NX, NZ, NY = 4, 8, 4
Z_GROUPS = [[z * NY + y for z in range(NZ)] for y in range(NY)]
Y_GROUPS = [[z * NY + y for y in range(NY)] for z in range(NZ)]
SWAP = [(0, 1), (1, 0)]
F32, BF16 = jnp.float32, jnp.bfloat16
VMEM = pl.BlockSpec(memory_space=pltpu.VMEM)
SMEM = pl.BlockSpec(memory_space=pltpu.SMEM)
ANY = pl.BlockSpec(memory_space=pl.ANY)
CONTRACT_LAST = (((1,), (1,)), ((), ()))
CONTRACT_FIRST = (((0,), (0,)), ((), ()))
dot = functools.partial(jnp.dot, preferred_element_type=F32)
dot_general = functools.partial(lax.dot_general, preferred_element_type=F32)


def a2a_z(v):
    return lax.all_to_all(v, "fsdp", 0, 0, axis_index_groups=Z_GROUPS)


def a2a_y(v):
    return lax.all_to_all(v, "fsdp", 0, 0, axis_index_groups=Y_GROUPS)


def copies(v, n):
    return jnp.broadcast_to(v[None], (n,) + v.shape)


def swap(v):
    return lax.ppermute(v, "seq", SWAP)


def shift_y(v, k):
    return lax.ppermute(
        v, "fsdp", [(z * NY + y, z * NY + (y + k) % NY) for z in range(NZ) for y in range(NY)]
    )


def shift_z(v, k):
    return lax.ppermute(
        v, "fsdp", [(z * NY + y, (z + k) % NZ * NY + y) for z in range(NZ) for y in range(NY)]
    )


def shift_x(v, k):
    return lax.ppermute(v, "slide", [(x, (x + k) % NX) for x in range(NX)])


def after(v, other):
    return v + (other[(0,) * other.ndim].astype(F32) * 0).astype(v.dtype)


def params(mib):
    return pltpu.CompilerParams(vmem_limit_bytes=mib * 1024 * 1024)


def cost(gflop, mb, mexp=0):
    return pl.CostEstimate(
        flops=int(gflop * 1e9), bytes_accessed=int(mb * 1e6), transcendentals=int(mexp * 1e6)
    )


def forward_kernel(tiles, at_ref, tok_ref, pm_ref, po_ref, gain_ref, out_ref, nm_ref, no_ref, inv_ref):
    tok = tok_ref[...]
    mixed = [dot(tok, pm_ref[...]), dot(tok, po_ref[...])]
    rows, half = mixed[0].shape
    centre = sum(jnp.sum(m, axis=-1, keepdims=True) for m in mixed) * (0.5 / half)
    shifted = [m - centre for m in mixed]
    var = sum(jnp.sum(m * m, axis=-1, keepdims=True) for m in shifted) * (0.5 / half)
    inv_std = lax.rsqrt(var + 1e-06)
    inv_ref[...] = jnp.broadcast_to(inv_std, inv_ref.shape)
    pooled = []
    for i, (m, n_ref) in enumerate(zip(shifted, (nm_ref, no_ref))):
        n = m * inv_std
        n_ref[...] = n
        mean = jnp.sum(n.reshape(tiles, rows // tiles, half), axis=1) * (tiles / rows)
        pooled.append(mean * gain_ref[i : i + 1, :])
    span = pl.ds(pl.multiple_of(pl.program_id(0) * tiles, tiles), tiles)
    for s in range(2):

        @pl.when(at_ref[0] == s)
        def _():
            out_ref[span, :half] = pooled[s]
            out_ref[span, half:] = pooled[1 - s]


def forward(at, tokens, pm, po, gain, tiles):
    rows, aw = tokens.shape
    half = pm.shape[1]
    steps = 2
    spec = pl.BlockSpec((rows // steps, half), lambda i: (i, 0))
    return pl.pallas_call(
        functools.partial(forward_kernel, tiles // steps),
        out_shape=(
            jax.ShapeDtypeStruct((tiles, 2 * half), F32),
            jax.ShapeDtypeStruct((rows, half), F32),
            jax.ShapeDtypeStruct((rows, half), F32),
            jax.ShapeDtypeStruct((rows, 128), F32),
        ),
        grid=(steps,),
        in_specs=[SMEM, pl.BlockSpec((rows // steps, aw), lambda i: (i, 0)), VMEM, VMEM, VMEM],
        out_specs=(
            pl.BlockSpec((tiles, 2 * half), lambda i: (0, 0)),
            spec,
            spec,
            pl.BlockSpec((rows // steps, 128), lambda i: (i, 0)),
        ),
        compiler_params=params(32),
        cost_estimate=cost(2.4, 10),
        name="forward",
    )(at, tokens, pm, po, gain)


def backward_kernel(_, tok_ref, nm_ref, no_ref, inv_ref, gm_ref, go_ref, xm_ref, xo_ref, tm_ref, to_ref, am_ref, ao_ref):
    step, steps = pl.program_id(0), pl.num_programs(0)
    tok = tok_ref[...]
    normed = [nm_ref[...], no_ref[...]]
    inv_std = inv_ref[:, :1]
    rows, half = normed[0].shape
    tiles = gm_ref.shape[1]
    grads = [gm_ref[0], go_ref[0]]
    mean = sum(jnp.sum(g, axis=-1, keepdims=True) for g in grads) * (0.5 / half)

    def per_token(v):
        return jnp.broadcast_to(v[:, None, :], (tiles, rows // tiles, v.shape[1])).reshape(rows, v.shape[1])

    along = sum(jnp.sum(per_token(g) * n, axis=-1, keepdims=True) for g, n in zip(grads, normed)) * (0.5 / half)
    mixed = [(inv_std * (per_token(g - mean) - n * along)).astype(BF16) for g, n in zip(grads, normed)]
    xm_ref[...] = mixed[0]
    xo_ref[...] = mixed[1]
    for acc_ref, term_ref, m in ((am_ref, tm_ref, mixed[0]), (ao_ref, to_ref, mixed[1])):
        term = dot_general(tok, m, CONTRACT_FIRST)

        @pl.when(step == 0)
        def _():
            acc_ref[...] = term

        @pl.when(step > 0)
        def _():
            acc_ref[...] += term

        @pl.when(step == steps - 1)
        def _():
            block = term_ref.shape[2]
            for z in range(NZ):
                for y in range(NY):
                    term_ref[y, z] = acc_ref[pl.ds((z * NY + y) * block, block), :].astype(BF16)


def backward(before, tokens, nm, no, inv_std, grads):
    rows, aw = tokens.shape
    half = nm.shape[1]
    tiles = grads[0].shape[0]
    steps = 2
    grads = [g.reshape(steps, tiles // steps, half) for g in grads]
    gspec = pl.BlockSpec((1, tiles // steps, half), lambda i: (i, 0, 0))
    tspec = pl.BlockSpec((NY, NZ, aw // (NY * NZ), half), lambda i: (0, 0, 0, 0))
    term = jax.ShapeDtypeStruct((NY, NZ, aw // (NY * NZ), half), BF16)
    wide = pl.BlockSpec((rows // steps, half), lambda i: (i, 0))
    mixed = jax.ShapeDtypeStruct((rows, half), BF16)
    return pl.pallas_call(
        backward_kernel,
        out_shape=(mixed, mixed, term, term),
        grid=(steps,),
        in_specs=[
            ANY,
            pl.BlockSpec((rows // steps, aw), lambda i: (i, 0)),
            wide,
            wide,
            pl.BlockSpec((rows // steps, 128), lambda i: (i, 0)),
            gspec,
            gspec,
        ],
        out_specs=(wide, wide, tspec, tspec),
        scratch_shapes=[pltpu.VMEM((aw, half), F32), pltpu.VMEM((aw, half), F32)],
        compiler_params=params(40),
        cost_estimate=cost(2.4, 16),
        name="backward",
    )(before, tokens, nm, no, inv_std, *grads)


def head_out_grad_kernel(at_ref, xm_ref, xo_ref, pm_ref, po_ref, out_ref, done_ref):
    done_ref[...] = jnp.zeros_like(done_ref)
    grad = dot_general(xm_ref[...], pm_ref[...], CONTRACT_LAST) + dot_general(xo_ref[...], po_ref[...], CONTRACT_LAST)
    out_ref[...] = grad.astype(BF16)


def head_out_grad_of(at, xm, xo, pm, po):
    rows, half = xm.shape
    aw = pm.shape[0]
    steps = 2
    spec = pl.BlockSpec((rows // steps, half), lambda i: (i, 0))
    return pl.pallas_call(
        head_out_grad_kernel,
        out_shape=(jax.ShapeDtypeStruct((rows, aw), BF16), jax.ShapeDtypeStruct((8, 128), F32)),
        grid=(steps,),
        in_specs=[SMEM, spec, spec, VMEM, VMEM],
        out_specs=(
            pl.BlockSpec((rows // steps, aw), lambda i: (i, 0)),
            pl.BlockSpec((8, 128), lambda i: (0, 0)),
        ),
        compiler_params=params(32),
        cost_estimate=cost(0.01, 0.1),
        name="head_out_grad",
    )(at, xm, xo, pm, po)


def pair_sum_kernel(at_ref, mine_ref, other_ref, *out_refs):
    for k, out_ref in enumerate(out_refs):
        y = lax.rem(at_ref[1] + k, NY)
        for z in range(NZ):
            out_ref[z] = (mine_ref[y, z].astype(F32) + other_ref[y, z].astype(F32)).astype(BF16)


def pair_sum(at, mine, other):
    return pl.pallas_call(
        pair_sum_kernel,
        out_shape=[jax.ShapeDtypeStruct(mine.shape[1:], BF16)] * NY,
        in_specs=[SMEM, VMEM, VMEM],
        out_specs=[VMEM] * NY,
        compiler_params=params(32),
        cost_estimate=cost(0.001, 0.1),
        name="pair_sum",
    )(at, mine, other)


def sum_kernel(n, *refs):
    if refs[0].shape == refs[-1].shape:
        parts = [ref[...] for ref in refs[:n]]
    else:
        parts = [refs[0][z] for z in range(refs[0].shape[0])]
    refs[-1][...] = sum(part.astype(F32) for part in parts).astype(BF16)


def sum_of(name, before, parts, gflop=0.001):
    if isinstance(parts, jax.Array):
        parts = [parts]
        shape = parts[0].shape[1:]
    else:
        shape = parts[0].shape
    return pl.pallas_call(
        functools.partial(sum_kernel, len(parts)),
        out_shape=jax.ShapeDtypeStruct(shape, BF16),
        in_specs=[VMEM] * len(parts) + [ANY] * len(before),
        out_specs=VMEM,
        compiler_params=params(32),
        cost_estimate=cost(gflop, 0.1),
        name=name,
    )(*parts, *before)


def by_z_kernel(at_ref, *refs):
    for k, ref in enumerate(refs[:-1]):
        refs[-1][lax.rem(at_ref[4] + NZ - k, NZ)] = ref[...]


def by_z(at, pieces):
    return pl.pallas_call(
        by_z_kernel,
        out_shape=jax.ShapeDtypeStruct((NZ,) + pieces[0].shape, BF16),
        in_specs=[SMEM] + [VMEM] * NZ,
        out_specs=VMEM,
        compiler_params=params(32),
        cost_estimate=cost(0.001, 0.1),
        name="by_z",
    )(at, *pieces)


def arrange_kernel(at_ref, in_ref, *refs):
    proj_ref, heads_ref = refs[-2:]
    for y in range(NY):
        for z in range(NZ):
            proj_ref[z, y] = in_ref[y, z]
    for i in range(2):
        heads_ref[i] = in_ref[2 * at_ref[0] + i, NZ]


def arrange(at, gathered, before):
    block = gathered.shape[2:]
    return pl.pallas_call(
        arrange_kernel,
        out_shape=(jax.ShapeDtypeStruct((NZ, NY) + block, BF16), jax.ShapeDtypeStruct((2,) + block, BF16)),
        in_specs=[SMEM, VMEM] + [ANY] * len(before),
        out_specs=(VMEM, VMEM),
        compiler_params=params(32),
        cost_estimate=cost(0.001, 0.1),
        name="arrange",
    )(at, gathered, *before)


def by_y_kernel(cuts, at_ref, *refs):
    for k, ref in enumerate(refs[:NY]):
        y = lax.rem(at_ref[1] + NY - k, NY)
        for (start, stop), out_ref in zip(cuts, refs[NY:]):
            for z in range(NZ):
                out_ref[z, y] = ref[z, start:stop, :]


def by_y(at, pieces, *sizes):
    zs, _, cols = pieces[0].shape
    stops = [sum(sizes[: i + 1]) for i in range(len(sizes))]
    cuts = [(stop - size, stop) for stop, size in zip(stops, sizes)]
    return pl.pallas_call(
        functools.partial(by_y_kernel, cuts),
        out_shape=[jax.ShapeDtypeStruct((zs, NY, size, cols), BF16) for size in sizes],
        in_specs=[SMEM] + [VMEM] * NY,
        out_specs=[VMEM] * len(sizes),
        compiler_params=params(32),
        cost_estimate=cost(0.01, 1),
        name="by_y",
    )(at, *pieces)


def place(row, s):
    return s * 512 + ((row // 16) % NZ * NY + row // (16 * NZ)) * 16 + row % 16


def bias_kernel(heads, at_ref, seg_ref, dil_ref, out_ref, done_ref, q_ref, k_ref):
    s, y, count = at_ref[0], at_ref[1], at_ref[2]
    rows = q_ref.shape[0]
    span = 128 // heads

    def fill(ref, pos, valid):
        lane = lax.broadcasted_iota(jnp.int32, pos.shape, 1)
        column, head = lane & (span - 1), y * heads + lax.shift_right_logical(lane, jnp.full_like(lane, 5))
        hits = None
        for c in range(seg_ref.shape[0]):
            width = seg_ref[c]
            bits = 6 + sum((width > 64 << b).astype(jnp.int32) for b in range(4))
            first = lax.shift_right_logical(jnp.int32(2 * rows), bits)
            ids = first + lax.shift_right_logical(pos, jnp.full_like(pos, bits))
            hit = (ids == column) & (((pos ^ head) & (dil_ref[c] - 1)) == 0)
            hits = hit if hits is None else hits | hit
        ref[...] = jnp.where(hits & valid, 1.0, 0.0).astype(BF16)

    h = pl.program_id(0)

    @pl.when(h == 0)
    def _():
        row = lax.broadcasted_iota(jnp.int32, (rows, 128), 0)
        pos = place(row, s)
        fill(q_ref, pos, pos >= 0)
        row = lax.broadcasted_iota(jnp.int32, (2 * rows, 128), 0)
        pos = place(row % rows, row // rows)
        fill(k_ref, pos, pos < count)
        done_ref[...] = jnp.zeros_like(done_ref)

    block = 128
    of_head = lax.broadcasted_iota(jnp.int32, (1, 128), 1) // span == h
    for start in range(0, rows, block):
        span_rows = pl.ds(start, block)
        queries = jnp.where(of_head, q_ref[span_rows, :], 0).astype(BF16)
        counted = dot_general(queries, k_ref[...], CONTRACT_LAST)
        out_ref[0, span_rows, :] = jnp.where(counted > 0.5, jnp.log2(jnp.maximum(counted, 1.0)), -1e30)


def biases(at, seg_lengths, dilation, heads, rows):
    return pl.pallas_call(
        functools.partial(bias_kernel, heads),
        out_shape=(jax.ShapeDtypeStruct((heads, rows, 2 * rows), F32), jax.ShapeDtypeStruct((8, 128), F32)),
        grid=(heads,),
        in_specs=[SMEM] * 3,
        out_specs=(
            pl.BlockSpec((1, rows, 2 * rows), lambda h: (h, 0, 0)),
            pl.BlockSpec((8, 128), lambda h: (0, 0)),
        ),
        scratch_shapes=[pltpu.VMEM((rows, 128), BF16), pltpu.VMEM((2 * rows, 128), BF16)],
        compiler_params=params(60),
        cost_estimate=cost(1, 1),
        name="biases",
    )(at, seg_lengths, dilation)


def spread_kernel(common_ref, own_ref, _, out_ref):
    blocks = common_ref.shape[0]
    for y in range(NY):
        out_ref[y, :blocks] = common_ref[...]
        out_ref[y, blocks] = own_ref[y]


def spread(common, own, before):
    return pl.pallas_call(
        spread_kernel,
        out_shape=jax.ShapeDtypeStruct((NY, common.shape[0] + 1) + common.shape[1:], BF16),
        in_specs=[VMEM, VMEM, ANY],
        out_specs=VMEM,
        compiler_params=params(32),
        cost_estimate=cost(0.001, 0.1),
        name="spread",
    )(common, own, before)


def attend_kernel(at_ref, hm_ref, ho_ref, wm_ref, wo_ref, bias_ref, *refs):
    out_ref, w_ref, q_ref, k_ref, v_ref = refs[-5:]
    s = at_ref[0]
    rows = hm_ref.shape[0]
    half = hm_ref.shape[1] // 2
    heads, block, keys = bias_ref.shape
    seg = q_ref.shape[2]

    @pl.when(pl.program_id(0) == 0)
    def _():
        for z in range(NZ):
            w_ref[z, s] = wm_ref[z]
            w_ref[z, 1 - s] = wo_ref[z]
        w_mine = w_ref[pl.ds(s * (NZ // 2), NZ // 2)].reshape(half, w_ref.shape[3])
        w_other = w_ref[pl.ds((1 - s) * (NZ // 2), NZ // 2)].reshape(half, w_ref.shape[3])
        for core in range(2):
            lanes = slice(core * half, (core + 1) * half)
            all_parts = dot(hm_ref[:, lanes], w_mine) + dot(ho_ref[:, lanes], w_other)
            span = pl.ds(core * rows, rows)
            q_ref[core] = all_parts[:, :seg].astype(BF16)
            k_ref[span, :] = all_parts[:, seg : 2 * seg].astype(BF16)
            v_ref[span, :] = all_parts[:, 2 * seg :].astype(BF16)

    lane_head = lax.broadcasted_iota(jnp.int32, (1, seg), 1) // HS
    scale = HS ** (-0.5) * 1.4426950408889634
    queries = q_ref[s, pl.ds(pl.multiple_of(pl.program_id(0) * block, block), block), :]
    queries = jnp.concatenate([jnp.where(lane_head == h, queries, 0).astype(BF16) for h in range(heads)])
    scores = dot_general(queries, k_ref[...], CONTRACT_LAST)
    scores = scores * scale + bias_ref[...].reshape(heads * block, keys)
    weights = jnp.exp2(scores - jnp.max(scores, axis=-1, keepdims=True))
    total = jnp.sum(weights, axis=-1, keepdims=True)
    part = dot(weights.astype(BF16), v_ref[...]) * (1.0 / total)
    for h in range(heads):
        turned = part[h * block : (h + 1) * block].T
        out_ref[h * HS : (h + 1) * HS, :] = turned[h * HS : (h + 1) * HS].astype(BF16)


def attend(at, hm, ho, wm, wo, bias, before):
    heads, rows, keys = bias.shape
    seg = wm.shape[2] // 3
    block = 128
    return pl.pallas_call(
        attend_kernel,
        out_shape=jax.ShapeDtypeStruct((heads * HS, rows), BF16),
        grid=(rows // block,),
        in_specs=[SMEM] + [VMEM] * 4 + [pl.BlockSpec((heads, block, keys), lambda i: (0, i, 0))] + [ANY] * len(before),
        out_specs=pl.BlockSpec((heads * HS, block), lambda i: (0, i)),
        scratch_shapes=[
            pltpu.VMEM((NZ, 2) + wm.shape[1:], BF16),
            pltpu.VMEM((2, rows, seg), BF16),
            pltpu.VMEM((keys, seg), BF16),
            pltpu.VMEM((keys, seg), BF16),
        ],
        compiler_params=params(48),
        cost_estimate=cost(8, 12, 2),
        name="attend",
    )(at, hm, ho, wm, wo, bias, *before)


def finish_kernel(at_ref, a0_ref, a1_ref, a2_ref, a3_ref, wm_ref, wo_ref, hm_ref, ho_ref, out_ref):
    s, y, count = at_ref[0], at_ref[1], at_ref[2]
    rows, half = hm_ref.shape[0], hm_ref.shape[1] // 2
    tiles = out_ref.shape[2]
    mine = other = 0.0
    for k, att_ref in enumerate((a0_ref, a1_ref, a2_ref, a3_ref)):
        depth = att_ref.shape[0]
        span = pl.ds(pl.multiple_of(lax.rem(y + NY - k, NY) * depth, depth), depth)
        mine = mine + dot_general(att_ref[...], wm_ref[span, :], CONTRACT_FIRST)
        other = other + dot_general(att_ref[...], wo_ref[span, :], CONTRACT_FIRST)
    lanes = pl.ds(pl.multiple_of(s * half, half), half)
    mine = mine + hm_ref[:, lanes].astype(F32)
    other = other + ho_ref[:, lanes].astype(F32)
    row = lax.broadcasted_iota(jnp.int32, (rows, half), 0)
    valid = place(row, s) < count
    left = jnp.where(valid, jnp.where(s == 0, mine, other), 0.0).astype(BF16)
    right = jnp.where(valid, jnp.where(s == 0, other, mine), 0.0).astype(BF16)
    span = NZ * tiles
    for y in range(NY):
        for part, lanes in ((left, slice(0, half)), (right, slice(half, 2 * half))):
            out_ref[:, y, :, lanes] = part[y * span : (y + 1) * span].reshape(NZ, tiles, half)


def finish(at, att, wm, wo, hm, ho, tiles):
    return pl.pallas_call(
        finish_kernel,
        out_shape=jax.ShapeDtypeStruct((NZ, NY, tiles, hm.shape[1]), BF16),
        in_specs=[SMEM] + [VMEM] * 8,
        out_specs=VMEM,
        compiler_params=params(32),
        cost_estimate=cost(0.6, 4),
        name="finish",
    )(at, *att, wm, wo, hm, ho)


def body(
    head_out,
    proj_weight,
    norm_gain,
    embed_cot,
    tile_counts,
    seg_lengths,
    dilation,
    embed_weight,
    qkv_weight,
    out_weight,
):
    tokens = head_out[0]
    n_rows, aw = tokens.shape
    dt = proj_weight.shape[1]
    half = dt // 2
    tiles = embed_cot.shape[1]
    per_tile = n_rows // tiles
    fsdp = NZ * NY
    f = lax.axis_index("fsdp")
    s = lax.axis_index("seq")
    y = f % NY
    count = tile_counts[0]
    ds = out_weight.shape[1]
    shard_len = fsdp * tiles
    x = lax.axis_index("slide")
    at = jnp.stack([s, y, count, x, f // NY]).astype(jnp.int32)
    dslice = lax.dynamic_slice_in_dim
    heads = ds // HS // NY
    width = heads * HS

    def of_y(v, k):
        return lax.dynamic_index_in_dim(v, (y + k) % NY, 0, keepdims=False)

    bias, zero = biases(at, seg_lengths, dilation, heads, shard_len)

    rows = proj_weight.shape[0]
    w_heads = qkv_weight.reshape(rows, 3, NY, width).transpose(2, 0, 1, 3)
    w_heads = jnp.pad(w_heads, ((0, 0), (0, 0), (0, 0), (0, 256 - width))).reshape(NY, rows, 3 * 256)

    quarter = ds // 2
    first = a2a_z(copies(dslice(proj_weight, s * half, half, 1), NZ))
    others = jnp.concatenate([dslice(w, s * quarter, quarter, 1) for w in (embed_weight, out_weight)])
    others = after(others, first)
    others = [others] + [shift_z(others, k) for k in range(1, NZ)]
    gathered = a2a_y(spread(first, w_heads, zero))
    proj_mine, w_heads = arrange(at, gathered, others[1:])
    proj_mine, w_heads = proj_mine.reshape(aw, half), w_heads.reshape(2 * rows, half)
    proj_other = swap(proj_mine)
    others = by_z(at, others)
    others = [others] + [shift_y(others, k) for k in range(1, NY)]

    def halves(v):
        return dslice(v, s * half, half, v.ndim - 1), dslice(v, (1 - s) * half, half, v.ndim - 1)

    gain = halves(norm_gain)
    embed, normed_mine, normed_other, inv_std = forward(at, tokens, proj_mine, proj_other, jnp.stack(gain), tiles)
    embed = embed.astype(BF16)
    embed_other = swap(embed)
    embed = jnp.concatenate([jnp.where(s == 0, embed, embed_other), jnp.where(s == 0, embed_other, embed)])

    base = (s * fsdp + f) * tiles
    valid = (base + jnp.arange(tiles, dtype=jnp.int32) < count).astype(F32)
    grads = [c * valid[:, None] / per_tile * g for c, g in zip(halves(embed_cot[0].astype(F32)), gain)]

    w_embed, w_out = by_y(at, others, 2 * rows, rows)
    w_embed, w_out = w_embed.reshape(dt, quarter), w_out.reshape(ds, quarter)
    w_out_other = swap(w_out)
    hidden = dot(embed, w_embed).astype(BF16)
    hidden = jnp.concatenate([hidden[:tiles], hidden[tiles:]], axis=1)
    mixed_mine, mixed_other, term_mine, term_other = backward(
        hidden, tokens, normed_mine, normed_other, inv_std, grads
    )
    second = a2a_z(copies(jnp.concatenate([hidden, w_heads]), NZ))

    parts = pair_sum(at, term_mine, swap(term_other))
    hidden = a2a_y(copies(after(second[:, :tiles], parts[0]), NY)).reshape(shard_len, ds)
    hidden_other = swap(hidden)
    parts = [parts[0]] + [shift_y(parts[k], k) for k in range(1, NY)]
    share = a2a_z(sum_of("y_sum", [hidden], parts, 6))

    w_heads = second[:, tiles:]
    w_heads_other = swap(w_heads)
    attended = attend(at, hidden, hidden_other, w_heads, w_heads_other, bias, [])
    head_out_grad, zero = head_out_grad_of(after(at, attended), mixed_mine, mixed_other, proj_mine, proj_other)
    received = [attended] + [shift_y(attended, k) for k in range(1, NY)]
    share = sum_of("z_sum", [attended], share)
    parts = [share] + [shift_x(share, k) for k in range(1, NX)]
    slide_out = finish(after(at, zero), received, w_out, w_out_other, hidden, hidden_other, tiles)
    share = sum_of("x_sum", [slide_out], parts)
    other = swap(share)
    slide_out = slide_out.reshape(1, shard_len, ds)
    proj_grad = jnp.concatenate([jnp.where(s == 0, share, other), jnp.where(s == 0, other, share)], axis=1)
    return (slide_out, head_out_grad[None], proj_grad)


def solution(mesh):
    return jax.shard_map(
        body,
        mesh=mesh,
        in_specs=(
            P("slide", ("seq", "fsdp"), None),
            P("fsdp", None),
            P(),
            P("slide", ("seq", "fsdp"), None),
            P("slide"),
            P(),
            P(),
            P("fsdp", None),
            P("fsdp", None),
            P("fsdp", None),
        ),
        out_specs=(P("slide", "seq", None), P("slide", ("seq", "fsdp"), None), P("fsdp", None)),
        check_vma=False,
    )
```
